32 devices in a mesh: grp: 2 (over x), sub: 16 (over z, y, core).
Axes of the slice: x: 2, y: 2, z: 4, core: 2. Of those that a mesh axis runs over, the one named last changes fastest.
Arguments:
- overall_quantity_unnormalized: float32 [16, 16, 256, 128], P(None, 'grp', 'sub'), may hold values from 0.05 to 1
- reservoir_pressure_field: float32 [16, 256, 128], P('grp', 'sub'), may hold values from 0.7 to 1.3
- reservoir_heat_level: float32 [16, 256, 128], P('grp', 'sub'), may hold values from 0.9 to 1.2
- condensed_flag: int32 [16, 256, 128], P('grp', 'sub'), may hold values 0 or 1
- permeability_field: float32 [16, 256, 128], P('grp', 'sub'), may hold values from 0.1 to 10
- pore_capacity: float32 [16, 256, 128], P('grp', 'sub'), may hold values from 0.05 to 0.3
- former_chemical_quantity: float32 [16, 16, 256, 128], P(None, 'grp', 'sub'), may hold values from 0 to 0.03
- transmissibility_multipliers: float32 [3], replicated, may hold values from 0.3 to 3
- viscosity_pair: float32 [2], replicated, may hold values from 0.3 to 3
- crit_kelvin_values: float32 [16], replicated, may hold values from 0.3 to 2.5
- attraction_parameters: float32 [16], replicated, may hold values from 0.3 to 4
- repulsive_parameters: float32 [16], replicated, may hold values from 0.02 to 0.15
- attraction_thermal_gradients: float32 [16], replicated, may hold values from 0.3 to 1.2
- binary_coupling_matrix: float32 [16, 16], replicated, may hold values from 0 to 0.3, as said below
- injected_recipe_unnormalized: float32 [16], replicated, may hold values from 0.05 to 1
- perforated_locale: int32 [8192], P(('grp', 'sub')), may hold values from 0 to 16383
- perforated_member: int32 [8192, 1], P(('grp', 'sub')), may hold values from 0 to 15; in each aligned block of 256 rows (0 to 255, 256 to 511, ...) at most 40 rows name the same one
- connection_conduit_piece: int32 [8192], P(('grp', 'sub')), may hold values from 0 to 31
- connection_inflow_strength: float32 [8192], P(('grp', 'sub')), may hold values from 0.02 to 0.2
- group_member_place: int32 [2, 16], P('grp'), may hold values from 0 to 15, each once within a row
- conduit_pieces_toe_forward: int32 [32, 32], P(('grp', 'sub')), may hold values from 0 to 31, each once within a row
- conduit_piece_pressures: float32 [32, 32], P(('grp', 'sub')), may hold values from 0.7 to 1.3
- downstream_exit_pressure: float32 [32], P(('grp', 'sub')), may hold values from 0.6 to 1.2
- friction_factors: float32 [32], P(('grp', 'sub')), may hold values from 3.0517578e-05 to 0.00030517578
Outputs:
- residual: float32 [16, 16, 256, 128], P(None, 'grp', 'sub')
- ln_phi: bfloat16 [16, 16, 256, 128], P(None, 'grp', 'sub')
- well_residual: float32 [32, 32], P(('grp', 'sub'))
The draws below stay inside these ranges and needn't reach their ends.
Inputs may be any that keep to these rules, and one draw needn't show every extreme that they name: `perforated_locale`: flattened index (first, second, layer) of a cell of the listing device's own block. `perforated_member`: a well of the listing device's group; among the 256 rows of one device at most 40 name the same well. `group_member_place`: each row is a permutation; slot j of a group lies on the group's device j. `conduit_pieces_toe_forward`: each row is a permutation of the segments. `binary_coupling_matrix`: symmetric with zero diagonal.
All inputs are finite; a program needn't handle non-finite values. No bound on the sum of `condensed_flag` on one device may be relied on, other than what follows from the above.
Results may differ from the reference program's by a relative error of at most 0.001.
Values sent between devices are 32-bit elements; how exact they have to be, the bound alone decides.
No kernel may reach another device: no remote copies, remote signals or barrier semaphores. Data moves between devices by JAX's collectives and lax.ppermute only.
A program may use at most 64 MiB of HBM per device.

```python
import math
import jax
import jax.numpy as jnp
import numpy as np
from jax import lax

CHEMICAL_KINDS = 16
CX = 8
CY = 16
STRATA_NUMBER = 128
NEWT = 8
PERF_DEV = 256
SEGS = 32
GRID_NX_EXTENT = 16
GRID_NY_EXTENT = 256
WELL_G = 16
WELLS = 32
CAP = 40
N_GRP = 2
N_SUB = 16
DEVICES = 32


def draw_binary_coupling_matrix(key, part):
    values = jax.random.uniform(key, (CHEMICAL_KINDS, CHEMICAL_KINDS), jnp.float32, 0.0, 0.3)
    both = 0.5 * (values + values.T)
    return both * (1.0 - jnp.eye(CHEMICAL_KINDS, dtype=jnp.float32))


def place_ends(values, rng, low, high):
    longest = values.shape.index(max(values.shape))
    spots = []
    for shift in (0, 1):
        where = [jax.random.randint(jax.random.fold_in(rng, axis), (), 0, length) for axis, length in enumerate(values.shape)]
        where[longest] = (where[longest] + shift) % values.shape[longest]
        spots.append(tuple(where))
    return values.at[spots[0]].set(low).at[spots[1]].set(high)


def level_of(own_key, extent, pieces, low, high):
    loudness, own = 1.0, jax.random.fold_in(own_key, 6)
    for dim, shards_of in pieces:
        heights = jnp.exp(jax.random.uniform(jax.random.fold_in(own, dim), (shards_of,), jnp.float32, low / len(pieces), high / len(pieces)))
        loudness = loudness * jnp.repeat(heights, extent[dim] // shards_of).reshape([-1 if axis == dim else 1 for axis in range(len(extent))])
    return loudness


def assign_block(rng, own, number, rows, number_of, top, reach, skew):
    sequence = jax.random.permutation(rng, number_of)
    heavy_load, common = shares(number_of, rows * top, reach, skew, True), shares(number_of, rows * top, reach, skew, False)
    places = jnp.arange(number_of)

    def named(sizes, offset_by):
        used = int((sizes > 0).sum())
        fixed = max(1, used // 4)
        passed = fixed + (places - fixed + offset_by * (used - fixed)) % max(1, number_of - fixed)
        return jnp.zeros((number_of,), jnp.int32).at[sequence[jnp.where(places < fixed, places, passed)]].set(jnp.asarray(sizes, jnp.int32))

    sizes = jnp.where(number % 4 == 0, named(heavy_load, number // 4), named(common, number - number // 4 - 1))
    mixed = jax.random.permutation(jax.random.fold_in(own, 3), number_of)
    giver, taker = mixed[0:number_of // 2 * 2:2], mixed[1:number_of // 2 * 2:2]
    margin = jnp.minimum(sizes[giver] - 1, reach - sizes[taker]) // 2
    margin = jnp.where((giver == sequence[0]) | (taker == sequence[0]) | (sizes[taker] == 0), 0, jnp.maximum(margin, 0))
    passed = jax.random.randint(jax.random.fold_in(own, 4), (number_of // 2,), 0, 1 << 20) % (margin + 1)
    sizes = sizes.at[giver].add(-passed).at[taker].add(passed)
    members = jnp.searchsorted(jnp.cumsum(sizes), jnp.arange(rows * top), side="right").astype(jnp.int32)
    listing = members.reshape(top, rows).T
    listing = listing[jax.random.permutation(jax.random.fold_in(own, 1), rows)]
    offset_by = jax.random.randint(jax.random.fold_in(own, 2), (rows, 1), 0, top)
    return jnp.take_along_axis(listing, (jnp.arange(top)[None, :] + offset_by) % top, axis=1)


def shares(number_of, total, reach, lean, full):
    portions = [(1 << 20) // math.isqrt(standing ** lean) + 1 for standing in range(1, number_of + 1)]
    largest = reach if full else min(reach, max(-(-total // number_of), total * portions[0] // sum(portions)))
    least = 1 if total - largest >= number_of - 1 else 0
    counts, rest = [largest] + [least] * (number_of - 1), total - largest - least * (number_of - 1)
    while rest > 0:
        candidates = [i for i in range(1, number_of) if counts[i] < largest] or [i for i in range(1, number_of) if counts[i] < reach]
        whole, left = sum([portions[i] for i in candidates]), rest
        for i in candidates:
            more = min(reach - counts[i], max(1, left * portions[i] // whole), rest)
            counts[i] = counts[i] + more
            rest = rest - more
    return np.array(counts)


def setup_inputs(seed: int = 0) -> dict:
    streams_of = jax.random.split(jax.random.key(seed), 25)
    overall_quantity_unnormalized = jnp.clip(jnp.exp(math.log(1.0) - 2.9957323 * jax.random.uniform(streams_of[0], (CHEMICAL_KINDS, GRID_NX_EXTENT, GRID_NY_EXTENT, STRATA_NUMBER), jnp.float32) ** level_of(streams_of[0], (CHEMICAL_KINDS, GRID_NX_EXTENT, GRID_NY_EXTENT, STRATA_NUMBER), ((1, 2), (2, 16)), -0.2, 0.2)), 0.05, 1.0)
    reservoir_pressure_field = jnp.clip(0.7 + 0.59999996 * jax.random.uniform(streams_of[1], (GRID_NX_EXTENT, GRID_NY_EXTENT, STRATA_NUMBER), jnp.float32) ** level_of(streams_of[1], (GRID_NX_EXTENT, GRID_NY_EXTENT, STRATA_NUMBER), ((0, 2), (1, 16)), -0.2, 0.2), 0.7, 1.3)
    reservoir_heat_level = jnp.clip(0.9 + 0.30000007 * jax.random.uniform(streams_of[2], (GRID_NX_EXTENT, GRID_NY_EXTENT, STRATA_NUMBER), jnp.float32) ** level_of(streams_of[2], (GRID_NX_EXTENT, GRID_NY_EXTENT, STRATA_NUMBER), ((0, 2), (1, 16)), -0.2, 0.2), 0.9, 1.2)
    condensed_flag = place_ends((jax.random.randint(streams_of[3], (GRID_NX_EXTENT, GRID_NY_EXTENT, STRATA_NUMBER), 0, 2) < 1).astype(jnp.int32), jax.random.fold_in(streams_of[3], 1), 0, 1)
    permeability_field = jnp.clip(jnp.exp(math.log(10.0) - 4.6051702 * jax.random.uniform(streams_of[4], (GRID_NX_EXTENT, GRID_NY_EXTENT, STRATA_NUMBER), jnp.float32) ** level_of(streams_of[4], (GRID_NX_EXTENT, GRID_NY_EXTENT, STRATA_NUMBER), ((0, 2), (1, 16)), -0.2, 0.2)), 0.1, 10.0)
    pore_capacity = jnp.clip(jnp.exp(math.log(0.3) - 1.7917595 * jax.random.uniform(streams_of[5], (GRID_NX_EXTENT, GRID_NY_EXTENT, STRATA_NUMBER), jnp.float32) ** level_of(streams_of[5], (GRID_NX_EXTENT, GRID_NY_EXTENT, STRATA_NUMBER), ((0, 2), (1, 16)), -0.2, 0.2)), 0.05, 0.3)
    former_chemical_quantity = jnp.clip(0.03 * jax.random.uniform(streams_of[6], (CHEMICAL_KINDS, GRID_NX_EXTENT, GRID_NY_EXTENT, STRATA_NUMBER), jnp.float32) ** level_of(streams_of[6], (CHEMICAL_KINDS, GRID_NX_EXTENT, GRID_NY_EXTENT, STRATA_NUMBER), ((1, 2), (2, 16)), -0.2, 0.2), 0.0, 0.03)
    transmissibility_multipliers = jnp.clip(jnp.exp(jax.random.uniform(streams_of[7], (3,), jnp.float32, math.log(0.3), math.log(3.0))), 0.3, 3.0)
    viscosity_pair = jnp.clip(jnp.exp(jax.random.uniform(streams_of[8], (2,), jnp.float32, math.log(0.3), math.log(3.0))), 0.3, 3.0)
    crit_kelvin_values = jnp.clip(jnp.exp(jax.random.uniform(streams_of[9], (CHEMICAL_KINDS,), jnp.float32, math.log(0.3), math.log(2.5))), 0.3, 2.5)
    attraction_parameters = jnp.clip(jnp.exp(jax.random.uniform(streams_of[10], (CHEMICAL_KINDS,), jnp.float32, math.log(0.3), math.log(4.0))), 0.3, 4.0)
    repulsive_parameters = jnp.clip(jnp.exp(jax.random.uniform(streams_of[11], (CHEMICAL_KINDS,), jnp.float32, math.log(0.02), math.log(0.15))), 0.02, 0.15)
    attraction_thermal_gradients = jnp.clip(jax.random.uniform(streams_of[12], (CHEMICAL_KINDS,), jnp.float32, 0.3, 1.2), 0.3, 1.2)
    binary_coupling_matrix = draw_binary_coupling_matrix(jax.random.fold_in(streams_of[24], 71), 0)
    injected_recipe_unnormalized = jnp.clip(jnp.exp(jax.random.uniform(streams_of[14], (CHEMICAL_KINDS,), jnp.float32, math.log(0.05), math.log(1.0))), 0.05, 1.0)
    perforated_locale = place_ends(jax.random.randint(streams_of[15], (DEVICES * PERF_DEV,), 0, CX * CY * STRATA_NUMBER), jax.random.fold_in(streams_of[15], 1), 0, (CX * CY * STRATA_NUMBER) - 1).astype(jnp.int32)
    perforated_member_keys = jax.random.split(jax.random.fold_in(streams_of[16], 1), (DEVICES * PERF_DEV) // PERF_DEV)
    perforated_member_turns = jax.random.permutation(jax.random.fold_in(streams_of[16], 3), (DEVICES * PERF_DEV) // PERF_DEV)
    perforated_member = jax.vmap(lambda own, number: assign_block(jax.random.fold_in(streams_of[16], 2), own, number, PERF_DEV, WELL_G, 1, CAP, 2))(perforated_member_keys, perforated_member_turns).reshape((DEVICES * PERF_DEV, 1))
    connection_conduit_piece = place_ends(jax.random.randint(streams_of[17], (DEVICES * PERF_DEV,), 0, SEGS), jax.random.fold_in(streams_of[17], 1), 0, SEGS - 1).astype(jnp.int32)
    connection_inflow_strength = jnp.clip(jnp.exp(math.log(0.2) - 2.3025851 * jax.random.uniform(streams_of[18], (DEVICES * PERF_DEV,), jnp.float32) ** level_of(streams_of[18], (DEVICES * PERF_DEV,), ((0, 32),), -0.2, 0.2)), 0.02, 0.2)
    group_member_place = jax.vmap(lambda own: jax.random.permutation(own, WELL_G))(jax.random.split(streams_of[19], N_GRP)).reshape((N_GRP, WELL_G)).astype(jnp.int32)
    conduit_pieces_toe_forward = jax.vmap(lambda own: jax.random.permutation(own, SEGS))(jax.random.split(streams_of[20], WELLS)).reshape((WELLS, SEGS)).astype(jnp.int32)
    conduit_piece_pressures = jnp.clip(0.7 + 0.59999996 * jax.random.uniform(streams_of[21], (WELLS, SEGS), jnp.float32) ** level_of(streams_of[21], (WELLS, SEGS), ((0, 32),), -0.2, 0.2), 0.7, 1.3)
    downstream_exit_pressure = jnp.clip(0.6 + 0.6 * jax.random.uniform(streams_of[22], (WELLS,), jnp.float32) ** level_of(streams_of[22], (WELLS,), ((0, 32),), -0.2, 0.2), 0.6, 1.2)
    friction_factors = jnp.clip(jnp.exp(math.log(0.00030517578) - 2.3025851 * jax.random.uniform(streams_of[23], (WELLS,), jnp.float32) ** level_of(streams_of[23], (WELLS,), ((0, 32),), -0.2, 0.2)), 3.0517578125e-05, 0.00030517578)
    return dict(overall_quantity_unnormalized=overall_quantity_unnormalized, reservoir_pressure_field=reservoir_pressure_field, reservoir_heat_level=reservoir_heat_level, condensed_flag=condensed_flag, permeability_field=permeability_field, pore_capacity=pore_capacity, former_chemical_quantity=former_chemical_quantity, transmissibility_multipliers=transmissibility_multipliers, viscosity_pair=viscosity_pair, crit_kelvin_values=crit_kelvin_values, attraction_parameters=attraction_parameters, repulsive_parameters=repulsive_parameters, attraction_thermal_gradients=attraction_thermal_gradients, binary_coupling_matrix=binary_coupling_matrix, injected_recipe_unnormalized=injected_recipe_unnormalized, perforated_locale=perforated_locale, perforated_member=perforated_member, connection_conduit_piece=connection_conduit_piece, connection_inflow_strength=connection_inflow_strength, group_member_place=group_member_place, conduit_pieces_toe_forward=conduit_pieces_toe_forward, conduit_piece_pressures=conduit_piece_pressures, downstream_exit_pressure=downstream_exit_pressure, friction_factors=friction_factors)


ROOT_TWO = math.sqrt(2.0)

def gas_oil_partition(overall_quantity_unnormalized, reservoir_pressure_field, reservoir_heat_level, condensed_flag, crit_kelvin_values, attraction_parameters, repulsive_parameters, attraction_thermal_gradients, binary_coupling_matrix, viscosity_pair):
    shape = overall_quantity_unnormalized.shape
    replicate_across = (slice(None),) + (None,) * (len(shape) - 1)
    chemical_labels = overall_quantity_unnormalized / lax.optimization_barrier(jnp.sum(overall_quantity_unnormalized, axis=0))
    thermal_adjuster = (1.0 + attraction_thermal_gradients[replicate_across] * (1.0 - jnp.sqrt(reservoir_heat_level / crit_kelvin_values[replicate_across]))) ** 2
    blended_attraction = attraction_parameters[replicate_across] * thermal_adjuster * reservoir_pressure_field / (reservoir_heat_level * reservoir_heat_level)
    roots = jnp.sqrt(blended_attraction)
    mixture_excluded_volume = repulsive_parameters[replicate_across] * reservoir_pressure_field / reservoir_heat_level
    mixed = jnp.dot(1.0 - binary_coupling_matrix, (roots * chemical_labels).reshape(shape[0], -1), precision=lax.Precision.HIGHEST).reshape(shape)
    psi = roots * mixed
    big_a = lax.optimization_barrier(jnp.sum(chemical_labels * psi, axis=0))
    big_b = lax.optimization_barrier(jnp.sum(chemical_labels * mixture_excluded_volume, axis=0))
    deviation_zvalue = jnp.where(condensed_flag == 1, big_b + 0.01, 1.0 + big_b)
    lin_c2 = big_b - 1.0
    lin_c1 = big_a - 3.0 * big_b * big_b - 2.0 * big_b
    lin_c0 = big_b * big_b + big_b * big_b * big_b - big_a * big_b
    for step in range(NEWT):
        value = ((deviation_zvalue + lin_c2) * deviation_zvalue + lin_c1) * deviation_zvalue + lin_c0
        slope = (3.0 * deviation_zvalue + 2.0 * lin_c2) * deviation_zvalue + lin_c1
        deviation_zvalue = jnp.maximum(deviation_zvalue - value / jnp.maximum(slope, 0.1), big_b + 0.01)
    ratio = jnp.log((deviation_zvalue + (1.0 + ROOT_TWO) * big_b) / (deviation_zvalue + (1.0 - ROOT_TWO) * big_b))
    natural_log_activity = mixture_excluded_volume / big_b * (deviation_zvalue - 1.0) - jnp.log(deviation_zvalue - big_b) - (psi / (ROOT_TWO * big_b) - big_a * mixture_excluded_volume / (2.0 * ROOT_TWO * big_b * big_b)) * ratio
    blended_dilution_ratio = reservoir_pressure_field / (deviation_zvalue * reservoir_heat_level)
    visc = jnp.where(condensed_flag == 1, viscosity_pair[1], viscosity_pair[0])
    relative_flow_ease = blended_dilution_ratio / visc
    return (chemical_labels, natural_log_activity, blended_dilution_ratio, relative_flow_ease)

def face(c_a, p_a, k_a, c_b, p_b, k_b, factor):
    trans = factor * 2.0 * k_a * k_b / (k_a + k_b)
    return trans * (p_a - p_b) * jnp.where(p_a > p_b, c_a, c_b)

def shifted(arr, axis, upward):
    width = [(0, 0)] * arr.ndim
    width[axis] = (1, 1)
    padded = jnp.pad(arr, width)
    size = arr.shape[axis]
    start = 2 if upward else 0
    return lax.slice_in_dim(padded, start, start + size, axis=arr.ndim + axis if axis < 0 else axis)

def reference(overall_quantity_unnormalized, reservoir_pressure_field, reservoir_heat_level, condensed_flag, permeability_field, pore_capacity, former_chemical_quantity, transmissibility_multipliers, viscosity_pair, crit_kelvin_values, attraction_parameters, repulsive_parameters, attraction_thermal_gradients, binary_coupling_matrix, injected_recipe_unnormalized, perforated_locale, perforated_member, connection_conduit_piece, connection_inflow_strength, group_member_place, conduit_pieces_toe_forward, conduit_piece_pressures, downstream_exit_pressure, friction_factors):
    species_share = jnp.moveaxis(overall_quantity_unnormalized, 0, 1)
    earlier_share = jnp.moveaxis(former_chemical_quantity, 0, 1)

    def stratum_plane(items):
        crude_sample, pressure_level, kelvin_level, label_vector, pore, old = items
        chemical_labels, natural_log_activity, blended_dilution_ratio, relative_flow_ease = gas_oil_partition(crude_sample, pressure_level, kelvin_level, label_vector, crit_kelvin_values, attraction_parameters, repulsive_parameters, attraction_thermal_gradients, binary_coupling_matrix, viscosity_pair)
        storage_term = pore * blended_dilution_ratio * chemical_labels - old
        return (chemical_labels, natural_log_activity, relative_flow_ease, storage_term)
    chemical_labels, natural_log_activity, relative_flow_ease, storage_term = lax.map(stratum_plane, (species_share, reservoir_pressure_field, reservoir_heat_level, condensed_flag, pore_capacity, earlier_share))
    carried = relative_flow_ease[:, None] * chemical_labels
    carried_pad = jnp.pad(carried, ((1, 1), (0, 0), (0, 0), (0, 0)))
    press_pad = jnp.pad(reservoir_pressure_field, ((1, 1), (0, 0), (0, 0)))
    perm_pad = jnp.pad(permeability_field, ((1, 1), (0, 0), (0, 0)))

    def slab_flux(index):
        cwin = lax.dynamic_slice_in_dim(carried_pad, index, 3, 0)
        pwin = lax.dynamic_slice_in_dim(press_pad, index, 3, 0)
        kwin = lax.dynamic_slice_in_dim(perm_pad, index, 3, 0)
        c_a, p_a, k_a = (cwin[1], pwin[1], kwin[1])
        total = lax.dynamic_index_in_dim(storage_term, index, 0, keepdims=False)
        total = total + face(c_a, p_a, k_a, cwin[2], pwin[2], kwin[2], transmissibility_multipliers[0])
        total = total + face(c_a, p_a, k_a, cwin[0], pwin[0], kwin[0], transmissibility_multipliers[0])
        for axis, factor in ((0, transmissibility_multipliers[1]), (1, transmissibility_multipliers[2])):
            for upward in (True, False):
                total = total + face(c_a, p_a, k_a, shifted(c_a, axis - 2, upward), shifted(p_a, axis - 2, upward), shifted(k_a, axis - 2, upward), factor)
        return total
    resid_x = lax.map(slab_flux, jnp.arange(GRID_NX_EXTENT, dtype=jnp.int32))
    rows = jnp.arange(N_GRP * N_SUB * PERF_DEV, dtype=jnp.int32)
    device = rows // PERF_DEV
    grp_index = device // N_SUB
    sub_index = device % N_SUB
    cell_x = grp_index * CX + perforated_locale // (CY * STRATA_NUMBER)
    cell_y = sub_index * CY + perforated_locale // STRATA_NUMBER % CY
    cell_z = perforated_locale % STRATA_NUMBER
    p_cell = reservoir_pressure_field[cell_x, cell_y, cell_z]
    m_cell = relative_flow_ease[cell_x, cell_y, cell_z]
    z_cell = chemical_labels[cell_x, :, cell_y, cell_z].T
    slot = grp_index * WELL_G + group_member_place[grp_index, perforated_member[:, 0]]
    p_seg = conduit_piece_pressures[slot, connection_conduit_piece]
    drop = p_cell - p_seg
    injected = injected_recipe_unnormalized / jnp.sum(injected_recipe_unnormalized)
    inflow = (connection_inflow_strength * m_cell * drop)[None, :] * jnp.where(drop[None, :] > 0, z_cell, injected[:, None])
    resid_x = resid_x.at[cell_x, :, cell_y, cell_z].add(inflow.T)
    residual = jnp.moveaxis(resid_x, 1, 0)
    ln_phi = jnp.moveaxis(natural_log_activity, 1, 0).astype(jnp.bfloat16)
    totals = lax.optimization_barrier(jnp.sum(inflow, axis=0))
    rate = jax.ops.segment_sum(totals, slot * SEGS + connection_conduit_piece, num_segments=WELLS * SEGS).reshape(WELLS, SEGS)
    ordered = jnp.take_along_axis(rate, conduit_pieces_toe_forward, axis=1)
    running = jnp.cumsum(ordered, axis=1)
    press_ord = jnp.take_along_axis(conduit_piece_pressures, conduit_pieces_toe_forward, axis=1)
    nexts = jnp.concatenate([press_ord[:, 1:], downstream_exit_pressure[:, None]], axis=1)
    res_ord = press_ord - nexts - friction_factors[:, None] * running * jnp.abs(running)
    well_rows = jnp.arange(WELLS, dtype=jnp.int32)[:, None]
    well_residual = jnp.zeros((WELLS, SEGS), jnp.float32).at[well_rows, conduit_pieces_toe_forward].set(res_ord)
    return (residual, ln_phi, well_residual)
```

```python
import functools
import math

import jax
import jax.numpy as jnp
from jax import lax
from jax.experimental import pallas as pl
from jax.experimental.pallas import tpu as pltpu
from jax.sharding import PartitionSpec as P

NEWT = 8
ROOT_TWO = math.sqrt(2.0)
LANES = 128
SUBLANES = 8
F32 = jnp.float32
BF16 = jnp.bfloat16
VMEM_LIMIT = 48 * 1024 * 1024
MARGIN = 8


def iota(shape, dim):
    return lax.broadcasted_iota(jnp.int32, shape, dim)


def pieces_of(x, count):
    out = []
    for _ in range(count):
        piece = x.astype(BF16)
        out.append(piece)
        x = x - piece.astype(F32)
    return out


def mat(a, b):
    return lax.dot_general(a, b, (((1,), (0,)), ((), ())), preferred_element_type=F32)


def mat_nt(a, b):
    return lax.dot_general(a, b, (((1,), (1,)), ((), ())), preferred_element_type=F32)


def mat_hot(x, hot, count=3):
    return sum(mat(piece, hot) for piece in pieces_of(x, count))


def hot_mat_nt(hot, x, count=3):
    return sum(mat_nt(hot, piece) for piece in pieces_of(x, count))


def hot(cond):
    return jnp.where(cond, 1.0, 0.0).astype(BF16)


def place_hots(loc, rows):
    n = loc.shape[1]
    row_hot = iota((rows, n), 0) == loc // LANES
    lane_hot = iota((LANES, n), 0) == loc % LANES
    return row_hot, lane_hot


def slot_hot_of(member, place):
    wells = place.shape[1]
    slot_of = hot(iota((wells, wells), 0) == place)
    member_hot = hot(iota((wells, member.shape[1]), 0) == member)
    return mat(slot_of, member_hot)


def phase_kernel(
    nx,
    ny,
    axes,
    amount,
    press,
    heat,
    flag,
    perm,
    visc,
    crit,
    attract,
    covol,
    slope,
    coupling,
    loc,
    member,
    seg,
    strength,
    place,
    lnphi_out,
    carried_out,
    mob_out,
    edge_x_out,
    edge_ya_out,
    edge_yb_out,
    part_out,
    pcell_out,
    amount_v,
    split_v,
    psi_v,
    carried_v,
    lnphi_v,
    field_v,
    table_v,
    in_sems,
    out_sems,
    edge_sem,
):
    nc = amount.shape[0]
    per = 2
    chunks = nx // per
    rows = per * ny
    loads = []
    for c in range(chunks):
        span = pl.ds(c * rows, rows)
        copy = pltpu.make_async_copy(amount.at[:, span], amount_v.at[:, span], in_sems.at[c])
        copy.start()
        loads.append(copy)

    for i in range(nc):
        root = jnp.sqrt(jnp.full((SUBLANES, LANES), attract[i], F32))
        kappa = jnp.full((SUBLANES, LANES), slope[i], F32)
        tc = jnp.full((SUBLANES, LANES), crit[i], F32)
        table_v[0, i] = root * (1.0 + kappa)
        table_v[1, i] = root * kappa / jnp.sqrt(tc)
        table_v[2, i] = jnp.full((SUBLANES, LANES), covol[i], F32)

    size = nc * ny
    spread = hot(iota((size, nc), 0) // ny == iota((size, nc), 1))
    same_row = iota((size, size), 0) % ny == iota((size, size), 1) % ny
    mixers = []
    for piece in pieces_of(1.0 - coupling[...], 2):
        wide = mat(spread, piece).astype(BF16)
        mixers.append(jnp.where(same_row, mat_nt(wide, spread), 0.0).astype(BF16))
    mixer = jnp.concatenate([mixers[0], mixers[0], mixers[1]], axis=1)

    shape3 = (ny // SUBLANES, SUBLANES, LANES)
    stores = []
    half = chunks // 2
    for h in range(2):
        for c in range(h * half, (h + 1) * half):
            loads[c].wait()
            for x in range(c * per, (c + 1) * per):
                span = pl.ds(x * ny, ny)
                lanes = pl.ds(x * LANES, LANES)
                root_t = jnp.sqrt(heat[span].reshape(shape3))
                total = jnp.zeros(shape3, F32)
                volume = jnp.zeros(shape3, F32)
                for i in range(nc):
                    o = amount_v[i, span].reshape(shape3)
                    v = jnp.abs(table_v[0, i] - table_v[1, i] * root_t) * o
                    total += o
                    volume += table_v[2, i] * o
                    high, low = pieces_of(v.reshape(ny, LANES), 2)
                    split_v[pl.ds(i * ny, ny), lanes] = high
                    split_v[pl.ds(size + i * ny, ny), lanes] = low
                    split_v[pl.ds(2 * size + i * ny, ny), lanes] = high
                field_v[0, span] = total.reshape(ny, LANES)
                field_v[1, span] = volume.reshape(ny, LANES)
            lanes = pl.ds(c * per * LANES, per * LANES)
            mixed = mat(mixer, split_v[:, lanes])
            for k in range(per):
                x = c * per + k
                span = pl.ds(x * ny, ny)
                root_t = jnp.sqrt(heat[span].reshape(shape3))
                total = jnp.zeros(shape3, F32)
                for i in range(nc):
                    m = mixed[i * ny : (i + 1) * ny, k * LANES : (k + 1) * LANES].reshape(shape3)
                    psi = jnp.abs(table_v[0, i] - table_v[1, i] * root_t) * m
                    total += amount_v[i, span].reshape(shape3) * psi
                    psi_v[i, span] = psi.reshape(ny, LANES)
                field_v[2, span] = total.reshape(ny, LANES)

        span = pl.ds(h * half * rows, half * rows)
        p, t = press[span], heat[span]
        liquid = flag[span] == 1
        r = 1.0 / field_v[0, span]
        rt = 1.0 / t
        ratio_pt = p * rt
        g = ratio_pt * rt
        beta = field_v[1, span] * r
        gr = g * r
        big_a = gr * r * field_v[2, span]
        big_b = ratio_pt * beta
        z = jnp.where(liquid, big_b + 0.01, 1.0 + big_b)
        floor = big_b + 0.01
        c2 = big_b - 1.0
        c1 = big_a - 3.0 * big_b * big_b - 2.0 * big_b
        c0 = big_b * big_b + big_b * big_b * big_b - big_a * big_b
        twice = 2.0 * c2
        for _ in range(NEWT):
            value = ((z + c2) * z + c1) * z + c0
            incline = (3.0 * z + twice) * z + c1
            z = jnp.maximum(z - value / jnp.maximum(incline, 0.1), floor)
        log_ratio = jnp.log((z + (1.0 + ROOT_TWO) * big_b) / (z + (1.0 - ROOT_TWO) * big_b))
        lb = log_ratio / (ROOT_TWO * big_b)
        e0 = jnp.log(z - big_b)
        e1 = (z - 1.0 + 0.5 * big_a * lb) / beta
        e2 = gr * lb
        rho = ratio_pt / z
        mob = rho / jnp.where(liquid, visc[1], visc[0])
        mob_out[span] = mob
        field_v[0, span] = e0
        field_v[1, span] = e1
        field_v[2, span] = e2
        field_v[3, span] = mob * r
        for x in range(h * half * per, (h + 1) * half * per):
            span = pl.ds(x * ny, ny)
            e0, e1, e2, mr = (field_v[k, span].reshape(shape3) for k in range(4))
            for i in range(nc):
                value = table_v[2, i] * e1 - e0 - psi_v[i, span].reshape(shape3) * e2
                lnphi_v[i, span] = value.reshape(ny, LANES).astype(BF16)
                carried_v[i, span] = (mr * amount_v[i, span].reshape(shape3)).reshape(ny, LANES)
        span = pl.ds(h * half * rows, half * rows)
        for source, target in ((lnphi_v, lnphi_out), (carried_v, carried_out)):
            copy = pltpu.make_async_copy(
                source.at[:, span], target.at[:, span], out_sems.at[len(stores)]
            )
            copy.start()
            stores.append(copy)

    odd_g = lax.axis_index(axes[0]) % 2 == 1
    odd_s = lax.axis_index(axes[1]) % 2 == 1
    many = edge_x_out.shape[0]
    for k in range(many):
        at_low = odd_g if k == 0 else jnp.logical_not(odd_g)
        span = pl.ds(pl.multiple_of(jnp.where(at_low, 0, (nx - 1) * ny), ny), ny)
        for source, target in (
            (carried_v.at[:, span], edge_x_out.at[k, pl.ds(0, nc)]),
            (press.at[span], edge_x_out.at[k, nc]),
            (perm.at[span], edge_x_out.at[k, nc + 1]),
        ):
            copy = pltpu.make_async_copy(source, target, edge_sem.at[0])
            copy.start()
            stores.append(copy)
    low, high = pl.ds(0, nx, stride=ny), pl.ds(ny - 1, nx, stride=ny)
    for i in range(nc + 2):
        if i < nc:
            a, b = carried_v[i, low], carried_v[i, high]
        else:
            source = press if i == nc else perm
            a, b = source[low], source[high]
        edge_ya_out[i] = jnp.where(odd_s, a, b)
        edge_yb_out[i] = jnp.where(odd_s, b, a)

    row_hot, lane_hot = place_hots(loc[...], nx * ny)
    lane_hot = hot(lane_hot)

    def cells_of(field):
        return jnp.sum(jnp.where(row_hot, mat_hot(field, lane_hot), 0.0), axis=0, keepdims=True)

    p_cell = cells_of(press[...])
    pcell_out[...] = p_cell
    weight = strength[...] * cells_of(mob_out[...])
    segments = part_out.shape[1] // 2
    seg_hot = iota((segments, loc.shape[1]), 0) == seg[...]
    sums = jnp.concatenate(
        [jnp.where(seg_hot, weight, 0.0), jnp.where(seg_hot, weight * (p_cell - 1.0), 0.0)], axis=0
    )
    slot_hot = slot_hot_of(member[...], place[...])
    part_out[...] = hot_mat_nt(slot_hot.astype(BF16), sums)
    for copy in stores:
        copy.wait()


def flux_kernel(
    nx,
    ny,
    axes,
    carried,
    press,
    perm,
    pore,
    flag,
    mob,
    old,
    edge_x,
    edge_ya,
    edge_yb,
    parts,
    seg_press,
    loc,
    member,
    seg,
    strength,
    place,
    pcell,
    trans,
    visc,
    inject,
    own_press,
    order,
    exit_press,
    friction,
    resid_out,
    well_out,
    c_v,
    p_v,
    k_v,
    y_v,
    old_v,
    res_v,
    in_sems,
    out_sems,
):
    nc = carried.shape[0]
    step = ny + 2 * MARGIN
    g, s = lax.axis_index(axes[0]), lax.axis_index(axes[1])
    ng, ns = lax.axis_size(axes[0]), lax.axis_size(axes[1])
    odd_g, odd_s = g % 2, s % 2
    has_low_y, has_high_y = s > 0, s < ns - 1
    has_low_x, has_high_x = g > 0, g < ng - 1

    def inner(x):
        return pl.ds((x + 1) * step + MARGIN, ny)

    copies = []

    def go(source, target, sem):
        copy = pltpu.make_async_copy(source, target, sem)
        copy.start()
        return copy

    edge_copies = [
        go(edge_ya.at[1 - odd_s], y_v.at[1 - odd_s], in_sems.at[0]),
        go(edge_yb.at[odd_s], y_v.at[odd_s], in_sems.at[0]),
    ]
    for k in range(edge_x.shape[0]):
        mine = 1 - odd_g if k == 0 else odd_g
        plane = jnp.where(mine == 1, nx + 1, 0)
        span = pl.ds(pl.multiple_of(plane * step + MARGIN, MARGIN), ny)
        edge_copies.append(go(edge_x.at[k, mine, pl.ds(0, nc)], c_v.at[:, span], in_sems.at[0]))
        edge_copies.append(go(edge_x.at[k, mine, nc], p_v.at[span], in_sems.at[0]))
        edge_copies.append(go(edge_x.at[k, mine, nc + 1], k_v.at[span], in_sems.at[0]))
    plane_copies = []
    for x in range(nx):
        span = pl.ds(x * ny, ny)
        plane_copies.append(
            [
                go(carried.at[:, span], c_v.at[:, inner(x)], in_sems.at[1 + x]),
                go(old.at[:, span], old_v.at[:, span], in_sems.at[1 + x]),
            ]
        )
    for x in range(nx):
        span = pl.ds(x * ny, ny)
        p_v[inner(x)] = press[span]
        k_v[inner(x)] = perm[span]
    if edge_x.shape[0] == 1:
        plane = jnp.where(odd_g == 1, nx + 1, 0)
        span = pl.ds(pl.multiple_of(plane * step + MARGIN, MARGIN), ny)
        zero = jnp.zeros((ny, LANES), F32)
        p_v[span] = zero
        k_v[span] = zero
        for i in range(nc):
            c_v[i, span] = zero

    row_hot, lane_hot = place_hots(loc[...], nx * ny)
    slot_hot = slot_hot_of(member[...], place[...])
    segments = own_press.shape[1]
    seg_hot = hot(iota((segments, loc.shape[1]), 0) == seg[...])
    p_seg = jnp.sum(mat_hot(seg_press[...], seg_hot) * slot_hot, axis=0, keepdims=True)
    push = strength[...] * (pcell[...] - p_seg)
    flows = jnp.concatenate(
        [
            jnp.where(lane_hot, jnp.maximum(push, 0.0), 0.0),
            jnp.where(lane_hot, jnp.minimum(push, 0.0), 0.0),
        ],
        axis=0,
    )
    spread = hot_mat_nt(hot(row_hot), flows, 2)

    gathered = jnp.sum(parts[...], axis=0)
    own = jnp.sum(jnp.where(iota(gathered.shape, 0) == s, gathered, 0.0), axis=0, keepdims=True)
    well_p = own_press[...]
    rate = own[:, segments:] - (well_p - 1.0) * own[:, :segments]
    order_hot = hot(iota((segments, segments), 0) == order[...])
    both = mat_hot(jnp.concatenate([rate, well_p], axis=0), order_hot)
    upper = hot(iota((segments, segments), 0) <= iota((segments, segments), 1))
    running = mat_hot(both[0:1], upper)
    press_ord = both[1:2]
    after = hot(iota((segments, segments), 0) == iota((segments, segments), 1) + 1)
    last = iota((1, segments), 1) == segments - 1
    nexts = jnp.where(last, exit_press[0], mat_hot(press_ord, after))
    res_ord = press_ord - nexts - friction[0] * running * jnp.abs(running)
    well_out[...] = sum(mat_nt(piece, order_hot) for piece in pieces_of(res_ord, 3))

    for copy in edge_copies:
        copy.wait()
    for side in range(2):
        start = step + (MARGIN - 1 if side == 0 else MARGIN + ny)
        span = pl.ds(start, nx, stride=step)
        for i in range(nc):
            c_v[i, span] = y_v[side, i]
        p_v[span] = y_v[side, nc]
        k_v[span] = jnp.where(has_low_y if side == 0 else has_high_y, y_v[side, nc + 1], 0.0)

    lane = iota((ny, LANES), 1)
    share = 1.0 / sum(jnp.full((ny, LANES), inject[i], F32) for i in range(nc))
    stores = []
    for x in range(nx):
        base = (x + 1) * step + MARGIN
        here = pl.ds(base, ny)
        rows = pl.ds(x * ny, ny)
        p_a, k_a = p_v[here], k_v[here]

        def face(p_b, k_b, axis):
            t = 2.0 * trans[axis] * k_a * k_b / (k_a + k_b)
            flow = t * (p_a - p_b)
            return jnp.maximum(flow, 0.0), jnp.minimum(flow, 0.0)

        spots = [
            (pl.ds(base + step, ny), 0),
            (pl.ds(base - step, ny), 0),
            (pl.ds(base + 1, ny), 1),
            (pl.ds(base - 1, ny), 1),
        ]
        centre = pore[rows] * jnp.where(flag[rows] == 1, visc[1], visc[0])
        centre += spread[x * ny : (x + 1) * ny, :LANES]
        ins = []
        for k, (spot, axis) in enumerate(spots):
            k_b = k_v[spot]
            if k == 0 and x == nx - 1:
                k_b = jnp.where(has_high_x, k_b, 0.0)
            if k == 1 and x == 0:
                k_b = jnp.where(has_low_x, k_b, 0.0)
            out, into = face(p_v[spot], k_b, axis)
            centre += out
            ins.append(into)
        for shift, edge in ((LANES - 1, LANES - 1), (1, 0)):
            k_b = jnp.where(lane == edge, 0.0, pltpu.roll(k_a, shift, 1))
            out, into = face(pltpu.roll(p_a, shift, 1), k_b, 2)
            centre += out
            ins.append(into)
        pushed = mob[rows] * spread[x * ny : (x + 1) * ny, LANES:] * share
        for copy in plane_copies[x]:
            copy.wait()
        if x + 1 < nx:
            for copy in plane_copies[x + 1]:
                copy.wait()
            plane_copies[x + 1] = []
        for i in range(nc):
            c = c_v[i, here]
            value = centre * c - old_v[i, rows] + inject[i] * pushed
            for into, (spot, _) in zip(ins[:4], spots):
                value += into * c_v[i, spot]
            value += ins[4] * pltpu.roll(c, LANES - 1, 1)
            value += ins[5] * pltpu.roll(c, 1, 1)
            res_v[i, rows] = value
        stores.append(go(res_v.at[:, rows], resid_out.at[:, rows], out_sems.at[x]))
    for copy in stores:
        copy.wait()


def pairs_of(count, other):
    return [[i, (i + 1) % count] for i in range(1 if other else 0, count, 2)]


def per_device(
    amount,
    press,
    heat,
    flag,
    perm,
    pore,
    old,
    trans,
    visc,
    crit,
    attract,
    covol,
    slope,
    coupling,
    inject,
    locale,
    member,
    seg,
    strength,
    place,
    order,
    seg_press,
    exit_press,
    friction,
):
    axes = ("grp", "sub")
    nc, nx, ny, nz = amount.shape
    ng, ns = lax.axis_size("grp"), lax.axis_size("sub")
    rows = nx * ny
    perfs = locale.shape[0]
    wells, segments = place.shape[1], seg_press.shape[1]
    flat = lambda a: a.reshape(a.shape[:-3] + (rows, nz))
    line = lambda a: a.reshape(1, perfs)
    vm = pl.BlockSpec(memory_space=pltpu.VMEM)
    sm = pl.BlockSpec(memory_space=pltpu.SMEM)
    hbm = pl.BlockSpec(memory_space=pl.ANY)
    many_x = 1 if ng == 2 else 2

    amount, old = flat(amount), flat(old)
    press, heat, flag, perm, pore = (flat(a) for a in (press, heat, flag, perm, pore))
    locale, member, seg, strength = (line(a) for a in (locale, member, seg, strength))

    all_press = lax.all_gather(seg_press, "sub", tiled=True)

    lnphi, carried, mob, edge_x, edge_ya, edge_yb, part, pcell = pl.pallas_call(
        functools.partial(phase_kernel, nx, ny, axes),
        out_shape=(
            jax.ShapeDtypeStruct((nc, rows, nz), BF16),
            jax.ShapeDtypeStruct((nc, rows, nz), F32),
            jax.ShapeDtypeStruct((rows, nz), F32),
            jax.ShapeDtypeStruct((many_x, nc + 2, ny, nz), F32),
            jax.ShapeDtypeStruct((nc + 2, nx, nz), F32),
            jax.ShapeDtypeStruct((nc + 2, nx, nz), F32),
            jax.ShapeDtypeStruct((wells, 2 * segments), F32),
            jax.ShapeDtypeStruct((1, perfs), F32),
        ),
        in_specs=[hbm] + [vm] * 4 + [sm] * 5 + [vm] * 6,
        out_specs=(hbm, hbm, vm, hbm, vm, vm, vm, vm),
        scratch_shapes=[
            pltpu.VMEM((nc, rows, nz), F32),
            pltpu.VMEM((3 * nc * ny, nx * nz), BF16),
            pltpu.VMEM((nc, rows, nz), F32),
            pltpu.VMEM((nc, rows, nz), F32),
            pltpu.VMEM((nc, rows, nz), BF16),
            pltpu.VMEM((4, rows, nz), F32),
            pltpu.VMEM((3, nc, SUBLANES, LANES), F32),
            pltpu.SemaphoreType.DMA((nx // 2,)),
            pltpu.SemaphoreType.DMA((4,)),
            pltpu.SemaphoreType.DMA((1,)),
        ],
        compiler_params=pltpu.CompilerParams(vmem_limit_bytes=VMEM_LIMIT),
        name="phase",
    )(
        amount, press, heat, flag, perm, visc, crit, attract, covol, slope, coupling,
        locale, member, seg, strength, place,
    )

    groups_a, groups_b = pairs_of(ns, False), pairs_of(ns, True)
    got_ya = lax.all_gather(edge_ya, "sub", axis_index_groups=groups_a)
    got_yb = lax.all_gather(edge_yb, "sub", axis_index_groups=groups_b)
    got_x = [
        lax.all_gather(edge_x[k], "grp", axis_index_groups=pairs_of(ng, k == 1))
        for k in range(many_x)
    ]
    got_x = got_x[0][None] if many_x == 1 else jnp.stack(got_x)
    parts = lax.all_gather(part, "sub")

    resid, well = pl.pallas_call(
        functools.partial(flux_kernel, nx, ny, axes),
        out_shape=(
            jax.ShapeDtypeStruct((nc, rows, nz), F32),
            jax.ShapeDtypeStruct((1, segments), F32),
        ),
        in_specs=[hbm] + [vm] * 5 + [hbm] * 4 + [vm] * 8 + [sm] * 3 + [vm] * 2 + [sm] * 2,
        out_specs=(hbm, vm),
        scratch_shapes=[
            pltpu.VMEM((nc, (nx + 2) * (ny + 2 * MARGIN), nz), F32),
            pltpu.VMEM(((nx + 2) * (ny + 2 * MARGIN), nz), F32),
            pltpu.VMEM(((nx + 2) * (ny + 2 * MARGIN), nz), F32),
            pltpu.VMEM((2, nc + 2, nx, nz), F32),
            pltpu.VMEM((nc, rows, nz), F32),
            pltpu.VMEM((nc, rows, nz), F32),
            pltpu.SemaphoreType.DMA((1 + nx,)),
            pltpu.SemaphoreType.DMA((nx,)),
        ],
        compiler_params=pltpu.CompilerParams(vmem_limit_bytes=VMEM_LIMIT),
        name="flux",
    )(
        carried, press, perm, pore, flag, mob, old, got_x, got_ya, got_yb, parts, all_press,
        locale, member, seg, strength, place, pcell,
        trans, visc, inject, seg_press, order, exit_press, friction,
    )
    block = (nc, nx, ny, nz)
    return resid.reshape(block), lnphi.reshape(block), well


def solution(mesh):
    cells, parts = P("grp", "sub", None), P(None, "grp", "sub", None)
    listed = P(("grp", "sub"))
    row = P(("grp", "sub"), None)
    in_specs = (
        (parts,) + (cells,) * 5 + (parts,) + (P(),) * 8
        + (listed, row, listed, listed, P("grp", None), row, row, listed, listed)
    )
    return jax.shard_map(
        per_device, mesh=mesh, in_specs=in_specs, out_specs=(parts, parts, row), check_vma=False
    )
```

```python
import functools
import math

import jax
import jax.numpy as jnp
from jax import lax
from jax.experimental import pallas as pl
from jax.experimental.pallas import tpu as pltpu
from jax.sharding import PartitionSpec as P

NEWT = 8
ROOT_TWO = math.sqrt(2.0)
LANES = 128
SUBLANES = 8
F32 = jnp.float32
BF16 = jnp.bfloat16
VMEM_LIMIT = 48 * 1024 * 1024
MARGIN = 8
SMALL, FIELDS = 14, 4


def iota(shape, dim):
    return lax.broadcasted_iota(jnp.int32, shape, dim)


def pieces_of(x, count):
    out = []
    for _ in range(count):
        piece = x.astype(BF16)
        out.append(piece)
        x = x - piece.astype(F32)
    return out


def mat(a, b):
    return lax.dot_general(a, b, (((1,), (0,)), ((), ())), preferred_element_type=F32)


def mat_nt(a, b):
    return lax.dot_general(a, b, (((1,), (1,)), ((), ())), preferred_element_type=F32)


def mat_hot(x, hot, count=3):
    return sum(mat(piece, hot) for piece in pieces_of(x, count))


def hot_mat_nt(hot, x, count=3):
    return sum(mat_nt(hot, piece) for piece in pieces_of(x, count))


def inverse(x):
    r = pl.reciprocal(x, approx=True)
    return r * (2.0 - x * r)


def hot(cond):
    return jnp.where(cond, 1.0, 0.0).astype(BF16)


def place_hots(loc, rows):
    n = loc.shape[1]
    row_hot = iota((rows, n), 0) == loc // LANES
    lane_hot = iota((LANES, n), 0) == loc % LANES
    return row_hot, lane_hot


def slot_hot_of(member, place):
    wells = place.shape[1]
    slot_of = hot(iota((wells, wells), 0) == place)
    member_hot = hot(iota((wells, member.shape[1]), 0) == member)
    return mat(slot_of, member_hot)


def phase_kernel(
    nx,
    ny,
    axes,
    amount,
    *rest,
):
    count = SMALL + FIELDS
    sources, rest = rest[:count], rest[count:]
    (
        lnphi_out,
        carried_out,
        mob_out,
        edge_x_out,
        edge_ya_out,
        edge_yb_out,
        part_out,
        pcell_out,
        consts_out,
    ) = rest[:9]
    targets, rest = rest[9 : 9 + count], rest[9 + count :]
    amount_v, split_v, psi_v, lnphi_v, field_v, table_v, small_sems, in_sems, out_sems = rest
    visc, crit, attract, covol, slope, trans, inject = targets[:7]
    coupling, loc, member, seg, strength, place, own_press = targets[7 : SMALL]
    heat, press, flag, perm = targets[SMALL :]
    nc = amount.shape[0]
    per = 2
    chunks = nx // per
    rows = per * ny

    def go(source, target, sem):
        copy = pltpu.make_async_copy(source, target, sem)
        copy.start()
        return copy

    small = [go(a, b, small_sems.at[k]) for k, (a, b) in enumerate(zip(sources, targets))]
    heat_load, press_load, flag_load, perm_load = small[SMALL :]
    loads = []
    for c in range(chunks):
        span = pl.ds(c * rows, rows)
        loads.append(go(amount.at[:, span], amount_v.at[:, span], in_sems.at[c]))
    for copy in small[: SMALL]:
        copy.wait()

    for i in range(nc):
        root = jnp.sqrt(jnp.full((SUBLANES, LANES), attract[i], F32))
        kappa = jnp.full((SUBLANES, LANES), slope[i], F32)
        tc = jnp.full((SUBLANES, LANES), crit[i], F32)
        table_v[0, i] = root * (1.0 + kappa)
        table_v[1, i] = root * kappa / jnp.sqrt(tc)
        table_v[2, i] = jnp.full((SUBLANES, LANES), covol[i], F32)

    total = sum(inject[i] for i in range(nc))
    share = 1.0 / jnp.full((SUBLANES, LANES), total, F32)
    numbers = [trans[0], trans[1], trans[2], visc[0], visc[1]]
    for i in range(nc):
        consts_out[i] = inject[i] * share
    for i, number in enumerate(numbers):
        consts_out[nc + i] = jnp.full((SUBLANES, LANES), number, F32)

    size = nc * ny
    spread = hot(iota((size, nc), 0) // ny == iota((size, nc), 1))
    same_row = iota((size, size), 0) % ny == iota((size, size), 1) % ny
    mixers = []
    for piece in pieces_of(1.0 - coupling[...], 2):
        wide = mat(spread, piece).astype(BF16)
        mixers.append(jnp.where(same_row, mat_nt(wide, spread), 0.0).astype(BF16))
    mixer = jnp.concatenate([mixers[0], mixers[0], mixers[1]], axis=1)

    shape3 = (ny // SUBLANES, SUBLANES, LANES)
    stores = []
    half = chunks // 2
    heat_load.wait()
    for h in range(2):
        for c in range(h * half, (h + 1) * half):
            loads[c].wait()
            for x in range(c * per, (c + 1) * per):
                span = pl.ds(x * ny, ny)
                lanes = pl.ds(x * LANES, LANES)
                root_t = jnp.sqrt(heat[span].reshape(shape3))
                total = jnp.zeros(shape3, F32)
                volume = jnp.zeros(shape3, F32)
                for i in range(nc):
                    o = amount_v[i, span].reshape(shape3)
                    v = jnp.abs(table_v[0, i] - table_v[1, i] * root_t) * o
                    total += o
                    volume += table_v[2, i] * o
                    high, low = pieces_of(v.reshape(ny, LANES), 2)
                    split_v[pl.ds(i * ny, ny), lanes] = high
                    split_v[pl.ds(size + i * ny, ny), lanes] = low
                    split_v[pl.ds(2 * size + i * ny, ny), lanes] = high
                field_v[0, span] = total.reshape(ny, LANES)
                field_v[1, span] = volume.reshape(ny, LANES)
            lanes = pl.ds(c * per * LANES, per * LANES)
            mixed = mat(mixer, split_v[:, lanes])
            for k in range(per):
                x = c * per + k
                span = pl.ds(x * ny, ny)
                root_t = jnp.sqrt(heat[span].reshape(shape3))
                total = jnp.zeros(shape3, F32)
                for i in range(nc):
                    m = mixed[i * ny : (i + 1) * ny, k * LANES : (k + 1) * LANES].reshape(shape3)
                    psi = jnp.abs(table_v[0, i] - table_v[1, i] * root_t) * m
                    total += amount_v[i, span].reshape(shape3) * psi
                    psi_v[i, span] = psi.reshape(ny, LANES)
                field_v[2, span] = total.reshape(ny, LANES)

        if h == 0:
            press_load.wait()
            flag_load.wait()
        span = pl.ds(h * half * rows, half * rows)
        p, t = press[span], heat[span]
        liquid = flag[span] == 1
        r = inverse(field_v[0, span])
        rt = inverse(t)
        ratio_pt = p * rt
        g = ratio_pt * rt
        beta = field_v[1, span] * r
        gr = g * r
        big_a = gr * r * field_v[2, span]
        big_b = ratio_pt * beta
        z = jnp.where(liquid, big_b + 0.01, 1.0 + big_b)
        floor = big_b + 0.01
        c2 = big_b - 1.0
        c1 = big_a - 3.0 * big_b * big_b - 2.0 * big_b
        c0 = big_b * big_b + big_b * big_b * big_b - big_a * big_b
        twice = 2.0 * c2
        for _ in range(NEWT):
            value = ((z + c2) * z + c1) * z + c0
            incline = (3.0 * z + twice) * z + c1
            z = jnp.maximum(z - value * inverse(jnp.maximum(incline, 0.1)), floor)
        log_ratio = jnp.log(
            (z + (1.0 + ROOT_TWO) * big_b) * inverse(z + (1.0 - ROOT_TWO) * big_b)
        )
        lb = log_ratio * inverse(ROOT_TWO * big_b)
        e0 = jnp.log(z - big_b)
        e1 = (z - 1.0 + 0.5 * big_a * lb) * inverse(beta)
        e2 = gr * lb
        mob = ratio_pt * inverse(z * jnp.where(liquid, visc[1], visc[0]))
        mob_out[span] = mob
        field_v[0, span] = e0
        field_v[1, span] = e1
        field_v[2, span] = e2
        field_v[3, span] = mob * r
        for x in range(h * half * per, (h + 1) * half * per):
            span = pl.ds(x * ny, ny)
            e0, e1, e2, mr = (field_v[k, span].reshape(shape3) for k in range(4))
            for i in range(nc):
                value = table_v[2, i] * e1 - e0 - psi_v[i, span].reshape(shape3) * e2
                lnphi_v[i, span] = value.reshape(ny, LANES).astype(BF16)
                carried = (mr * amount_v[i, span].reshape(shape3)).reshape(ny, LANES)
                carried_out[i, pl.ds(MARGIN + x * ny, ny)] = carried
        span = pl.ds(h * half * rows, half * rows)
        stores.append(go(lnphi_v.at[:, span], lnphi_out.at[:, span], out_sems.at[h]))

    perm_load.wait()
    odd_g = lax.axis_index(axes[0]) % 2 == 1
    odd_s = lax.axis_index(axes[1]) % 2 == 1
    for k in range(edge_x_out.shape[0]):
        at_low = odd_g if k == 0 else jnp.logical_not(odd_g)
        start = pl.multiple_of(jnp.where(at_low, 0, (nx - 1) * ny), ny)
        for i in range(nc):
            edge_x_out[k, i] = carried_out[i, pl.ds(start + MARGIN, ny)]
        edge_x_out[k, nc] = press[pl.ds(start, ny)]
        edge_x_out[k, nc + 1] = perm[pl.ds(start, ny)]
    for i in range(nc + 2):
        source = carried_out.at[i] if i < nc else press if i == nc else perm
        skip = MARGIN if i < nc else 0
        low = source[pl.ds(skip, nx, stride=ny)]
        high = source[pl.ds(skip + ny - 1, nx, stride=ny)]
        edge_ya_out[i] = jnp.where(odd_s, low, high)
        edge_yb_out[i] = jnp.where(odd_s, high, low)

    row_hot, lane_hot = place_hots(loc[...], nx * ny)
    lane_hot = hot(lane_hot)

    def cells_of(field):
        return jnp.sum(jnp.where(row_hot, mat_hot(field, lane_hot), 0.0), axis=0, keepdims=True)

    p_cell = cells_of(press[...])
    pcell_out[...] = p_cell
    weight = strength[...] * cells_of(mob_out[...])
    segments = own_press.shape[1]
    perfs = loc.shape[1]
    place_of = iota((LANES, perfs), 0)
    sums = jnp.where(place_of == seg[...], weight, 0.0)
    sums += jnp.where(place_of == seg[...] + segments, weight * (p_cell - 1.0), 0.0)
    slot_hot = slot_hot_of(member[...], place[...])
    shift = hot(iota((segments, LANES), 0) + 2 * segments == iota((segments, LANES), 1))
    part_out[...] = hot_mat_nt(slot_hot.astype(BF16), sums) + mat_hot(own_press[...], shift)
    for copy in stores:
        copy.wait()


def flux_kernel(
    nx,
    ny,
    axes,
    many_x,
    carried,
    press,
    perm,
    pore,
    flag,
    mob,
    old,
    edge_ya,
    edge_yb,
    well_rows,
    loc,
    member,
    seg,
    strength,
    place,
    pcell,
    consts,
    own_press,
    order,
    exit_press,
    friction,
    *rest,
):
    edge_x, (resid_out, well_out, y_v, res_v, out_sems) = rest[:many_x], rest[many_x:]
    nc = carried.shape[0]
    g, s = lax.axis_index(axes[0]), lax.axis_index(axes[1])
    ng, ns = lax.axis_size(axes[0]), lax.axis_size(axes[1])
    odd_g, odd_s = g % 2 == 1, s % 2 == 1
    has_low_y, has_high_y = s > 0, s < ns - 1
    has_low_x, has_high_x = g > 0, g < ng - 1

    for i in range(nc + 2):
        a, b = edge_ya[i], edge_yb[i]
        low, high = jnp.where(odd_s, a, b), jnp.where(odd_s, b, a)
        if i == nc + 1:
            low, high = jnp.where(has_low_y, low, 0.0), jnp.where(has_high_y, high, 0.0)
        y_v[0, i] = low
        y_v[1, i] = high

    def side_x(i, high):
        if many_x == 1:
            return edge_x[0][i]
        return jnp.where(odd_g != high, edge_x[0][i], edge_x[1][i])

    row_hot, lane_hot = place_hots(loc[...], nx * ny)
    slot_hot = slot_hot_of(member[...], place[...])
    segments = own_press.shape[1]
    gathered = well_rows[...]
    seg_hot = hot(iota((LANES, loc.shape[1]), 0) == seg[...] + 2 * segments)
    p_seg = jnp.sum(mat_hot(gathered, seg_hot) * slot_hot, axis=0, keepdims=True)
    push = strength[...] * (pcell[...] - p_seg)
    flows = jnp.concatenate(
        [
            jnp.where(lane_hot, jnp.maximum(push, 0.0), 0.0),
            jnp.where(lane_hot, jnp.minimum(push, 0.0), 0.0),
        ],
        axis=0,
    )
    spread = hot_mat_nt(hot(row_hot), flows, 2)

    own = jnp.sum(gathered, axis=0, keepdims=True)
    well_p = own_press[...]
    rate = own[:, segments : 2 * segments] - (well_p - 1.0) * own[:, :segments]
    order_hot = hot(iota((segments, segments), 0) == order[...])
    both = mat_hot(jnp.concatenate([rate, well_p], axis=0), order_hot)
    upper = hot(iota((segments, segments), 0) <= iota((segments, segments), 1))
    running = mat_hot(both[0:1], upper)
    press_ord = both[1:2]
    after = hot(iota((segments, segments), 0) == iota((segments, segments), 1) + 1)
    last = iota((1, segments), 1) == segments - 1
    nexts = jnp.where(last, exit_press[...], mat_hot(press_ord, after))
    res_ord = press_ord - nexts - friction[...] * running * jnp.abs(running)
    well_out[...] = sum(mat_nt(piece, order_hot) for piece in pieces_of(res_ord, 3))

    lane = iota((ny, LANES), 1)
    row = iota((ny, LANES), 0)
    first, final = row == 0, row == ny - 1

    def const(k):
        return jnp.concatenate([consts[k]] * (ny // SUBLANES), axis=0)

    stores = []
    for x in range(nx):
        rows = pl.ds(x * ny, ny)
        p_a, k_a = press[rows], perm[rows]
        twice_k = 2.0 * k_a

        def face(p_b, k_b, axis):
            t = const(nc + axis) * (twice_k * k_b) * inverse(k_a + k_b)
            flow = t * (p_a - p_b)
            return jnp.maximum(flow, 0.0), jnp.minimum(flow, 0.0)

        def other_x(field, i, high):
            at = x + 1 if high else x - 1
            return field[pl.ds(at * ny, ny)] if 0 <= at < nx else side_x(i, high)

        def other_y(field, i, high):
            if high:
                return jnp.where(final, y_v[1, i, pl.ds(x, 1)], pltpu.roll(field, ny - 1, 0))
            return jnp.where(first, y_v[0, i, pl.ds(x, 1)], pltpu.roll(field, 1, 0))

        centre = pore[rows] * jnp.where(flag[rows] == 1, const(nc + 4), const(nc + 3))
        centre += spread[x * ny : (x + 1) * ny, :LANES]
        ins = []
        for high in (True, False):
            p_b, k_b = other_x(press, nc, high), other_x(perm, nc + 1, high)
            if x == nx - 1 and high:
                k_b = jnp.where(has_high_x, k_b, 0.0)
            if x == 0 and not high:
                k_b = jnp.where(has_low_x, k_b, 0.0)
            ins.append(face(p_b, k_b, 0))
        for high in (True, False):
            ins.append(face(other_y(p_a, nc, high), other_y(k_a, nc + 1, high), 1))
        for shift, edge in ((LANES - 1, LANES - 1), (1, 0)):
            k_b = jnp.where(lane == edge, 0.0, pltpu.roll(k_a, shift, 1))
            ins.append(face(pltpu.roll(p_a, shift, 1), k_b, 2))
        for out, _ in ins:
            centre += out
        ins = [into for _, into in ins]
        pushed = mob[rows] * spread[x * ny : (x + 1) * ny, LANES:]
        for i in range(nc):
            base = MARGIN + x * ny
            c = carried[i, pl.ds(base, ny)]
            value = centre * c - old[i, rows] + const(i) * pushed
            for k, high in ((0, True), (1, False)):
                at = x + 1 if high else x - 1
                inside = 0 <= at < nx
                c_b = carried[i, pl.ds(MARGIN + at * ny, ny)] if inside else side_x(i, high)
                value += ins[k] * c_b
            up, down = carried[i, pl.ds(base + 1, ny)], carried[i, pl.ds(base - 1, ny)]
            value += ins[2] * jnp.where(final, y_v[1, i, pl.ds(x, 1)], up)
            value += ins[3] * jnp.where(first, y_v[0, i, pl.ds(x, 1)], down)
            value += ins[4] * pltpu.roll(c, LANES - 1, 1)
            value += ins[5] * pltpu.roll(c, 1, 1)
            res_v[i, rows] = value
        copy = pltpu.make_async_copy(res_v.at[:, rows], resid_out.at[:, rows], out_sems.at[x])
        copy.start()
        stores.append(copy)
    for copy in stores:
        copy.wait()


def swaps_of(count, other):
    pairs = [(i, i + 1) for i in range(1 if other else 0, count - 1, 2)]
    return pairs + [(b, a) for a, b in pairs]


def per_device(
    amount,
    press,
    heat,
    flag,
    perm,
    pore,
    old,
    trans,
    visc,
    crit,
    attract,
    covol,
    slope,
    coupling,
    inject,
    locale,
    member,
    seg,
    strength,
    place,
    order,
    seg_press,
    exit_press,
    friction,
):
    axes = ("grp", "sub")
    nc, nx, ny, nz = amount.shape
    ng, ns = lax.axis_size("grp"), lax.axis_size("sub")
    rows = nx * ny
    perfs = locale.shape[0]
    wells, segments = place.shape[1], seg_press.shape[1]
    flat = lambda a: a.reshape(a.shape[:-3] + (rows, nz))
    line = lambda a: a.reshape(1, perfs)
    vm = pl.BlockSpec(memory_space=pltpu.VMEM)
    hbm = pl.BlockSpec(memory_space=pltpu.HBM)
    many_x = 1 if ng == 2 else 2

    amount, old = flat(amount), flat(old)
    press, heat, flag, perm, pore = (flat(a) for a in (press, heat, flag, perm, pore))
    locale, member, seg, strength = (line(a) for a in (locale, member, seg, strength))
    exit_press, friction = exit_press.reshape(1, 1), friction.reshape(1, 1)

    sources = (
        visc, crit, attract, covol, slope, trans, inject,
        coupling, locale, member, seg, strength, place, seg_press,
        heat, press, flag, perm,
    )
    kept = [
        pltpu.SMEM(a.shape, a.dtype) if a.ndim == 1 else pltpu.VMEM(a.shape, a.dtype)
        for a in sources
    ]
    in_hbm = lambda a: pltpu.with_memory_space_constraint(a, pltpu.HBM)

    lnphi, carried, mob, edge_x, edge_ya, edge_yb, part, pcell, consts = pl.pallas_call(
        functools.partial(phase_kernel, nx, ny, axes),
        out_shape=(
            jax.ShapeDtypeStruct((nc, rows, nz), BF16),
            jax.ShapeDtypeStruct((nc, rows + 2 * MARGIN, nz), F32),
            jax.ShapeDtypeStruct((rows, nz), F32),
            jax.ShapeDtypeStruct((many_x, nc + 2, ny, nz), F32),
            jax.ShapeDtypeStruct((nc + 2, nx, nz), F32),
            jax.ShapeDtypeStruct((nc + 2, nx, nz), F32),
            jax.ShapeDtypeStruct((wells, LANES), F32),
            jax.ShapeDtypeStruct((1, perfs), F32),
            jax.ShapeDtypeStruct((nc + 8, SUBLANES, LANES), F32),
        ),
        in_specs=[hbm] * (1 + len(sources)),
        out_specs=(hbm,) + (vm,) * 8,
        scratch_shapes=[
            *kept,
            pltpu.VMEM((nc, rows, nz), F32),
            pltpu.VMEM((3 * nc * ny, nx * nz), BF16),
            pltpu.VMEM((nc, rows, nz), F32),
            pltpu.VMEM((nc, rows, nz), BF16),
            pltpu.VMEM((4, rows, nz), F32),
            pltpu.VMEM((3, nc, SUBLANES, LANES), F32),
            pltpu.SemaphoreType.DMA((len(sources),)),
            pltpu.SemaphoreType.DMA((nx // 2,)),
            pltpu.SemaphoreType.DMA((2,)),
        ],
        compiler_params=pltpu.CompilerParams(vmem_limit_bytes=VMEM_LIMIT),
        name="phase",
    )(in_hbm(amount), *(in_hbm(a) for a in sources))

    well_rows = lax.all_to_all(part, "sub", split_axis=0, concat_axis=0, tiled=True)
    got_x = [lax.ppermute(edge_x[k], "grp", swaps_of(ng, k == 1)) for k in range(many_x)]
    got_yb = lax.ppermute(edge_yb, "sub", swaps_of(ns, True))
    got_ya = lax.ppermute(edge_ya, "sub", swaps_of(ns, False))

    resid, well = pl.pallas_call(
        functools.partial(flux_kernel, nx, ny, axes, many_x),
        out_shape=(
            jax.ShapeDtypeStruct((nc, rows, nz), F32),
            jax.ShapeDtypeStruct((1, segments), F32),
        ),
        in_specs=[vm] * (21 + many_x),
        out_specs=(hbm, vm),
        scratch_shapes=[
            pltpu.VMEM((2, nc + 2, nx, nz), F32),
            pltpu.VMEM((nc, rows, nz), F32),
            pltpu.SemaphoreType.DMA((nx,)),
        ],
        compiler_params=pltpu.CompilerParams(vmem_limit_bytes=VMEM_LIMIT),
        name="flux",
    )(
        carried, press, perm, pore, flag, mob, old, got_ya, got_yb, well_rows,
        locale, member, seg, strength, place, pcell,
        consts, seg_press, order, exit_press, friction, *got_x,
    )
    block = (nc, nx, ny, nz)
    return resid.reshape(block), lnphi.reshape(block), well


def solution(mesh):
    cells, parts = P("grp", "sub", None), P(None, "grp", "sub", None)
    listed = P(("grp", "sub"))
    row = P(("grp", "sub"), None)
    in_specs = (
        (parts,) + (cells,) * 5 + (parts,) + (P(),) * 8
        + (listed, row, listed, listed, P("grp", None), row, row, listed, listed)
    )
    return jax.shard_map(
        per_device, mesh=mesh, in_specs=in_specs, out_specs=(parts, parts, row), check_vma=False
    )
```

```python
import functools
import math

import jax
import jax.numpy as jnp
from jax import lax
from jax.experimental import pallas as pl
from jax.experimental.pallas import tpu as pltpu
from jax.sharding import PartitionSpec as P

NEWT = 8
ROOT_TWO = math.sqrt(2.0)
LANES = 128
SUBLANES = 8
F32 = jnp.float32
BF16 = jnp.bfloat16
VMEM_LIMIT = 48 * 1024 * 1024
MARGIN = 8
SMALL, FIELDS = 14, 4


def iota(shape, dim):
    return lax.broadcasted_iota(jnp.int32, shape, dim)


def pieces_of(x, count):
    out = []
    for _ in range(count):
        piece = x.astype(BF16)
        out.append(piece)
        x = x - piece.astype(F32)
    return out


def mat(a, b):
    return lax.dot_general(a, b, (((1,), (0,)), ((), ())), preferred_element_type=F32)


def mat_nt(a, b):
    return lax.dot_general(a, b, (((1,), (1,)), ((), ())), preferred_element_type=F32)


def mat_hot(x, hot, count=3):
    return sum(mat(piece, hot) for piece in pieces_of(x, count))


def hot_mat_nt(hot, x, count=3):
    return sum(mat_nt(hot, piece) for piece in pieces_of(x, count))


def inverse(x):
    r = pl.reciprocal(x, approx=True)
    return r * (2.0 - x * r)


def hot(cond):
    return jnp.where(cond, 1.0, 0.0).astype(BF16)


def place_hots(loc, rows):
    n = loc.shape[1]
    row_hot = iota((rows, n), 0) == loc // LANES
    lane_hot = iota((LANES, n), 0) == loc % LANES
    return row_hot, lane_hot


def slot_hot_of(member, place):
    wells = place.shape[1]
    slot_of = hot(iota((wells, wells), 0) == wells - 1 - place)
    member_hot = hot(iota((wells, member.shape[1]), 0) == member)
    return mat(slot_of, member_hot)


def phase_kernel(
    nx,
    ny,
    axes,
    amount,
    *rest,
):
    count = SMALL + FIELDS
    sources, rest = rest[:count], rest[count:]
    (
        lnphi_out,
        carried_out,
        mob_out,
        edge_x_out,
        edge_ya_out,
        edge_yb_out,
        part_out,
        pcell_out,
        consts_out,
    ) = rest[:9]
    targets, rest = rest[9 : 9 + count], rest[9 + count :]
    amount_v, split_v, psi_v, lnphi_v, field_v, table_v, small_sems, in_sems, out_sems = rest
    visc, crit, attract, covol, slope, trans, inject = targets[:7]
    coupling, loc, member, seg, strength, place, own_press = targets[7 : SMALL]
    heat, press, flag, perm = targets[SMALL :]
    nc = amount.shape[0]
    per = 2
    chunks = nx // per
    rows = per * ny

    def go(source, target, sem):
        copy = pltpu.make_async_copy(source, target, sem)
        copy.start()
        return copy

    small = [go(a, b, small_sems.at[k]) for k, (a, b) in enumerate(zip(sources, targets))]
    heat_load, press_load, flag_load, perm_load = small[SMALL :]
    loads = []
    for c in range(chunks):
        span = pl.ds(c * rows, rows)
        loads.append(go(amount.at[:, span], amount_v.at[:, span], in_sems.at[c]))
    for copy in small[: SMALL]:
        copy.wait()

    for i in range(nc):
        root = jnp.sqrt(jnp.full((SUBLANES, LANES), attract[i], F32))
        kappa = jnp.full((SUBLANES, LANES), slope[i], F32)
        tc = jnp.full((SUBLANES, LANES), crit[i], F32)
        table_v[0, i] = root * (1.0 + kappa)
        table_v[1, i] = root * kappa / jnp.sqrt(tc)
        table_v[2, i] = jnp.full((SUBLANES, LANES), covol[i], F32)

    total = sum(inject[i] for i in range(nc))
    share = 1.0 / jnp.full((SUBLANES, LANES), total, F32)
    numbers = [trans[0], trans[1], trans[2], visc[0], visc[1]]
    for i in range(nc):
        consts_out[i] = inject[i] * share
    for i, number in enumerate(numbers):
        consts_out[nc + i] = jnp.full((SUBLANES, LANES), number, F32)

    size = nc * ny
    spread = hot(iota((size, nc), 0) // ny == iota((size, nc), 1))
    same_row = iota((size, size), 0) % ny == iota((size, size), 1) % ny
    mixers = []
    for piece in pieces_of(1.0 - coupling[...], 2):
        wide = mat(spread, piece).astype(BF16)
        mixers.append(jnp.where(same_row, mat_nt(wide, spread), 0.0).astype(BF16))
    mixer = jnp.concatenate([mixers[0], mixers[0], mixers[1]], axis=1)

    shape3 = (ny // SUBLANES, SUBLANES, LANES)
    stores = []
    half = chunks // 2
    heat_load.wait()
    for h in range(2):
        for c in range(h * half, (h + 1) * half):
            loads[c].wait()
            for x in range(c * per, (c + 1) * per):
                span = pl.ds(x * ny, ny)
                lanes = pl.ds(x * LANES, LANES)
                root_t = jnp.sqrt(heat[span].reshape(shape3))
                total = jnp.zeros(shape3, F32)
                volume = jnp.zeros(shape3, F32)
                for i in range(nc):
                    o = amount_v[i, span].reshape(shape3)
                    v = jnp.abs(table_v[0, i] - table_v[1, i] * root_t) * o
                    total += o
                    volume += table_v[2, i] * o
                    high, low = pieces_of(v.reshape(ny, LANES), 2)
                    split_v[pl.ds(i * ny, ny), lanes] = high
                    split_v[pl.ds(size + i * ny, ny), lanes] = low
                    split_v[pl.ds(2 * size + i * ny, ny), lanes] = high
                field_v[0, span] = total.reshape(ny, LANES)
                field_v[1, span] = volume.reshape(ny, LANES)
            lanes = pl.ds(c * per * LANES, per * LANES)
            mixed = mat(mixer, split_v[:, lanes])
            for k in range(per):
                x = c * per + k
                span = pl.ds(x * ny, ny)
                root_t = jnp.sqrt(heat[span].reshape(shape3))
                total = jnp.zeros(shape3, F32)
                for i in range(nc):
                    m = mixed[i * ny : (i + 1) * ny, k * LANES : (k + 1) * LANES].reshape(shape3)
                    psi = jnp.abs(table_v[0, i] - table_v[1, i] * root_t) * m
                    total += amount_v[i, span].reshape(shape3) * psi
                    psi_v[i, span] = psi.reshape(ny, LANES)
                field_v[2, span] = total.reshape(ny, LANES)

        if h == 0:
            press_load.wait()
            flag_load.wait()
        span = pl.ds(h * half * rows, half * rows)
        p, t = press[span], heat[span]
        liquid = flag[span] == 1
        r = inverse(field_v[0, span])
        rt = inverse(t)
        ratio_pt = p * rt
        g = ratio_pt * rt
        beta = field_v[1, span] * r
        gr = g * r
        big_a = gr * r * field_v[2, span]
        big_b = ratio_pt * beta
        z = jnp.where(liquid, big_b + 0.01, 1.0 + big_b)
        floor = big_b + 0.01
        c2 = big_b - 1.0
        c1 = big_a - 3.0 * big_b * big_b - 2.0 * big_b
        c0 = big_b * big_b + big_b * big_b * big_b - big_a * big_b
        twice = 2.0 * c2
        for _ in range(NEWT):
            value = ((z + c2) * z + c1) * z + c0
            incline = (3.0 * z + twice) * z + c1
            z = jnp.maximum(z - value * inverse(jnp.maximum(incline, 0.1)), floor)
        log_ratio = jnp.log(
            (z + (1.0 + ROOT_TWO) * big_b) * inverse(z + (1.0 - ROOT_TWO) * big_b)
        )
        lb = log_ratio * inverse(ROOT_TWO * big_b)
        e0 = jnp.log(z - big_b)
        e1 = (z - 1.0 + 0.5 * big_a * lb) * inverse(beta)
        e2 = gr * lb
        mob = ratio_pt * inverse(z * jnp.where(liquid, visc[1], visc[0]))
        mob_out[span] = mob
        field_v[0, span] = e0
        field_v[1, span] = e1
        field_v[2, span] = e2
        field_v[3, span] = mob * r
        for x in range(h * half * per, (h + 1) * half * per):
            span = pl.ds(x * ny, ny)
            e0, e1, e2, mr = (field_v[k, span].reshape(shape3) for k in range(4))
            for i in range(nc):
                value = table_v[2, i] * e1 - e0 - psi_v[i, span].reshape(shape3) * e2
                lnphi_v[i, span] = value.reshape(ny, LANES).astype(BF16)
                carried = (mr * amount_v[i, span].reshape(shape3)).reshape(ny, LANES)
                carried_out[i, pl.ds(MARGIN + x * ny, ny)] = carried
        span = pl.ds(h * half * rows, half * rows)
        stores.append(go(lnphi_v.at[:, span], lnphi_out.at[:, span], out_sems.at[h]))

    perm_load.wait()
    odd_g = lax.axis_index(axes[0]) % 2 == 1
    odd_s = lax.axis_index(axes[1]) % 2 == 1
    for k in range(edge_x_out.shape[0]):
        at_low = odd_g if k == 0 else jnp.logical_not(odd_g)
        start = pl.multiple_of(jnp.where(at_low, 0, (nx - 1) * ny), ny)
        for i in range(nc):
            edge_x_out[k, i] = carried_out[i, pl.ds(start + MARGIN, ny)]
        edge_x_out[k, nc] = press[pl.ds(start, ny)]
        edge_x_out[k, nc + 1] = perm[pl.ds(start, ny)]
    for i in range(nc + 2):
        source = carried_out.at[i] if i < nc else press if i == nc else perm
        skip = MARGIN if i < nc else 0
        low = source[pl.ds(skip, nx, stride=ny)]
        high = source[pl.ds(skip + ny - 1, nx, stride=ny)]
        edge_ya_out[i] = jnp.where(odd_s, low, high)
        edge_yb_out[i] = jnp.where(odd_s, high, low)

    row_hot, lane_hot = place_hots(loc[...], nx * ny)
    lane_hot = hot(lane_hot)

    def cells_of(field):
        return jnp.sum(jnp.where(row_hot, mat_hot(field, lane_hot), 0.0), axis=0, keepdims=True)

    p_cell = cells_of(press[...])
    pcell_out[...] = p_cell
    weight = strength[...] * cells_of(mob_out[...])
    segments = own_press.shape[1]
    perfs = loc.shape[1]
    place_of = iota((LANES, perfs), 0)
    sums = jnp.where(place_of == seg[...], weight, 0.0)
    sums += jnp.where(place_of == seg[...] + segments, weight * (p_cell - 1.0), 0.0)
    slot_hot = slot_hot_of(member[...], place[...])
    shift = hot(iota((segments, LANES), 0) + 2 * segments == iota((segments, LANES), 1))
    part_out[...] = hot_mat_nt(slot_hot.astype(BF16), sums) + mat_hot(own_press[...], shift)
    for copy in stores:
        copy.wait()


def flux_kernel(
    nx,
    ny,
    axes,
    many_x,
    carried,
    press,
    perm,
    pore,
    flag,
    mob,
    old,
    edge_ya,
    edge_yb,
    well_rows,
    loc,
    member,
    seg,
    strength,
    place,
    pcell,
    consts,
    own_press,
    order,
    exit_press,
    friction,
    *rest,
):
    edge_x, (resid_out, well_out, y_v, res_v, out_sems) = rest[:many_x], rest[many_x:]
    nc = carried.shape[0]
    g, s = lax.axis_index(axes[0]), lax.axis_index(axes[1])
    ng, ns = lax.axis_size(axes[0]), lax.axis_size(axes[1])
    odd_g, odd_s = g % 2 == 1, s % 2 == 1
    has_low_y, has_high_y = s > 0, s < ns - 1
    has_low_x, has_high_x = g > 0, g < ng - 1

    for i in range(nc + 2):
        a, b = edge_ya[i], edge_yb[i]
        low, high = jnp.where(odd_s, a, b), jnp.where(odd_s, b, a)
        if i == nc + 1:
            low, high = jnp.where(has_low_y, low, 0.0), jnp.where(has_high_y, high, 0.0)
        y_v[0, i] = low
        y_v[1, i] = high

    def side_x(i, high):
        if many_x == 1:
            return edge_x[0][i]
        return jnp.where(odd_g != high, edge_x[0][i], edge_x[1][i])

    row_hot, lane_hot = place_hots(loc[...], nx * ny)
    slot_hot = slot_hot_of(member[...], place[...])
    segments = own_press.shape[1]
    gathered = well_rows[...]
    seg_hot = hot(iota((LANES, loc.shape[1]), 0) == seg[...] + 2 * segments)
    p_seg = jnp.sum(mat_hot(gathered, seg_hot) * slot_hot, axis=0, keepdims=True)
    push = strength[...] * (pcell[...] - p_seg)
    flows = jnp.concatenate(
        [
            jnp.where(lane_hot, jnp.maximum(push, 0.0), 0.0),
            jnp.where(lane_hot, jnp.minimum(push, 0.0), 0.0),
        ],
        axis=0,
    )
    spread = hot_mat_nt(hot(row_hot), flows, 2)

    own = jnp.sum(gathered, axis=0, keepdims=True)
    well_p = own_press[...]
    rate = own[:, segments : 2 * segments] - (well_p - 1.0) * own[:, :segments]
    order_hot = hot(iota((segments, segments), 0) == order[...])
    both = mat_hot(jnp.concatenate([rate, well_p], axis=0), order_hot)
    upper = hot(iota((segments, segments), 0) <= iota((segments, segments), 1))
    running = mat_hot(both[0:1], upper)
    press_ord = both[1:2]
    after = hot(iota((segments, segments), 0) == iota((segments, segments), 1) + 1)
    last = iota((1, segments), 1) == segments - 1
    nexts = jnp.where(last, exit_press[...], mat_hot(press_ord, after))
    res_ord = press_ord - nexts - friction[...] * running * jnp.abs(running)
    well_out[...] = sum(mat_nt(piece, order_hot) for piece in pieces_of(res_ord, 3))

    lane = iota((ny, LANES), 1)
    row = iota((ny, LANES), 0)
    first, final = row == 0, row == ny - 1

    def const(k):
        return jnp.concatenate([consts[k]] * (ny // SUBLANES), axis=0)

    stores = []
    for x in range(nx):
        rows = pl.ds(x * ny, ny)
        p_a, k_a = press[rows], perm[rows]
        twice_k = 2.0 * k_a

        def face(p_b, k_b, axis):
            t = const(nc + axis) * (twice_k * k_b) * inverse(k_a + k_b)
            flow = t * (p_a - p_b)
            return jnp.maximum(flow, 0.0), jnp.minimum(flow, 0.0)

        def other_x(field, i, high):
            at = x + 1 if high else x - 1
            return field[pl.ds(at * ny, ny)] if 0 <= at < nx else side_x(i, high)

        def other_y(field, i, high):
            if high:
                return jnp.where(final, y_v[1, i, pl.ds(x, 1)], pltpu.roll(field, ny - 1, 0))
            return jnp.where(first, y_v[0, i, pl.ds(x, 1)], pltpu.roll(field, 1, 0))

        centre = pore[rows] * jnp.where(flag[rows] == 1, const(nc + 4), const(nc + 3))
        centre += spread[x * ny : (x + 1) * ny, :LANES]
        ins = []
        for high in (True, False):
            p_b, k_b = other_x(press, nc, high), other_x(perm, nc + 1, high)
            if x == nx - 1 and high:
                k_b = jnp.where(has_high_x, k_b, 0.0)
            if x == 0 and not high:
                k_b = jnp.where(has_low_x, k_b, 0.0)
            ins.append(face(p_b, k_b, 0))
        for high in (True, False):
            ins.append(face(other_y(p_a, nc, high), other_y(k_a, nc + 1, high), 1))
        for shift, edge in ((LANES - 1, LANES - 1), (1, 0)):
            k_b = jnp.where(lane == edge, 0.0, pltpu.roll(k_a, shift, 1))
            ins.append(face(pltpu.roll(p_a, shift, 1), k_b, 2))
        for out, _ in ins:
            centre += out
        ins = [into for _, into in ins]
        pushed = mob[rows] * spread[x * ny : (x + 1) * ny, LANES:]
        for i in range(nc):
            base = MARGIN + x * ny
            c = carried[i, pl.ds(base, ny)]
            value = centre * c - old[i, rows] + const(i) * pushed
            for k, high in ((0, True), (1, False)):
                at = x + 1 if high else x - 1
                inside = 0 <= at < nx
                c_b = carried[i, pl.ds(MARGIN + at * ny, ny)] if inside else side_x(i, high)
                value += ins[k] * c_b
            up, down = carried[i, pl.ds(base + 1, ny)], carried[i, pl.ds(base - 1, ny)]
            value += ins[2] * jnp.where(final, y_v[1, i, pl.ds(x, 1)], up)
            value += ins[3] * jnp.where(first, y_v[0, i, pl.ds(x, 1)], down)
            value += ins[4] * pltpu.roll(c, LANES - 1, 1)
            value += ins[5] * pltpu.roll(c, 1, 1)
            res_v[i, rows] = value
        copy = pltpu.make_async_copy(res_v.at[:, rows], resid_out.at[:, rows], out_sems.at[x])
        copy.start()
        stores.append(copy)
    for copy in stores:
        copy.wait()


def swaps_of(count, other):
    pairs = [(i, i + 1) for i in range(1 if other else 0, count - 1, 2)]
    return pairs + [(b, a) for a, b in pairs]


def per_device(
    amount,
    press,
    heat,
    flag,
    perm,
    pore,
    old,
    trans,
    visc,
    crit,
    attract,
    covol,
    slope,
    coupling,
    inject,
    locale,
    member,
    seg,
    strength,
    place,
    order,
    seg_press,
    exit_press,
    friction,
):
    axes = ("grp", "sub")
    nc, nx, ny, nz = amount.shape
    ng, ns = lax.axis_size("grp"), lax.axis_size("sub")
    rows = nx * ny
    perfs = locale.shape[0]
    wells, segments = place.shape[1], seg_press.shape[1]
    flat = lambda a: a.reshape(a.shape[:-3] + (rows, nz))
    line = lambda a: a.reshape(1, perfs)
    vm = pl.BlockSpec(memory_space=pltpu.VMEM)
    hbm = pl.BlockSpec(memory_space=pltpu.HBM)
    many_x = 1 if ng == 2 else 2

    amount, old = flat(amount), flat(old)
    press, heat, flag, perm, pore = (flat(a) for a in (press, heat, flag, perm, pore))
    locale, member, seg, strength = (line(a) for a in (locale, member, seg, strength))
    exit_press, friction = exit_press.reshape(1, 1), friction.reshape(1, 1)

    sources = (
        visc, crit, attract, covol, slope, trans, inject,
        coupling, locale, member, seg, strength, place, seg_press,
        heat, press, flag, perm,
    )
    kept = [
        pltpu.SMEM(a.shape, a.dtype) if a.ndim == 1 else pltpu.VMEM(a.shape, a.dtype)
        for a in sources
    ]
    in_hbm = lambda a: pltpu.with_memory_space_constraint(a, pltpu.HBM)

    lnphi, carried, mob, edge_x, edge_ya, edge_yb, part, pcell, consts = pl.pallas_call(
        functools.partial(phase_kernel, nx, ny, axes),
        out_shape=(
            jax.ShapeDtypeStruct((nc, rows, nz), BF16),
            jax.ShapeDtypeStruct((nc, rows + 2 * MARGIN, nz), F32),
            jax.ShapeDtypeStruct((rows, nz), F32),
            jax.ShapeDtypeStruct((many_x, nc + 2, ny, nz), F32),
            jax.ShapeDtypeStruct((nc + 2, nx, nz), F32),
            jax.ShapeDtypeStruct((nc + 2, nx, nz), F32),
            jax.ShapeDtypeStruct((wells, LANES), F32),
            jax.ShapeDtypeStruct((1, perfs), F32),
            jax.ShapeDtypeStruct((nc + 8, SUBLANES, LANES), F32),
        ),
        in_specs=[hbm] * (1 + len(sources)),
        out_specs=(hbm,) + (vm,) * 8,
        scratch_shapes=[
            *kept,
            pltpu.VMEM((nc, rows, nz), F32),
            pltpu.VMEM((3 * nc * ny, nx * nz), BF16),
            pltpu.VMEM((nc, rows, nz), F32),
            pltpu.VMEM((nc, rows, nz), BF16),
            pltpu.VMEM((4, rows, nz), F32),
            pltpu.VMEM((3, nc, SUBLANES, LANES), F32),
            pltpu.SemaphoreType.DMA((len(sources),)),
            pltpu.SemaphoreType.DMA((nx // 2,)),
            pltpu.SemaphoreType.DMA((2,)),
        ],
        compiler_params=pltpu.CompilerParams(vmem_limit_bytes=VMEM_LIMIT),
        name="phase",
    )(in_hbm(amount), *(in_hbm(a) for a in sources))

    backward = [list(range(ns))[::-1]]
    well_rows = lax.all_to_all(
        part, "sub", split_axis=0, concat_axis=0, axis_index_groups=backward, tiled=True
    )
    got_x = [lax.ppermute(edge_x[k], "grp", swaps_of(ng, k == 1)) for k in range(many_x)]
    got_yb = lax.ppermute(edge_yb, "sub", swaps_of(ns, True))
    got_ya = lax.ppermute(edge_ya, "sub", swaps_of(ns, False))

    resid, well = pl.pallas_call(
        functools.partial(flux_kernel, nx, ny, axes, many_x),
        out_shape=(
            jax.ShapeDtypeStruct((nc, rows, nz), F32),
            jax.ShapeDtypeStruct((1, segments), F32),
        ),
        in_specs=[vm] * (21 + many_x),
        out_specs=(hbm, vm),
        scratch_shapes=[
            pltpu.VMEM((2, nc + 2, nx, nz), F32),
            pltpu.VMEM((nc, rows, nz), F32),
            pltpu.SemaphoreType.DMA((nx,)),
        ],
        compiler_params=pltpu.CompilerParams(vmem_limit_bytes=VMEM_LIMIT),
        name="flux",
    )(
        carried, press, perm, pore, flag, mob, old, got_ya, got_yb, well_rows,
        locale, member, seg, strength, place, pcell,
        consts, seg_press, order, exit_press, friction, *got_x,
    )
    block = (nc, nx, ny, nz)
    return resid.reshape(block), lnphi.reshape(block), well


def solution(mesh):
    cells, parts = P("grp", "sub", None), P(None, "grp", "sub", None)
    listed = P(("grp", "sub"))
    row = P(("grp", "sub"), None)
    in_specs = (
        (parts,) + (cells,) * 5 + (parts,) + (P(),) * 8
        + (listed, row, listed, listed, P("grp", None), row, row, listed, listed)
    )
    return jax.shard_map(
        per_device, mesh=mesh, in_specs=in_specs, out_specs=(parts, parts, row), check_vma=False
    )
```

```python
import functools
import math

import jax
import jax.numpy as jnp
from jax import lax
from jax.experimental import pallas as pl
from jax.experimental.pallas import tpu as pltpu
from jax.sharding import PartitionSpec as P

NEWT = 8
ROOT_TWO = math.sqrt(2.0)
LANES = 128
SUBLANES = 8
F32 = jnp.float32
BF16 = jnp.bfloat16
VMEM_LIMIT = 48 * 1024 * 1024
MARGIN = 8
WHOLE = (
    "coupling", "crit", "attract", "slope", "covol", "heat", "press", "loc", "member", "place",
    "flag", "visc", "trans", "inject", "seg", "strength", "own_press", "perm",
)


def iota(shape, dim):
    return lax.broadcasted_iota(jnp.int32, shape, dim)


def pieces_of(x, count):
    out = []
    for _ in range(count):
        piece = x.astype(BF16)
        out.append(piece)
        x = x - piece.astype(F32)
    return out


def mat(a, b):
    return lax.dot_general(a, b, (((1,), (0,)), ((), ())), preferred_element_type=F32)


def mat_nt(a, b):
    return lax.dot_general(a, b, (((1,), (1,)), ((), ())), preferred_element_type=F32)


def mat_hot(x, hot, count=3):
    return sum(mat(piece, hot) for piece in pieces_of(x, count))


def hot_mat_nt(hot, x, count=3):
    return sum(mat_nt(hot, piece) for piece in pieces_of(x, count))


def inverse(x):
    r = pl.reciprocal(x, approx=True)
    return r * (2.0 - x * r)


def hot(cond):
    return jnp.where(cond, 1.0, 0.0).astype(BF16)


def place_hots(loc, rows):
    n = loc.shape[1]
    row_hot = iota((rows, n), 0) == loc // LANES
    lane_hot = iota((LANES, n), 0) == loc % LANES
    return row_hot, lane_hot


def reversed_bits(x, count):
    bits = count.bit_length() - 1
    return sum(((x >> b) & 1) << (bits - 1 - b) for b in range(bits))


def slot_hot_of(member, place, slots):
    wells = place.shape[1]
    slot_of = hot(slots == place)
    member_hot = hot(iota((wells, member.shape[1]), 0) == member)
    return mat(slot_of, member_hot)


def phase_kernel(
    nx,
    ny,
    axes,
    amount,
    *rest,
):
    sources, rest = rest[: len(WHOLE)], rest[len(WHOLE) :]
    (
        lnphi_out,
        carried_out,
        mob_out,
        edge_x_out,
        edge_ya_out,
        edge_yb_out,
        sums_out,
        known_out,
        pcell_out,
        consts_out,
    ) = rest[:10]
    targets, rest = rest[10 : 10 + len(WHOLE)], rest[10 + len(WHOLE) :]
    amount_v, split_v, psi_v, lnphi_v, field_v, table_v, small_sems, in_sems, out_sems = rest
    nc = amount.shape[0]
    per = 2
    chunks = nx // per
    half = chunks // 2
    rows = per * ny

    def go(source, target, sem):
        copy = pltpu.make_async_copy(source, target, sem)
        copy.start()
        return copy

    loads, copies = [], {}
    for k, name in enumerate(WHOLE):
        if name in ("press", "flag"):
            span = pl.ds(len(loads) * half * rows, half * rows)
            loads.append(go(amount.at[:, span], amount_v.at[:, span], in_sems.at[len(loads)]))
        copies[name] = go(sources[k], targets[k], small_sems.at[k])

    def arrived(*names):
        for name in names:
            copies[name].wait()
        return [targets[WHOLE.index(name)] for name in names]

    size = nc * ny
    spread = hot(iota((size, nc), 0) // ny == iota((size, nc), 1))
    same_row = iota((size, size), 0) % ny == iota((size, size), 1) % ny
    mixers = []
    (coupling,) = arrived("coupling")
    for piece in pieces_of(1.0 - coupling[...], 2):
        wide = mat(spread, piece).astype(BF16)
        mixers.append(jnp.where(same_row, mat_nt(wide, spread), 0.0).astype(BF16))
    mixer = jnp.concatenate([mixers[0], mixers[0], mixers[1]], axis=1)

    crit, attract, slope, covol = arrived("crit", "attract", "slope", "covol")
    for i in range(nc):
        root = jnp.sqrt(jnp.full((SUBLANES, LANES), attract[i], F32))
        kappa = jnp.full((SUBLANES, LANES), slope[i], F32)
        tc = jnp.full((SUBLANES, LANES), crit[i], F32)
        table_v[0, i] = root * (1.0 + kappa)
        table_v[1, i] = root * kappa / jnp.sqrt(tc)
        table_v[2, i] = jnp.full((SUBLANES, LANES), covol[i], F32)

    press, loc, member, place = arrived("press", "loc", "member", "place")
    row_hot, lane_hot = place_hots(loc[...], nx * ny)
    lane_hot = hot(lane_hot)

    def cells_of(field, count):
        found = mat_hot(field, lane_hot, count)
        return jnp.sum(jnp.where(row_hot, found, 0.0), axis=0, keepdims=True)

    p_cell = cells_of(press[...], 3)
    pcell_out[...] = p_cell
    wells = place.shape[1]
    own_slot = lax.axis_index(axes[1])
    row_slots = own_slot ^ reversed_bits(iota((wells, wells), 0), wells)
    slot_hot = slot_hot_of(member[...], place[...], row_slots).astype(BF16)
    (heat,) = arrived("heat")

    shape3 = (ny // SUBLANES, SUBLANES, LANES)
    stores = []
    for h in range(2):
        loads[h].wait()
        for c in range(h * half, (h + 1) * half):
            for x in range(c * per, (c + 1) * per):
                span = pl.ds(x * ny, ny)
                lanes = pl.ds(x * LANES, LANES)
                root_t = jnp.sqrt(heat[span].reshape(shape3))
                total = jnp.zeros(shape3, F32)
                volume = jnp.zeros(shape3, F32)
                for i in range(nc):
                    o = amount_v[i, span].reshape(shape3)
                    v = jnp.abs(table_v[0, i] - table_v[1, i] * root_t) * o
                    total += o
                    volume += table_v[2, i] * o
                    high, low = pieces_of(v.reshape(ny, LANES), 2)
                    split_v[pl.ds(i * ny, ny), lanes] = high
                    split_v[pl.ds(size + i * ny, ny), lanes] = low
                    split_v[pl.ds(2 * size + i * ny, ny), lanes] = high
                field_v[0, span] = total.reshape(ny, LANES)
                field_v[1, span] = volume.reshape(ny, LANES)
            lanes = pl.ds(c * per * LANES, per * LANES)
            mixed = mat(mixer, split_v[:, lanes])
            for k in range(per):
                x = c * per + k
                span = pl.ds(x * ny, ny)
                root_t = jnp.sqrt(heat[span].reshape(shape3))
                total = jnp.zeros(shape3, F32)
                for i in range(nc):
                    m = mixed[i * ny : (i + 1) * ny, k * LANES : (k + 1) * LANES].reshape(shape3)
                    psi = jnp.abs(table_v[0, i] - table_v[1, i] * root_t) * m
                    total += amount_v[i, span].reshape(shape3) * psi
                    psi_v[i, span] = psi.reshape(ny, LANES)
                field_v[2, span] = total.reshape(ny, LANES)

        if h == 0:
            flag, visc, trans, inject = arrived("flag", "visc", "trans", "inject")
        span = pl.ds(h * half * rows, half * rows)
        p, t = press[span], heat[span]
        liquid = flag[span] == 1
        r = inverse(field_v[0, span])
        rt = inverse(t)
        ratio_pt = p * rt
        g = ratio_pt * rt
        beta = field_v[1, span] * r
        gr = g * r
        big_a = gr * r * field_v[2, span]
        big_b = ratio_pt * beta
        z = jnp.where(liquid, big_b + 0.01, 1.0 + big_b)
        floor = big_b + 0.01
        c2 = big_b - 1.0
        c1 = big_a - 3.0 * big_b * big_b - 2.0 * big_b
        c0 = big_b * big_b + big_b * big_b * big_b - big_a * big_b
        twice = 2.0 * c2
        for _ in range(NEWT):
            value = ((z + c2) * z + c1) * z + c0
            incline = (3.0 * z + twice) * z + c1
            z = jnp.maximum(z - value * inverse(jnp.maximum(incline, 0.1)), floor)
        log_ratio = jnp.log(
            (z + (1.0 + ROOT_TWO) * big_b) * inverse(z + (1.0 - ROOT_TWO) * big_b)
        )
        lb = log_ratio * inverse(ROOT_TWO * big_b)
        e0 = jnp.log(z - big_b)
        e1 = (z - 1.0 + 0.5 * big_a * lb) * inverse(beta)
        e2 = gr * lb
        mob = ratio_pt * inverse(z * jnp.where(liquid, visc[1], visc[0]))
        mob_out[span] = mob
        field_v[0, span] = e0
        field_v[1, span] = e1
        field_v[2, span] = e2
        field_v[3, span] = mob * r
        for x in range(h * half * per, (h + 1) * half * per):
            span = pl.ds(x * ny, ny)
            e0, e1, e2, mr = (field_v[k, span].reshape(shape3) for k in range(4))
            for i in range(nc):
                value = table_v[2, i] * e1 - e0 - psi_v[i, span].reshape(shape3) * e2
                lnphi_v[i, span] = value.reshape(ny, LANES).astype(BF16)
                carried = (mr * amount_v[i, span].reshape(shape3)).reshape(ny, LANES)
                carried_out[i, pl.ds(MARGIN + x * ny, ny)] = carried
        span = pl.ds(h * half * rows, half * rows)
        stores.append(go(lnphi_v.at[:, span], lnphi_out.at[:, span], out_sems.at[h]))

    total = sum(inject[i] for i in range(nc))
    share = 1.0 / jnp.full((SUBLANES, LANES), total, F32)
    numbers = [trans[0], trans[1], trans[2], visc[0], visc[1]]
    for i in range(nc):
        consts_out[i] = inject[i] * share
    for i, number in enumerate(numbers):
        consts_out[nc + i] = jnp.full((SUBLANES, LANES), number, F32)

    seg, strength, own_press, perm = arrived("seg", "strength", "own_press", "perm")
    weight = strength[...] * cells_of(mob_out[...], 2)
    segments = own_press.shape[1]
    place_of = iota((LANES, loc.shape[1]), 0)
    sums = jnp.where(place_of == seg[...], weight, 0.0)
    sums += jnp.where(place_of == seg[...] + segments, weight * (p_cell - 1.0), 0.0)
    sums = hot_mat_nt(slot_hot, sums, 2)
    sums_out[...] = sums[: wells // 2]
    for k in range(wells // 2 // nx):
        start = wells // 2 + k * nx
        edge_ya_out[nc + 2 + k] = sums[start : start + nx]
    known_out[...] = jnp.zeros(known_out.shape, F32)
    known_out[:, pl.ds(0, segments)] = own_press[...]
    edge_ya_out[nc + 2 + wells // 2 // nx] = jnp.broadcast_to(known_out[...], (nx, LANES))

    odd_g = lax.axis_index(axes[0]) % 2 == 1
    odd_s = own_slot % 2 == 1
    for k in range(edge_x_out.shape[0]):
        at_low = odd_g if k == 0 else jnp.logical_not(odd_g)
        start = pl.multiple_of(jnp.where(at_low, 0, (nx - 1) * ny), ny)
        for i in range(nc):
            edge_x_out[k, i] = carried_out[i, pl.ds(start + MARGIN, ny)]
        edge_x_out[k, nc] = press[pl.ds(start, ny)]
        edge_x_out[k, nc + 1] = perm[pl.ds(start, ny)]
    for i in range(nc + 2):
        source = carried_out.at[i] if i < nc else press if i == nc else perm
        skip = MARGIN if i < nc else 0
        low = source[pl.ds(skip, nx, stride=ny)]
        high = source[pl.ds(skip + ny - 1, nx, stride=ny)]
        edge_ya_out[i] = jnp.where(odd_s, low, high)
        edge_yb_out[i] = jnp.where(odd_s, high, low)
    for copy in stores:
        copy.wait()


def flux_kernel(
    nx,
    ny,
    axes,
    many_x,
    carried,
    press,
    perm,
    pore,
    flag,
    mob,
    old,
    edge_ya,
    edge_yb,
    sums,
    known,
    loc,
    member,
    seg,
    strength,
    place,
    pcell,
    consts,
    own_press,
    order,
    exit_press,
    friction,
    *rest,
):
    edge_x, (resid_out, well_out, y_v, res_v, out_sems) = rest[:many_x], rest[many_x:]
    nc = carried.shape[0]
    g, s = lax.axis_index(axes[0]), lax.axis_index(axes[1])
    ng, ns = lax.axis_size(axes[0]), lax.axis_size(axes[1])
    odd_g, odd_s = g % 2 == 1, s % 2 == 1
    has_low_y, has_high_y = s > 0, s < ns - 1
    has_low_x, has_high_x = g > 0, g < ng - 1

    for i in range(nc + 2):
        a, b = edge_ya[i], edge_yb[i]
        low, high = jnp.where(odd_s, a, b), jnp.where(odd_s, b, a)
        if i == nc + 1:
            low, high = jnp.where(has_low_y, low, 0.0), jnp.where(has_high_y, high, 0.0)
        y_v[0, i] = low
        y_v[1, i] = high

    def side_x(i, high):
        if many_x == 1:
            return edge_x[0][i]
        return jnp.where(odd_g != high, edge_x[0][i], edge_x[1][i])

    row_hot, lane_hot = place_hots(loc[...], nx * ny)
    wells = place.shape[1]
    slot_hot = slot_hot_of(member[...], place[...], s ^ iota((wells, wells), 0))
    segments = own_press.shape[1]
    seg_hot = hot(iota((LANES, loc.shape[1]), 0) == seg[...])
    p_seg = jnp.sum(mat_hot(known[...], seg_hot) * slot_hot, axis=0, keepdims=True)
    push = strength[...] * (pcell[...] - p_seg)
    flows = jnp.concatenate(
        [
            jnp.where(lane_hot, jnp.maximum(push, 0.0), 0.0),
            jnp.where(lane_hot, jnp.minimum(push, 0.0), 0.0),
        ],
        axis=0,
    )
    spread = hot_mat_nt(hot(row_hot), flows, 2)

    own = sums[...]
    well_p = own_press[...]
    rate = own[:, segments : 2 * segments] - (well_p - 1.0) * own[:, :segments]
    order_hot = hot(iota((segments, segments), 0) == order[...])
    both = mat_hot(jnp.concatenate([rate, well_p], axis=0), order_hot)
    upper = hot(iota((segments, segments), 0) <= iota((segments, segments), 1))
    running = mat_hot(both[0:1], upper)
    press_ord = both[1:2]
    after = hot(iota((segments, segments), 0) == iota((segments, segments), 1) + 1)
    last = iota((1, segments), 1) == segments - 1
    nexts = jnp.where(last, exit_press[...], mat_hot(press_ord, after))
    res_ord = press_ord - nexts - friction[...] * running * jnp.abs(running)
    well_out[...] = sum(mat_nt(piece, order_hot) for piece in pieces_of(res_ord, 3))

    lane = iota((ny, LANES), 1)
    row = iota((ny, LANES), 0)
    first, final = row == 0, row == ny - 1

    def const(k):
        return jnp.concatenate([consts[k]] * (ny // SUBLANES), axis=0)

    stores = []
    for x in range(nx):
        rows = pl.ds(x * ny, ny)
        p_a, k_a = press[rows], perm[rows]
        twice_k = 2.0 * k_a

        def face(p_b, k_b, axis):
            t = const(nc + axis) * (twice_k * k_b) * inverse(k_a + k_b)
            flow = t * (p_a - p_b)
            return jnp.maximum(flow, 0.0), jnp.minimum(flow, 0.0)

        def other_x(field, i, high):
            at = x + 1 if high else x - 1
            return field[pl.ds(at * ny, ny)] if 0 <= at < nx else side_x(i, high)

        def other_y(field, i, high):
            if high:
                return jnp.where(final, y_v[1, i, pl.ds(x, 1)], pltpu.roll(field, ny - 1, 0))
            return jnp.where(first, y_v[0, i, pl.ds(x, 1)], pltpu.roll(field, 1, 0))

        centre = pore[rows] * jnp.where(flag[rows] == 1, const(nc + 4), const(nc + 3))
        centre += spread[x * ny : (x + 1) * ny, :LANES]
        ins = []
        for high in (True, False):
            p_b, k_b = other_x(press, nc, high), other_x(perm, nc + 1, high)
            if x == nx - 1 and high:
                k_b = jnp.where(has_high_x, k_b, 0.0)
            if x == 0 and not high:
                k_b = jnp.where(has_low_x, k_b, 0.0)
            ins.append(face(p_b, k_b, 0))
        for high in (True, False):
            ins.append(face(other_y(p_a, nc, high), other_y(k_a, nc + 1, high), 1))
        for shift, edge in ((LANES - 1, LANES - 1), (1, 0)):
            k_b = jnp.where(lane == edge, 0.0, pltpu.roll(k_a, shift, 1))
            ins.append(face(pltpu.roll(p_a, shift, 1), k_b, 2))
        for out, _ in ins:
            centre += out
        ins = [into for _, into in ins]
        pushed = mob[rows] * spread[x * ny : (x + 1) * ny, LANES:]
        for i in range(nc):
            base = MARGIN + x * ny
            c = carried[i, pl.ds(base, ny)]
            value = centre * c - old[i, rows] + const(i) * pushed
            for k, high in ((0, True), (1, False)):
                at = x + 1 if high else x - 1
                inside = 0 <= at < nx
                c_b = carried[i, pl.ds(MARGIN + at * ny, ny)] if inside else side_x(i, high)
                value += ins[k] * c_b
            up, down = carried[i, pl.ds(base + 1, ny)], carried[i, pl.ds(base - 1, ny)]
            value += ins[2] * jnp.where(final, y_v[1, i, pl.ds(x, 1)], up)
            value += ins[3] * jnp.where(first, y_v[0, i, pl.ds(x, 1)], down)
            value += ins[4] * pltpu.roll(c, LANES - 1, 1)
            value += ins[5] * pltpu.roll(c, 1, 1)
            res_v[i, rows] = value
        copy = pltpu.make_async_copy(res_v.at[:, rows], resid_out.at[:, rows], out_sems.at[x])
        copy.start()
        stores.append(copy)
    for copy in stores:
        copy.wait()


def swaps_of(count, other):
    if other:
        pairs = [(i, i + 1) for i in range(1, count - 1, 2)] + [(0, 0), (count - 1, count - 1)]
    else:
        pairs = [(i, i + 1) for i in range(0, count, 2)]
    return sorted(set(pairs + [(b, a) for a, b in pairs]))


def per_device(
    amount,
    press,
    heat,
    flag,
    perm,
    pore,
    old,
    trans,
    visc,
    crit,
    attract,
    covol,
    slope,
    coupling,
    inject,
    locale,
    member,
    seg,
    strength,
    place,
    order,
    seg_press,
    exit_press,
    friction,
):
    axes = ("grp", "sub")
    nc, nx, ny, nz = amount.shape
    ng, ns = lax.axis_size("grp"), lax.axis_size("sub")
    rows = nx * ny
    perfs = locale.shape[0]
    wells, segments = place.shape[1], seg_press.shape[1]
    flat = lambda a: a.reshape(a.shape[:-3] + (rows, nz))
    line = lambda a: a.reshape(1, perfs)
    vm = pl.BlockSpec(memory_space=pltpu.VMEM)
    hbm = pl.BlockSpec(memory_space=pltpu.HBM)
    many_x = 1 if ng == 2 else 2

    amount, old = flat(amount), flat(old)
    press, heat, flag, perm, pore = (flat(a) for a in (press, heat, flag, perm, pore))
    locale, member, seg, strength = (line(a) for a in (locale, member, seg, strength))
    exit_press, friction = exit_press.reshape(1, 1), friction.reshape(1, 1)

    sources = (
        coupling, crit, attract, slope, covol, heat, press, locale, member, place,
        flag, visc, trans, inject, seg, strength, seg_press, perm,
    )
    kept = [
        pltpu.SMEM(a.shape, a.dtype) if a.ndim == 1 else pltpu.VMEM(a.shape, a.dtype)
        for a in sources
    ]
    in_hbm = lambda a: pltpu.with_memory_space_constraint(a, pltpu.HBM)

    lnphi, carried, mob, edge_x, edge_ya, edge_yb, sums, known, pcell, consts = pl.pallas_call(
        functools.partial(phase_kernel, nx, ny, axes),
        out_shape=(
            jax.ShapeDtypeStruct((nc, rows, nz), BF16),
            jax.ShapeDtypeStruct((nc, rows + 2 * MARGIN, nz), F32),
            jax.ShapeDtypeStruct((rows, nz), F32),
            jax.ShapeDtypeStruct((many_x, nc + 2, ny, nz), F32),
            jax.ShapeDtypeStruct((nc + 2 + wells // 2 // nx + 1, nx, nz), F32),
            jax.ShapeDtypeStruct((nc + 2, nx, nz), F32),
            jax.ShapeDtypeStruct((wells // 2, LANES), F32),
            jax.ShapeDtypeStruct((1, LANES), F32),
            jax.ShapeDtypeStruct((1, perfs), F32),
            jax.ShapeDtypeStruct((nc + 8, SUBLANES, LANES), F32),
        ),
        in_specs=[hbm] * (1 + len(sources)),
        out_specs=(hbm,) + (vm,) * 9,
        scratch_shapes=[
            *kept,
            pltpu.VMEM((nc, rows, nz), F32),
            pltpu.VMEM((3 * nc * ny, nx * nz), BF16),
            pltpu.VMEM((nc, rows, nz), F32),
            pltpu.VMEM((nc, rows, nz), BF16),
            pltpu.VMEM((4, rows, nz), F32),
            pltpu.VMEM((3, nc, SUBLANES, LANES), F32),
            pltpu.SemaphoreType.DMA((len(sources),)),
            pltpu.SemaphoreType.DMA((2,)),
            pltpu.SemaphoreType.DMA((2,)),
        ],
        compiler_params=pltpu.CompilerParams(vmem_limit_bytes=VMEM_LIMIT),
        name="phase",
    )(in_hbm(amount), *(in_hbm(a) for a in sources))

    got_ya = lax.ppermute(edge_ya, "sub", swaps_of(ns, False))
    got_x = [lax.ppermute(edge_x[k], "grp", swaps_of(ng, k == 1)) for k in range(many_x)]
    got_yb = lax.ppermute(edge_yb, "sub", swaps_of(ns, True))
    left = wells // 2
    got = got_ya[nc + 2 :].reshape(left + nx, nz)
    step = 1
    while True:
        sums = sums[:left] + got[:left]
        known = jnp.concatenate([known, got[left : left + step]], axis=0)
        if left == 1:
            break
        left, step = left // 2, 2 * step
        swap = [(i, i ^ step) for i in range(ns)]
        got = lax.ppermute(jnp.concatenate([sums[left:], known], axis=0), "sub", swap)

    resid, well = pl.pallas_call(
        functools.partial(flux_kernel, nx, ny, axes, many_x),
        out_shape=(
            jax.ShapeDtypeStruct((nc, rows, nz), F32),
            jax.ShapeDtypeStruct((1, segments), F32),
        ),
        in_specs=[vm] * (22 + many_x),
        out_specs=(hbm, vm),
        scratch_shapes=[
            pltpu.VMEM((2, nc + 2, nx, nz), F32),
            pltpu.VMEM((nc, rows, nz), F32),
            pltpu.SemaphoreType.DMA((nx,)),
        ],
        compiler_params=pltpu.CompilerParams(vmem_limit_bytes=VMEM_LIMIT),
        name="flux",
    )(
        carried, press, perm, pore, flag, mob, old, got_ya, got_yb, sums, known,
        locale, member, seg, strength, place, pcell,
        consts, seg_press, order, exit_press, friction, *got_x,
    )
    block = (nc, nx, ny, nz)
    return resid.reshape(block), lnphi.reshape(block), well


def solution(mesh):
    cells, parts = P("grp", "sub", None), P(None, "grp", "sub", None)
    listed = P(("grp", "sub"))
    row = P(("grp", "sub"), None)
    in_specs = (
        (parts,) + (cells,) * 5 + (parts,) + (P(),) * 8
        + (listed, row, listed, listed, P("grp", None), row, row, listed, listed)
    )
    return jax.shard_map(
        per_device, mesh=mesh, in_specs=in_specs, out_specs=(parts, parts, row), check_vma=False
    )
```

```python
import functools
import math

import jax
import jax.numpy as jnp
from jax import lax
from jax.experimental import pallas as pl
from jax.experimental.pallas import tpu as pltpu
from jax.sharding import PartitionSpec as P

NEWT = 8
ROOT_TWO = math.sqrt(2.0)
LANES = 128
SUBLANES = 8
F32 = jnp.float32
BF16 = jnp.bfloat16
VMEM_LIMIT = 48 * 1024 * 1024
MARGIN = 8
WHOLE = (
    "coupling", "crit", "attract", "slope", "covol", "heat", "press", "loc", "member", "place",
    "flag", "visc", "trans", "inject", "seg", "strength", "own_press", "perm",
)


def iota(shape, dim):
    return lax.broadcasted_iota(jnp.int32, shape, dim)


def pieces_of(x, count):
    out = []
    for _ in range(count):
        piece = x.astype(BF16)
        out.append(piece)
        x = x - piece.astype(F32)
    return out


def mat(a, b):
    return lax.dot_general(a, b, (((1,), (0,)), ((), ())), preferred_element_type=F32)


def mat_nt(a, b):
    return lax.dot_general(a, b, (((1,), (1,)), ((), ())), preferred_element_type=F32)


def mat_hot(x, hot, count=3):
    return sum(mat(piece, hot) for piece in pieces_of(x, count))


def hot_mat_nt(hot, x, count=3):
    return sum(mat_nt(hot, piece) for piece in pieces_of(x, count))


def inverse(x):
    r = pl.reciprocal(x, approx=True)
    return r * (2.0 - x * r)


def hot(cond):
    return jnp.where(cond, 1.0, 0.0).astype(BF16)


def place_hots(loc, rows):
    n = loc.shape[1]
    row_hot = iota((rows, n), 0) == loc // LANES
    lane_hot = iota((LANES, n), 0) == loc % LANES
    return row_hot, lane_hot


def slot_hot_of(member, place):
    wells = place.shape[1]
    slot_of = hot(iota((wells, wells), 0) == wells - 1 - place)
    member_hot = hot(iota((wells, member.shape[1]), 0) == member)
    return mat(slot_of, member_hot)


def phase_kernel(
    nx,
    ny,
    axes,
    amount,
    *rest,
):
    sources, rest = rest[: len(WHOLE)], rest[len(WHOLE) :]
    (
        psi_v,
        terms_out,
        carried_out,
        mob_out,
        edge_x_out,
        edge_ya_out,
        edge_yb_out,
        part_out,
        pcell_out,
        consts_out,
    ) = rest[:10]
    targets, rest = rest[10 : 10 + len(WHOLE)], rest[10 + len(WHOLE) :]
    amount_v, split_v, field_v, table_v, small_sems, in_sems = rest
    nc = amount.shape[0]
    per = 2
    chunks = nx // per
    half = chunks // 2
    rows = per * ny

    def go(source, target, sem):
        copy = pltpu.make_async_copy(source, target, sem)
        copy.start()
        return copy

    loads, copies = [], {}
    for k, name in enumerate(WHOLE):
        if name in ("press", "flag"):
            span = pl.ds(len(loads) * half * rows, half * rows)
            loads.append(go(amount.at[:, span], amount_v.at[:, span], in_sems.at[len(loads)]))
        copies[name] = go(sources[k], targets[k], small_sems.at[k])

    def arrived(*names):
        for name in names:
            copies[name].wait()
        return [targets[WHOLE.index(name)] for name in names]

    size = nc * ny
    spread = hot(iota((size, nc), 0) // ny == iota((size, nc), 1))
    same_row = iota((size, size), 0) % ny == iota((size, size), 1) % ny
    mixers = []
    (coupling,) = arrived("coupling")
    for piece in pieces_of(1.0 - coupling[...], 2):
        wide = mat(spread, piece).astype(BF16)
        mixers.append(jnp.where(same_row, mat_nt(wide, spread), 0.0).astype(BF16))
    mixer = jnp.concatenate([mixers[0], mixers[0], mixers[1]], axis=1)

    crit, attract, slope, covol = arrived("crit", "attract", "slope", "covol")
    for i in range(nc):
        root = jnp.sqrt(jnp.full((SUBLANES, LANES), attract[i], F32))
        kappa = jnp.full((SUBLANES, LANES), slope[i], F32)
        tc = jnp.full((SUBLANES, LANES), crit[i], F32)
        table_v[0, i] = root * (1.0 + kappa)
        table_v[1, i] = root * kappa / jnp.sqrt(tc)
        table_v[2, i] = jnp.full((SUBLANES, LANES), covol[i], F32)

    press, loc, member, place = arrived("press", "loc", "member", "place")
    row_hot, lane_hot = place_hots(loc[...], nx * ny)
    lane_hot = hot(lane_hot)

    def cells_of(field, count):
        found = mat_hot(field, lane_hot, count)
        return jnp.sum(jnp.where(row_hot, found, 0.0), axis=0, keepdims=True)

    p_cell = cells_of(press[...], 3)
    pcell_out[...] = p_cell
    slot_hot = slot_hot_of(member[...], place[...]).astype(BF16)
    (heat,) = arrived("heat")

    shape3 = (ny // SUBLANES, SUBLANES, LANES)
    for h in range(2):
        loads[h].wait()
        for c in range(h * half, (h + 1) * half):
            for x in range(c * per, (c + 1) * per):
                span = pl.ds(x * ny, ny)
                lanes = pl.ds(x * LANES, LANES)
                root_t = jnp.sqrt(heat[span].reshape(shape3))
                total = jnp.zeros(shape3, F32)
                volume = jnp.zeros(shape3, F32)
                for i in range(nc):
                    o = amount_v[i, span].reshape(shape3)
                    v = jnp.abs(table_v[0, i] - table_v[1, i] * root_t) * o
                    total += o
                    volume += table_v[2, i] * o
                    high, low = pieces_of(v.reshape(ny, LANES), 2)
                    split_v[pl.ds(i * ny, ny), lanes] = high
                    split_v[pl.ds(size + i * ny, ny), lanes] = low
                    split_v[pl.ds(2 * size + i * ny, ny), lanes] = high
                field_v[0, span] = total.reshape(ny, LANES)
                field_v[1, span] = volume.reshape(ny, LANES)
            lanes = pl.ds(c * per * LANES, per * LANES)
            mixed = mat(mixer, split_v[:, lanes])
            for k in range(per):
                x = c * per + k
                span = pl.ds(x * ny, ny)
                root_t = jnp.sqrt(heat[span].reshape(shape3))
                total = jnp.zeros(shape3, F32)
                for i in range(nc):
                    m = mixed[i * ny : (i + 1) * ny, k * LANES : (k + 1) * LANES].reshape(shape3)
                    psi = jnp.abs(table_v[0, i] - table_v[1, i] * root_t) * m
                    total += amount_v[i, span].reshape(shape3) * psi
                    psi_v[i, span] = psi.reshape(ny, LANES)
                field_v[2, span] = total.reshape(ny, LANES)

        if h == 0:
            flag, visc, trans, inject = arrived("flag", "visc", "trans", "inject")
        span = pl.ds(h * half * rows, half * rows)
        p, t = press[span], heat[span]
        liquid = flag[span] == 1
        r = inverse(field_v[0, span])
        rt = inverse(t)
        ratio_pt = p * rt
        g = ratio_pt * rt
        beta = field_v[1, span] * r
        gr = g * r
        big_a = gr * r * field_v[2, span]
        big_b = ratio_pt * beta
        z = jnp.where(liquid, big_b + 0.01, 1.0 + big_b)
        floor = big_b + 0.01
        c2 = big_b - 1.0
        c1 = big_a - 3.0 * big_b * big_b - 2.0 * big_b
        c0 = big_b * big_b + big_b * big_b * big_b - big_a * big_b
        twice = 2.0 * c2
        for _ in range(NEWT):
            value = ((z + c2) * z + c1) * z + c0
            incline = (3.0 * z + twice) * z + c1
            z = jnp.maximum(z - value * inverse(jnp.maximum(incline, 0.1)), floor)
        log_ratio = jnp.log(
            (z + (1.0 + ROOT_TWO) * big_b) * inverse(z + (1.0 - ROOT_TWO) * big_b)
        )
        lb = log_ratio * inverse(ROOT_TWO * big_b)
        e0 = jnp.log(z - big_b)
        e1 = (z - 1.0 + 0.5 * big_a * lb) * inverse(beta)
        e2 = gr * lb
        mob = ratio_pt * inverse(z * jnp.where(liquid, visc[1], visc[0]))
        mob_out[span] = mob
        terms_out[0, span] = e0
        terms_out[1, span] = e1
        terms_out[2, span] = e2
        field_v[3, span] = mob * r
        for x in range(h * half * per, (h + 1) * half * per):
            span = pl.ds(x * ny, ny)
            mr = field_v[3, span]
            for i in range(nc):
                carried_out[i, pl.ds(MARGIN + x * ny, ny)] = mr * amount_v[i, span]

    total = sum(inject[i] for i in range(nc))
    share = 1.0 / jnp.full((SUBLANES, LANES), total, F32)
    numbers = [trans[0], trans[1], trans[2], visc[0], visc[1]]
    for i in range(nc):
        consts_out[i] = inject[i] * share
        consts_out[nc + 8 + i] = table_v[2, i]
    for i, number in enumerate(numbers):
        consts_out[nc + i] = jnp.full((SUBLANES, LANES), number, F32)

    seg, strength, own_press, perm = arrived("seg", "strength", "own_press", "perm")
    weight = strength[...] * cells_of(mob_out[...], 2)
    segments = own_press.shape[1]
    place_of = iota((LANES, loc.shape[1]), 0)
    sums = jnp.where(place_of == seg[...], weight, 0.0)
    sums += jnp.where(place_of == seg[...] + segments, weight * (p_cell - 1.0), 0.0)
    shift = hot(iota((segments, LANES), 0) + 2 * segments == iota((segments, LANES), 1))
    part_out[...] = hot_mat_nt(slot_hot, sums, 2) + mat_hot(own_press[...], shift)

    odd_g = lax.axis_index(axes[0]) % 2 == 1
    odd_s = lax.axis_index(axes[1]) % 2 == 1
    for k in range(edge_x_out.shape[0]):
        at_low = odd_g if k == 0 else jnp.logical_not(odd_g)
        start = pl.multiple_of(jnp.where(at_low, 0, (nx - 1) * ny), ny)
        for i in range(nc):
            edge_x_out[k, i] = carried_out[i, pl.ds(start + MARGIN, ny)]
        edge_x_out[k, nc] = press[pl.ds(start, ny)]
        edge_x_out[k, nc + 1] = perm[pl.ds(start, ny)]
    for i in range(nc + 2):
        source = carried_out.at[i] if i < nc else press if i == nc else perm
        skip = MARGIN if i < nc else 0
        low = source[pl.ds(skip, nx, stride=ny)]
        high = source[pl.ds(skip + ny - 1, nx, stride=ny)]
        edge_ya_out[i] = jnp.where(odd_s, low, high)
        edge_yb_out[i] = jnp.where(odd_s, high, low)


def fugacity_kernel(ny, psi, terms, consts, lnphi_out, lnphi_v, sems):
    nc, rows, _ = psi.shape
    shape3 = (ny // SUBLANES, SUBLANES, LANES)
    parts = sems.shape[0]
    stores = []
    for part in range(parts):
        for x in range(part * rows // parts // ny, (part + 1) * rows // parts // ny):
            span = pl.ds(x * ny, ny)
            e0, e1, e2 = (terms[k, span].reshape(shape3) for k in range(3))
            for i in range(nc):
                value = consts[nc + 8 + i] * e1 - e0 - psi[i, span].reshape(shape3) * e2
                lnphi_v[i, span] = value.reshape(ny, LANES).astype(BF16)
        span = pl.ds(part * rows // parts, rows // parts)
        copy = pltpu.make_async_copy(lnphi_v.at[:, span], lnphi_out.at[:, span], sems.at[part])
        copy.start()
        stores.append(copy)
    for copy in stores:
        copy.wait()


def flux_kernel(
    nx,
    ny,
    axes,
    many_x,
    carried,
    press,
    perm,
    pore,
    flag,
    mob,
    old,
    edge_ya,
    edge_yb,
    well_rows,
    loc,
    member,
    seg,
    strength,
    place,
    pcell,
    consts,
    own_press,
    order,
    exit_press,
    friction,
    *rest,
):
    edge_x, (resid_out, well_out, y_v, res_v, out_sems) = rest[:many_x], rest[many_x:]
    nc = carried.shape[0]
    g, s = lax.axis_index(axes[0]), lax.axis_index(axes[1])
    ng, ns = lax.axis_size(axes[0]), lax.axis_size(axes[1])
    odd_g, odd_s = g % 2 == 1, s % 2 == 1
    has_low_y, has_high_y = s > 0, s < ns - 1
    has_low_x, has_high_x = g > 0, g < ng - 1

    for i in range(nc + 2):
        a, b = edge_ya[i], edge_yb[i]
        low, high = jnp.where(odd_s, a, b), jnp.where(odd_s, b, a)
        if i == nc + 1:
            low, high = jnp.where(has_low_y, low, 0.0), jnp.where(has_high_y, high, 0.0)
        y_v[0, i] = low
        y_v[1, i] = high

    def side_x(i, high):
        if many_x == 1:
            return edge_x[0][i]
        return jnp.where(odd_g != high, edge_x[0][i], edge_x[1][i])

    row_hot, lane_hot = place_hots(loc[...], nx * ny)
    slot_hot = slot_hot_of(member[...], place[...])
    segments = own_press.shape[1]
    gathered = well_rows[...]
    seg_hot = hot(iota((LANES, loc.shape[1]), 0) == seg[...] + 2 * segments)
    p_seg = jnp.sum(mat_hot(gathered, seg_hot) * slot_hot, axis=0, keepdims=True)
    push = strength[...] * (pcell[...] - p_seg)
    flows = jnp.concatenate(
        [
            jnp.where(lane_hot, jnp.maximum(push, 0.0), 0.0),
            jnp.where(lane_hot, jnp.minimum(push, 0.0), 0.0),
        ],
        axis=0,
    )
    spread = hot_mat_nt(hot(row_hot), flows, 2)

    own = jnp.sum(gathered, axis=0, keepdims=True)
    well_p = own_press[...]
    rate = own[:, segments : 2 * segments] - (well_p - 1.0) * own[:, :segments]
    order_hot = hot(iota((segments, segments), 0) == order[...])
    both = mat_hot(jnp.concatenate([rate, well_p], axis=0), order_hot)
    upper = hot(iota((segments, segments), 0) <= iota((segments, segments), 1))
    running = mat_hot(both[0:1], upper)
    press_ord = both[1:2]
    after = hot(iota((segments, segments), 0) == iota((segments, segments), 1) + 1)
    last = iota((1, segments), 1) == segments - 1
    nexts = jnp.where(last, exit_press[...], mat_hot(press_ord, after))
    res_ord = press_ord - nexts - friction[...] * running * jnp.abs(running)
    well_out[...] = sum(mat_nt(piece, order_hot) for piece in pieces_of(res_ord, 3))

    lane = iota((ny, LANES), 1)
    row = iota((ny, LANES), 0)
    first, final = row == 0, row == ny - 1

    def const(k):
        return jnp.concatenate([consts[k]] * (ny // SUBLANES), axis=0)

    stores = []
    for x in range(nx):
        rows = pl.ds(x * ny, ny)
        p_a, k_a = press[rows], perm[rows]
        twice_k = 2.0 * k_a

        def face(p_b, k_b, axis):
            t = const(nc + axis) * (twice_k * k_b) * inverse(k_a + k_b)
            flow = t * (p_a - p_b)
            return jnp.maximum(flow, 0.0), jnp.minimum(flow, 0.0)

        def other_x(field, i, high):
            at = x + 1 if high else x - 1
            return field[pl.ds(at * ny, ny)] if 0 <= at < nx else side_x(i, high)

        def other_y(field, i, high):
            if high:
                return jnp.where(final, y_v[1, i, pl.ds(x, 1)], pltpu.roll(field, ny - 1, 0))
            return jnp.where(first, y_v[0, i, pl.ds(x, 1)], pltpu.roll(field, 1, 0))

        centre = pore[rows] * jnp.where(flag[rows] == 1, const(nc + 4), const(nc + 3))
        centre += spread[x * ny : (x + 1) * ny, :LANES]
        ins = []
        for high in (True, False):
            p_b, k_b = other_x(press, nc, high), other_x(perm, nc + 1, high)
            if x == nx - 1 and high:
                k_b = jnp.where(has_high_x, k_b, 0.0)
            if x == 0 and not high:
                k_b = jnp.where(has_low_x, k_b, 0.0)
            ins.append(face(p_b, k_b, 0))
        for high in (True, False):
            ins.append(face(other_y(p_a, nc, high), other_y(k_a, nc + 1, high), 1))
        for shift, edge in ((LANES - 1, LANES - 1), (1, 0)):
            k_b = jnp.where(lane == edge, 0.0, pltpu.roll(k_a, shift, 1))
            ins.append(face(pltpu.roll(p_a, shift, 1), k_b, 2))
        for out, _ in ins:
            centre += out
        ins = [into for _, into in ins]
        pushed = mob[rows] * spread[x * ny : (x + 1) * ny, LANES:]
        for i in range(nc):
            base = MARGIN + x * ny
            c = carried[i, pl.ds(base, ny)]
            value = centre * c - old[i, rows] + const(i) * pushed
            for k, high in ((0, True), (1, False)):
                at = x + 1 if high else x - 1
                inside = 0 <= at < nx
                c_b = carried[i, pl.ds(MARGIN + at * ny, ny)] if inside else side_x(i, high)
                value += ins[k] * c_b
            up, down = carried[i, pl.ds(base + 1, ny)], carried[i, pl.ds(base - 1, ny)]
            value += ins[2] * jnp.where(final, y_v[1, i, pl.ds(x, 1)], up)
            value += ins[3] * jnp.where(first, y_v[0, i, pl.ds(x, 1)], down)
            value += ins[4] * pltpu.roll(c, LANES - 1, 1)
            value += ins[5] * pltpu.roll(c, 1, 1)
            res_v[i, rows] = value
        copy = pltpu.make_async_copy(res_v.at[:, rows], resid_out.at[:, rows], out_sems.at[x])
        copy.start()
        stores.append(copy)
    for copy in stores:
        copy.wait()


def swaps_of(count, other):
    pairs = [(i, i + 1) for i in range(1 if other else 0, count - 1, 2)]
    return pairs + [(b, a) for a, b in pairs]


def other_swaps_of(groups, count):
    swaps = [(g * count + a, g * count + b) for g in range(groups) for a, b in swaps_of(count, True)]
    ends = [(g * count + e, (g ^ 1) * count + e) for g in range(groups) for e in (0, count - 1)]
    return sorted(swaps + ends)


def per_device(
    amount,
    press,
    heat,
    flag,
    perm,
    pore,
    old,
    trans,
    visc,
    crit,
    attract,
    covol,
    slope,
    coupling,
    inject,
    locale,
    member,
    seg,
    strength,
    place,
    order,
    seg_press,
    exit_press,
    friction,
):
    axes = ("grp", "sub")
    nc, nx, ny, nz = amount.shape
    ng, ns = lax.axis_size("grp"), lax.axis_size("sub")
    rows = nx * ny
    perfs = locale.shape[0]
    wells, segments = place.shape[1], seg_press.shape[1]
    flat = lambda a: a.reshape(a.shape[:-3] + (rows, nz))
    line = lambda a: a.reshape(1, perfs)
    vm = pl.BlockSpec(memory_space=pltpu.VMEM)
    hbm = pl.BlockSpec(memory_space=pltpu.HBM)
    many_x = 1 if ng == 2 else 2

    amount, old = flat(amount), flat(old)
    press, heat, flag, perm, pore = (flat(a) for a in (press, heat, flag, perm, pore))
    locale, member, seg, strength = (line(a) for a in (locale, member, seg, strength))
    exit_press, friction = exit_press.reshape(1, 1), friction.reshape(1, 1)

    sources = (
        coupling, crit, attract, slope, covol, heat, press, locale, member, place,
        flag, visc, trans, inject, seg, strength, seg_press, perm,
    )
    kept = [
        pltpu.SMEM(a.shape, a.dtype) if a.ndim == 1 else pltpu.VMEM(a.shape, a.dtype)
        for a in sources
    ]
    in_hbm = lambda a: pltpu.with_memory_space_constraint(a, pltpu.HBM)

    psi, terms, carried, mob, edge_x, edge_ya, edge_yb, part, pcell, consts = pl.pallas_call(
        functools.partial(phase_kernel, nx, ny, axes),
        out_shape=(
            jax.ShapeDtypeStruct((nc, rows, nz), F32),
            jax.ShapeDtypeStruct((3, rows, nz), F32),
            jax.ShapeDtypeStruct((nc, rows + 2 * MARGIN, nz), F32),
            jax.ShapeDtypeStruct((rows, nz), F32),
            jax.ShapeDtypeStruct((many_x, nc + 2, ny, nz), F32),
            jax.ShapeDtypeStruct((nc + 2, nx, nz), F32),
            jax.ShapeDtypeStruct((nc + 2, nx, nz), F32),
            jax.ShapeDtypeStruct((wells, LANES), F32),
            jax.ShapeDtypeStruct((1, perfs), F32),
            jax.ShapeDtypeStruct((2 * nc + 8, SUBLANES, LANES), F32),
        ),
        in_specs=[hbm] * (1 + len(sources)),
        out_specs=(vm,) * 10,
        scratch_shapes=[
            *kept,
            pltpu.VMEM((nc, rows, nz), F32),
            pltpu.VMEM((3 * nc * ny, nx * nz), BF16),
            pltpu.VMEM((4, rows, nz), F32),
            pltpu.VMEM((3, nc, SUBLANES, LANES), F32),
            pltpu.SemaphoreType.DMA((len(sources),)),
            pltpu.SemaphoreType.DMA((2,)),
        ],
        compiler_params=pltpu.CompilerParams(vmem_limit_bytes=VMEM_LIMIT),
        name="phase",
    )(in_hbm(amount), *(in_hbm(a) for a in sources))

    backward = [list(range(ns))[::-1]]
    well_rows = lax.all_to_all(
        part, "sub", split_axis=0, concat_axis=0, axis_index_groups=backward, tiled=True
    )
    got_x = [lax.ppermute(edge_x[k], "grp", swaps_of(ng, k == 1)) for k in range(many_x)]
    got_yb = lax.ppermute(edge_yb, axes, other_swaps_of(ng, ns))
    got_ya = lax.ppermute(edge_ya, "sub", swaps_of(ns, False))

    lnphi = pl.pallas_call(
        functools.partial(fugacity_kernel, ny),
        out_shape=jax.ShapeDtypeStruct((nc, rows, nz), BF16),
        in_specs=[vm] * 3,
        out_specs=hbm,
        scratch_shapes=[pltpu.VMEM((nc, rows, nz), BF16), pltpu.SemaphoreType.DMA((4,))],
        compiler_params=pltpu.CompilerParams(vmem_limit_bytes=VMEM_LIMIT),
        cost_estimate=pl.CostEstimate(
            flops=8 * nc * rows * nz, bytes_accessed=32 * nc * rows * nz, transcendentals=0
        ),
        name="fugacity",
    )(psi, terms, consts)

    resid, well = pl.pallas_call(
        functools.partial(flux_kernel, nx, ny, axes, many_x),
        out_shape=(
            jax.ShapeDtypeStruct((nc, rows, nz), F32),
            jax.ShapeDtypeStruct((1, segments), F32),
        ),
        in_specs=[vm] * (21 + many_x),
        out_specs=(hbm, vm),
        scratch_shapes=[
            pltpu.VMEM((2, nc + 2, nx, nz), F32),
            pltpu.VMEM((nc, rows, nz), F32),
            pltpu.SemaphoreType.DMA((nx,)),
        ],
        compiler_params=pltpu.CompilerParams(vmem_limit_bytes=VMEM_LIMIT),
        name="flux",
    )(
        carried, press, perm, pore, flag, mob, old, got_ya, got_yb, well_rows,
        locale, member, seg, strength, place, pcell,
        consts, seg_press, order, exit_press, friction, *got_x,
    )
    block = (nc, nx, ny, nz)
    return resid.reshape(block), lnphi.reshape(block), well


def solution(mesh):
    cells, parts = P("grp", "sub", None), P(None, "grp", "sub", None)
    listed = P(("grp", "sub"))
    row = P(("grp", "sub"), None)
    in_specs = (
        (parts,) + (cells,) * 5 + (parts,) + (P(),) * 8
        + (listed, row, listed, listed, P("grp", None), row, row, listed, listed)
    )
    return jax.shard_map(
        per_device, mesh=mesh, in_specs=in_specs, out_specs=(parts, parts, row), check_vma=False
    )
```

```python
import functools
import math

import jax
import jax.numpy as jnp
from jax import lax
from jax.experimental import pallas as pl
from jax.experimental.pallas import tpu as pltpu
from jax.sharding import PartitionSpec as P

NEWT = 8
ROOT_TWO = math.sqrt(2.0)
LANES = 128
SUBLANES = 8
F32 = jnp.float32
BF16 = jnp.bfloat16
VMEM_LIMIT = 48 * 1024 * 1024
MARGIN = 8
WHOLE = (
    "coupling", "crit", "attract", "slope", "covol", "heat", "press", "loc", "member", "place",
    "flag", "visc", "trans", "inject", "seg", "strength", "own_press", "perm",
)


def iota(shape, dim):
    return lax.broadcasted_iota(jnp.int32, shape, dim)


def pieces_of(x, count):
    out = []
    for _ in range(count):
        piece = x.astype(BF16)
        out.append(piece)
        x = x - piece.astype(F32)
    return out


def mat(a, b):
    return lax.dot_general(a, b, (((1,), (0,)), ((), ())), preferred_element_type=F32)


def mat_nt(a, b):
    return lax.dot_general(a, b, (((1,), (1,)), ((), ())), preferred_element_type=F32)


def mat_hot(x, hot, count=3):
    return sum(mat(piece, hot) for piece in pieces_of(x, count))


def hot_mat_nt(hot, x, count=3):
    return sum(mat_nt(hot, piece) for piece in pieces_of(x, count))


def inverse(x):
    r = pl.reciprocal(x, approx=True)
    return r * (2.0 - x * r)


def hot(cond):
    return jnp.where(cond, 1.0, 0.0).astype(BF16)


def place_hots(loc, rows):
    n = loc.shape[1]
    row_hot = iota((rows, n), 0) == loc // LANES
    lane_hot = iota((LANES, n), 0) == loc % LANES
    return row_hot, lane_hot


def slot_hot_of(member, place):
    wells = place.shape[1]
    slot_of = hot(iota((wells, wells), 0) == wells - 1 - place)
    member_hot = hot(iota((wells, member.shape[1]), 0) == member)
    return mat(slot_of, member_hot)


def phase_kernel(
    nx,
    ny,
    axes,
    amount,
    *rest,
):
    sources, rest = rest[: len(WHOLE)], rest[len(WHOLE) :]
    (
        psi_v,
        terms_out,
        carried_out,
        mob_out,
        edge_x_out,
        edge_ya_out,
        edge_yb_out,
        part_out,
        pcell_out,
        consts_out,
    ) = rest[:10]
    targets, rest = rest[10 : 10 + len(WHOLE)], rest[10 + len(WHOLE) :]
    amount_v, split_v, field_v, table_v, small_sems, in_sems = rest
    nc = amount.shape[0]
    per = 2
    chunks = nx // per
    half = chunks // 2
    rows = per * ny

    def go(source, target, sem):
        copy = pltpu.make_async_copy(source, target, sem)
        copy.start()
        return copy

    loads, copies = [], {}
    for k, name in enumerate(WHOLE):
        if name in ("press", "flag"):
            span = pl.ds(len(loads) * half * rows, half * rows)
            loads.append(go(amount.at[:, span], amount_v.at[:, span], in_sems.at[len(loads)]))
        copies[name] = go(sources[k], targets[k], small_sems.at[k])

    def arrived(*names):
        for name in names:
            copies[name].wait()
        return [targets[WHOLE.index(name)] for name in names]

    size = nc * ny
    spread = hot(iota((size, nc), 0) // ny == iota((size, nc), 1))
    same_row = iota((size, size), 0) % ny == iota((size, size), 1) % ny
    mixers = []
    (coupling,) = arrived("coupling")
    for piece in pieces_of(1.0 - coupling[...], 2):
        wide = mat(spread, piece).astype(BF16)
        mixers.append(jnp.where(same_row, mat_nt(wide, spread), 0.0).astype(BF16))
    mixer = jnp.concatenate([mixers[0], mixers[0], mixers[1]], axis=1)

    crit, attract, slope, covol = arrived("crit", "attract", "slope", "covol")
    for i in range(nc):
        root = jnp.sqrt(jnp.full((SUBLANES, LANES), attract[i], F32))
        kappa = jnp.full((SUBLANES, LANES), slope[i], F32)
        tc = jnp.full((SUBLANES, LANES), crit[i], F32)
        table_v[0, i] = root * (1.0 + kappa)
        table_v[1, i] = root * kappa / jnp.sqrt(tc)
        table_v[2, i] = jnp.full((SUBLANES, LANES), covol[i], F32)

    press, loc, member, place = arrived("press", "loc", "member", "place")
    row_hot, lane_hot = place_hots(loc[...], nx * ny)
    lane_hot = hot(lane_hot)

    def cells_of(field, count):
        found = mat_hot(field, lane_hot, count)
        return jnp.sum(jnp.where(row_hot, found, 0.0), axis=0, keepdims=True)

    p_cell = cells_of(press[...], 3)
    pcell_out[...] = p_cell
    slot_hot = slot_hot_of(member[...], place[...]).astype(BF16)
    (heat,) = arrived("heat")

    shape3 = (ny // SUBLANES, SUBLANES, LANES)
    for load in loads:
        load.wait()
    root_t = [jnp.sqrt(heat[pl.ds(x * ny, ny)].reshape(shape3)) for x in range(nx)]
    for x in range(nx):
        span, lanes = pl.ds(x * ny, ny), pl.ds(x * LANES, LANES)
        total = jnp.zeros(shape3, F32)
        volume = jnp.zeros(shape3, F32)
        for i in range(nc):
            o = amount_v[i, span].reshape(shape3)
            v = jnp.abs(table_v[0, i] - table_v[1, i] * root_t[x]) * o
            total += o
            volume += table_v[2, i] * o
            high, low = pieces_of(v.reshape(ny, LANES), 2)
            split_v[pl.ds(i * ny, ny), lanes] = high
            split_v[pl.ds(size + i * ny, ny), lanes] = low
            split_v[pl.ds(2 * size + i * ny, ny), lanes] = high
        field_v[0, span] = total.reshape(ny, LANES)
        field_v[1, span] = volume.reshape(ny, LANES)
    for c in range(chunks):
        mixed = mat(mixer, split_v[:, pl.ds(c * per * LANES, per * LANES)])
        for k in range(per):
            x = c * per + k
            span = pl.ds(x * ny, ny)
            total = jnp.zeros(shape3, F32)
            for i in range(nc):
                m = mixed[i * ny : (i + 1) * ny, k * LANES : (k + 1) * LANES].reshape(shape3)
                psi = jnp.abs(table_v[0, i] - table_v[1, i] * root_t[x]) * m
                total += amount_v[i, span].reshape(shape3) * psi
                psi_v[i, span] = psi.reshape(ny, LANES)
            field_v[2, span] = total.reshape(ny, LANES)

    flag, visc, trans, inject = arrived("flag", "visc", "trans", "inject")
    states = []
    for h in range(2):
        span = pl.ds(h * half * rows, half * rows)
        p, t = press[span], heat[span]
        liquid = flag[span] == 1
        r = inverse(field_v[0, span])
        rt = inverse(t)
        ratio_pt = p * rt
        beta = field_v[1, span] * r
        gr = ratio_pt * rt * r
        big_a = gr * r * field_v[2, span]
        big_b = ratio_pt * beta
        z = jnp.where(liquid, big_b + 0.01, 1.0 + big_b)
        c1 = big_a - 3.0 * big_b * big_b - 2.0 * big_b
        c0 = big_b * big_b + big_b * big_b * big_b - big_a * big_b
        states.append([z, big_b, big_b + 0.01, big_b - 1.0, c1, c0])
        field_v[1, span] = inverse(beta)
        field_v[3, span] = r
        terms_out[0, span] = ratio_pt
        terms_out[1, span] = 0.5 * big_a
        terms_out[2, span] = gr
    for _ in range(NEWT):
        for state in states:
            z, _, floor, c2, c1, c0 = state
            near = z + c2
            value = (near * z + c1) * z + c0
            incline = (near + near + z) * z + c1
            state[0] = jnp.maximum(z - value * inverse(jnp.maximum(incline, 0.1)), floor)
    for h, (z, big_b, *_) in enumerate(states):
        span = pl.ds(h * half * rows, half * rows)
        ratio_pt, gr = terms_out[0, span], terms_out[2, span]
        log_ratio = jnp.log(
            (z + (1.0 + ROOT_TWO) * big_b) * inverse(z + (1.0 - ROOT_TWO) * big_b)
        )
        lb = log_ratio * inverse(ROOT_TWO * big_b)
        mob = ratio_pt * inverse(z * jnp.where(flag[span] == 1, visc[1], visc[0]))
        mob_out[span] = mob
        field_v[3, span] = mob * field_v[3, span]
        terms_out[0, span] = jnp.log(z - big_b)
        terms_out[1, span] = (z - 1.0 + terms_out[1, span] * lb) * field_v[1, span]
        terms_out[2, span] = gr * lb
    for x in range(nx):
        span = pl.ds(x * ny, ny)
        mr = field_v[3, span]
        for i in range(nc):
            carried_out[i, pl.ds(MARGIN + x * ny, ny)] = mr * amount_v[i, span]

    total = sum(inject[i] for i in range(nc))
    share = 1.0 / jnp.full((1, LANES), total, F32)
    numbers = [trans[0], trans[1], trans[2], visc[0], visc[1]]
    for i in range(nc):
        consts_out[pl.ds(i, 1)] = inject[i] * share
        consts_out[pl.ds(nc + 8 + i, 1)] = jnp.full((1, LANES), covol[i], F32)
    for i, number in enumerate(numbers):
        consts_out[pl.ds(nc + i, 1)] = jnp.full((1, LANES), number, F32)

    seg, strength, own_press, perm = arrived("seg", "strength", "own_press", "perm")
    weight = strength[...] * cells_of(mob_out[...], 2)
    segments = own_press.shape[1]
    place_of = iota((LANES, loc.shape[1]), 0)
    sums = jnp.where(place_of == seg[...], weight, 0.0)
    sums += jnp.where(place_of == seg[...] + segments, weight * (p_cell - 1.0), 0.0)
    shift = hot(iota((segments, LANES), 0) + 2 * segments == iota((segments, LANES), 1))
    part_out[...] = hot_mat_nt(slot_hot, sums, 2) + mat_hot(own_press[...], shift)

    odd_g = lax.axis_index(axes[0]) % 2 == 1
    odd_s = lax.axis_index(axes[1]) % 2 == 1
    for k in range(edge_x_out.shape[0]):
        at_low = odd_g if k == 0 else jnp.logical_not(odd_g)
        start = pl.multiple_of(jnp.where(at_low, 0, (nx - 1) * ny), ny)
        for i in range(nc):
            edge_x_out[k, i] = carried_out[i, pl.ds(start + MARGIN, ny)]
        edge_x_out[k, nc] = press[pl.ds(start, ny)]
        edge_x_out[k, nc + 1] = perm[pl.ds(start, ny)]
    for i in range(nc + 2):
        source = carried_out.at[i] if i < nc else press if i == nc else perm
        skip = MARGIN if i < nc else 0
        low = source[pl.ds(skip, nx, stride=ny)]
        high = source[pl.ds(skip + ny - 1, nx, stride=ny)]
        edge_ya_out[i] = jnp.where(odd_s, low, high)
        edge_yb_out[i] = jnp.where(odd_s, high, low)


def fugacity_kernel(ny, psi, terms, consts, lnphi_out, lnphi_v, sems):
    nc, rows, _ = psi.shape
    parts = sems.shape[0]
    stores = []
    for part in range(parts):
        for x in range(part * rows // parts // ny, (part + 1) * rows // parts // ny):
            span = pl.ds(x * ny, ny)
            e0, e1, e2 = (terms[k, span] for k in range(3))
            for i in range(nc):
                value = consts[pl.ds(nc + 8 + i, 1)] * e1 - e0 - psi[i, span] * e2
                lnphi_v[i, span] = value.astype(BF16)
        span = pl.ds(part * rows // parts, rows // parts)
        copy = pltpu.make_async_copy(lnphi_v.at[:, span], lnphi_out.at[:, span], sems.at[part])
        copy.start()
        stores.append(copy)
    for copy in stores:
        copy.wait()


def flux_kernel(
    nx,
    ny,
    axes,
    many_x,
    carried,
    press_in,
    perm_in,
    pore_in,
    flag_in,
    old_in,
    mob,
    edge_ya,
    edge_yb,
    well_rows,
    loc,
    member,
    seg,
    strength,
    place,
    pcell,
    consts,
    own_press,
    order,
    exit_press,
    friction,
    *rest,
):
    edge_x, rest = rest[:many_x], rest[many_x:]
    resid_out, well_out, press, perm, pore, flag, old, y_v, res_v, in_sems, out_sems = rest
    nc = carried.shape[0]
    loads = []
    for k, (source, target) in enumerate(
        ((press_in, press), (perm_in, perm), (pore_in, pore), (flag_in, flag), (old_in, old))
    ):
        copy = pltpu.make_async_copy(source, target, in_sems.at[k])
        copy.start()
        loads.append(copy)
    g, s = lax.axis_index(axes[0]), lax.axis_index(axes[1])
    ng, ns = lax.axis_size(axes[0]), lax.axis_size(axes[1])
    odd_g, odd_s = g % 2 == 1, s % 2 == 1
    has_low_y, has_high_y = s > 0, s < ns - 1
    has_low_x, has_high_x = g > 0, g < ng - 1

    for i in range(nc + 2):
        a, b = edge_ya[i], edge_yb[i]
        low, high = jnp.where(odd_s, a, b), jnp.where(odd_s, b, a)
        if i == nc + 1:
            low, high = jnp.where(has_low_y, low, 0.0), jnp.where(has_high_y, high, 0.0)
        y_v[0, i] = low
        y_v[1, i] = high

    def side_x(i, high):
        if many_x == 1:
            return edge_x[0][i]
        return jnp.where(odd_g != high, edge_x[0][i], edge_x[1][i])

    row_hot, lane_hot = place_hots(loc[...], nx * ny)
    slot_hot = slot_hot_of(member[...], place[...])
    segments = own_press.shape[1]
    gathered = well_rows[...]
    seg_hot = hot(iota((LANES, loc.shape[1]), 0) == seg[...] + 2 * segments)
    p_seg = jnp.sum(mat_hot(gathered, seg_hot) * slot_hot, axis=0, keepdims=True)
    push = strength[...] * (pcell[...] - p_seg)
    flows = jnp.concatenate(
        [
            jnp.where(lane_hot, jnp.maximum(push, 0.0), 0.0),
            jnp.where(lane_hot, jnp.minimum(push, 0.0), 0.0),
        ],
        axis=0,
    )
    spread = hot_mat_nt(hot(row_hot), flows, 2)

    own = jnp.sum(gathered, axis=0, keepdims=True)
    well_p = own_press[...]
    rate = own[:, segments : 2 * segments] - (well_p - 1.0) * own[:, :segments]
    order_hot = hot(iota((segments, segments), 0) == order[...])
    both = mat_hot(jnp.concatenate([rate, well_p], axis=0), order_hot)
    upper = hot(iota((segments, segments), 0) <= iota((segments, segments), 1))
    running = mat_hot(both[0:1], upper)
    press_ord = both[1:2]
    after = hot(iota((segments, segments), 0) == iota((segments, segments), 1) + 1)
    last = iota((1, segments), 1) == segments - 1
    nexts = jnp.where(last, exit_press[...], mat_hot(press_ord, after))
    res_ord = press_ord - nexts - friction[...] * running * jnp.abs(running)
    well_out[...] = sum(mat_nt(piece, order_hot) for piece in pieces_of(res_ord, 3))

    lane = iota((ny, LANES), 1)
    row = iota((ny, LANES), 0)
    first, final = row == 0, row == ny - 1

    def const(k):
        return jnp.broadcast_to(consts[pl.ds(k, 1)], (ny, LANES))

    stores = []
    for load in loads:
        load.wait()
    for x in range(nx):
        rows = pl.ds(x * ny, ny)
        p_a, k_a = press[rows], perm[rows]
        twice_k = 2.0 * k_a

        def face(p_b, k_b, axis):
            t = const(nc + axis) * (twice_k * k_b) * inverse(k_a + k_b)
            flow = t * (p_a - p_b)
            return jnp.maximum(flow, 0.0), jnp.minimum(flow, 0.0)

        def other_x(field, i, high):
            at = x + 1 if high else x - 1
            return field[pl.ds(at * ny, ny)] if 0 <= at < nx else side_x(i, high)

        def other_y(field, i, high):
            if high:
                return jnp.where(final, y_v[1, i, pl.ds(x, 1)], pltpu.roll(field, ny - 1, 0))
            return jnp.where(first, y_v[0, i, pl.ds(x, 1)], pltpu.roll(field, 1, 0))

        centre = pore[rows] * jnp.where(flag[rows] == 1, const(nc + 4), const(nc + 3))
        centre += spread[x * ny : (x + 1) * ny, :LANES]
        ins = []
        for high in (True, False):
            p_b, k_b = other_x(press, nc, high), other_x(perm, nc + 1, high)
            if x == nx - 1 and high:
                k_b = jnp.where(has_high_x, k_b, 0.0)
            if x == 0 and not high:
                k_b = jnp.where(has_low_x, k_b, 0.0)
            ins.append(face(p_b, k_b, 0))
        for high in (True, False):
            ins.append(face(other_y(p_a, nc, high), other_y(k_a, nc + 1, high), 1))
        for shift, edge in ((LANES - 1, LANES - 1), (1, 0)):
            k_b = jnp.where(lane == edge, 0.0, pltpu.roll(k_a, shift, 1))
            ins.append(face(pltpu.roll(p_a, shift, 1), k_b, 2))
        for out, _ in ins:
            centre += out
        ins = [into for _, into in ins]
        pushed = mob[rows] * spread[x * ny : (x + 1) * ny, LANES:]
        for i in range(nc):
            base = MARGIN + x * ny
            c = carried[i, pl.ds(base, ny)]
            value = centre * c - old[i, rows] + const(i) * pushed
            for k, high in ((0, True), (1, False)):
                at = x + 1 if high else x - 1
                inside = 0 <= at < nx
                c_b = carried[i, pl.ds(MARGIN + at * ny, ny)] if inside else side_x(i, high)
                value += ins[k] * c_b
            up, down = carried[i, pl.ds(base + 1, ny)], carried[i, pl.ds(base - 1, ny)]
            value += ins[2] * jnp.where(final, y_v[1, i, pl.ds(x, 1)], up)
            value += ins[3] * jnp.where(first, y_v[0, i, pl.ds(x, 1)], down)
            value += ins[4] * pltpu.roll(c, LANES - 1, 1)
            value += ins[5] * pltpu.roll(c, 1, 1)
            res_v[i, rows] = value
        copy = pltpu.make_async_copy(res_v.at[:, rows], resid_out.at[:, rows], out_sems.at[x])
        copy.start()
        stores.append(copy)
    for copy in stores:
        copy.wait()


def swaps_of(count, other):
    pairs = [(i, i + 1) for i in range(1 if other else 0, count - 1, 2)]
    return pairs + [(b, a) for a, b in pairs]


def other_swaps_of(groups, count):
    swaps = [(g * count + a, g * count + b) for g in range(groups) for a, b in swaps_of(count, True)]
    ends = [(g * count + e, (g ^ 1) * count + e) for g in range(groups) for e in (0, count - 1)]
    return sorted(swaps + ends)


def per_device(
    amount,
    press,
    heat,
    flag,
    perm,
    pore,
    old,
    trans,
    visc,
    crit,
    attract,
    covol,
    slope,
    coupling,
    inject,
    locale,
    member,
    seg,
    strength,
    place,
    order,
    seg_press,
    exit_press,
    friction,
):
    axes = ("grp", "sub")
    nc, nx, ny, nz = amount.shape
    ng, ns = lax.axis_size("grp"), lax.axis_size("sub")
    rows = nx * ny
    perfs = locale.shape[0]
    wells, segments = place.shape[1], seg_press.shape[1]
    flat = lambda a: a.reshape(a.shape[:-3] + (rows, nz))
    line = lambda a: a.reshape(1, perfs)
    vm = pl.BlockSpec(memory_space=pltpu.VMEM)
    hbm = pl.BlockSpec(memory_space=pltpu.HBM)
    many_x = 1 if ng == 2 else 2

    amount, old = flat(amount), flat(old)
    press, heat, flag, perm, pore = (flat(a) for a in (press, heat, flag, perm, pore))
    locale, member, seg, strength = (line(a) for a in (locale, member, seg, strength))
    exit_press, friction = exit_press.reshape(1, 1), friction.reshape(1, 1)

    sources = (
        coupling, crit, attract, slope, covol, heat, press, locale, member, place,
        flag, visc, trans, inject, seg, strength, seg_press, perm,
    )
    kept = [
        pltpu.SMEM(a.shape, a.dtype) if a.ndim == 1 else pltpu.VMEM(a.shape, a.dtype)
        for a in sources
    ]
    in_hbm = lambda a: pltpu.with_memory_space_constraint(a, pltpu.HBM)

    psi, terms, carried, mob, edge_x, edge_ya, edge_yb, part, pcell, consts = pl.pallas_call(
        functools.partial(phase_kernel, nx, ny, axes),
        out_shape=(
            jax.ShapeDtypeStruct((nc, rows, nz), F32),
            jax.ShapeDtypeStruct((3, rows, nz), F32),
            jax.ShapeDtypeStruct((nc, rows + 2 * MARGIN, nz), F32),
            jax.ShapeDtypeStruct((rows, nz), F32),
            jax.ShapeDtypeStruct((many_x, nc + 2, ny, nz), F32),
            jax.ShapeDtypeStruct((nc + 2, nx, nz), F32),
            jax.ShapeDtypeStruct((nc + 2, nx, nz), F32),
            jax.ShapeDtypeStruct((wells, LANES), F32),
            jax.ShapeDtypeStruct((1, perfs), F32),
            jax.ShapeDtypeStruct((2 * nc + 8, LANES), F32),
        ),
        in_specs=[hbm] * (1 + len(sources)),
        out_specs=(vm,) * 10,
        scratch_shapes=[
            *kept,
            pltpu.VMEM((nc, rows, nz), F32),
            pltpu.VMEM((3 * nc * ny, nx * nz), BF16),
            pltpu.VMEM((4, rows, nz), F32),
            pltpu.VMEM((3, nc, SUBLANES, LANES), F32),
            pltpu.SemaphoreType.DMA((len(sources),)),
            pltpu.SemaphoreType.DMA((2,)),
        ],
        compiler_params=pltpu.CompilerParams(vmem_limit_bytes=VMEM_LIMIT),
        name="phase",
    )(in_hbm(amount), *(in_hbm(a) for a in sources))

    backward = [list(range(ns))[::-1]]
    well_rows = lax.all_to_all(
        part, "sub", split_axis=0, concat_axis=0, axis_index_groups=backward, tiled=True
    )
    got_x = [lax.ppermute(edge_x[k], "grp", swaps_of(ng, k == 1)) for k in range(many_x)]
    got_yb = lax.ppermute(edge_yb, axes, other_swaps_of(ng, ns))
    got_ya = lax.ppermute(edge_ya, "sub", swaps_of(ns, False))

    lnphi = pl.pallas_call(
        functools.partial(fugacity_kernel, ny),
        out_shape=jax.ShapeDtypeStruct((nc, rows, nz), BF16),
        in_specs=[vm] * 3,
        out_specs=hbm,
        scratch_shapes=[pltpu.VMEM((nc, rows, nz), BF16), pltpu.SemaphoreType.DMA((4,))],
        compiler_params=pltpu.CompilerParams(vmem_limit_bytes=VMEM_LIMIT),
        cost_estimate=pl.CostEstimate(
            flops=8 * nc * rows * nz, bytes_accessed=32 * nc * rows * nz, transcendentals=0
        ),
        name="fugacity",
    )(psi, terms, consts)

    resid, well = pl.pallas_call(
        functools.partial(flux_kernel, nx, ny, axes, many_x),
        out_shape=(
            jax.ShapeDtypeStruct((nc, rows, nz), F32),
            jax.ShapeDtypeStruct((1, segments), F32),
        ),
        in_specs=[vm] + [hbm] * 5 + [vm] * (15 + many_x),
        out_specs=(hbm, vm),
        scratch_shapes=[
            *(pltpu.VMEM(a.shape, a.dtype) for a in (press, perm, pore, flag, old)),
            pltpu.VMEM((2, nc + 2, nx, nz), F32),
            pltpu.VMEM((nc, rows, nz), F32),
            pltpu.SemaphoreType.DMA((5,)),
            pltpu.SemaphoreType.DMA((nx,)),
        ],
        compiler_params=pltpu.CompilerParams(vmem_limit_bytes=VMEM_LIMIT),
        name="flux",
    )(
        carried, *(in_hbm(a) for a in (press, perm, pore, flag, old)), mob, got_ya, got_yb, well_rows,
        locale, member, seg, strength, place, pcell,
        consts, seg_press, order, exit_press, friction, *got_x,
    )
    block = (nc, nx, ny, nz)
    return resid.reshape(block), lnphi.reshape(block), well


def solution(mesh):
    cells, parts = P("grp", "sub", None), P(None, "grp", "sub", None)
    listed = P(("grp", "sub"))
    row = P(("grp", "sub"), None)
    in_specs = (
        (parts,) + (cells,) * 5 + (parts,) + (P(),) * 8
        + (listed, row, listed, listed, P("grp", None), row, row, listed, listed)
    )
    return jax.shard_map(
        per_device, mesh=mesh, in_specs=in_specs, out_specs=(parts, parts, row), check_vma=False
    )
```

```python
import functools
import math

import jax
import jax.numpy as jnp
from jax import lax
from jax.experimental import pallas as pl
from jax.experimental.pallas import tpu as pltpu
from jax.sharding import PartitionSpec as P

NEWT = 8
ROOT_TWO = math.sqrt(2.0)
LANES = 128
SUBLANES = 8
F32 = jnp.float32
BF16 = jnp.bfloat16
VMEM_LIMIT = 48 * 1024 * 1024
MARGIN = 8
WHOLE = (
    "coupling", "crit", "attract", "slope", "covol", "heat", "press", "loc", "member", "place",
    "flag", "visc", "trans", "inject", "seg", "strength", "own_press", "perm",
)


def iota(shape, dim):
    return lax.broadcasted_iota(jnp.int32, shape, dim)


def pieces_of(x, count):
    out = []
    for _ in range(count):
        piece = x.astype(BF16)
        out.append(piece)
        x = x - piece.astype(F32)
    return out


def mat(a, b):
    return lax.dot_general(a, b, (((1,), (0,)), ((), ())), preferred_element_type=F32)


def mat_nt(a, b):
    return lax.dot_general(a, b, (((1,), (1,)), ((), ())), preferred_element_type=F32)


def mat_hot(x, hot, count=3):
    return sum(mat(piece, hot) for piece in pieces_of(x, count))


def hot_mat_nt(hot, x, count=3):
    return sum(mat_nt(hot, piece) for piece in pieces_of(x, count))


def inverse(x):
    r = pl.reciprocal(x, approx=True)
    return r * (2.0 - x * r)


def hot(cond):
    return jnp.where(cond, 1.0, 0.0).astype(BF16)


def place_hots(loc, rows):
    n = loc.shape[1]
    row_hot = iota((rows, n), 0) == loc // LANES
    lane_hot = iota((LANES, n), 0) == loc % LANES
    return row_hot, lane_hot


def slot_hot_of(member, place):
    wells = place.shape[1]
    slot_of = hot(iota((wells, wells), 0) == wells - 1 - place)
    member_hot = hot(iota((wells, member.shape[1]), 0) == member)
    return mat(slot_of, member_hot)


def phase_kernel(
    nx,
    ny,
    axes,
    amount,
    *rest,
):
    sources, rest = rest[: len(WHOLE)], rest[len(WHOLE) :]
    (
        psi_v,
        terms_out,
        carried_out,
        mob_out,
        edge_x_out,
        edge_ya_out,
        edge_yb_out,
        part_out,
        pcell_out,
        consts_out,
    ) = rest[:10]
    targets, rest = rest[10 : 10 + len(WHOLE)], rest[10 + len(WHOLE) :]
    amount_v, split_v, field_v, table_v, small_sems, in_sems = rest
    nc = amount.shape[0]
    per = 2
    chunks = nx // per
    half = chunks // 2
    rows = per * ny

    def go(source, target, sem):
        copy = pltpu.make_async_copy(source, target, sem)
        copy.start()
        return copy

    loads, copies = [], {}
    for k, name in enumerate(WHOLE):
        if name in ("press", "flag"):
            span = pl.ds(len(loads) * half * rows, half * rows)
            loads.append(go(amount.at[:, span], amount_v.at[:, span], in_sems.at[len(loads)]))
        copies[name] = go(sources[k], targets[k], small_sems.at[k])

    def arrived(*names):
        return [targets[WHOLE.index(name)] for name in names]

    for copy in [*copies.values(), *loads]:
        copy.wait()

    size = nc * ny
    spread = hot(iota((size, nc), 0) // ny == iota((size, nc), 1))
    same_row = iota((size, size), 0) % ny == iota((size, size), 1) % ny
    mixers = []
    (coupling,) = arrived("coupling")
    for piece in pieces_of(1.0 - coupling[...], 2):
        wide = mat(spread, piece).astype(BF16)
        mixers.append(jnp.where(same_row, mat_nt(wide, spread), 0.0).astype(BF16))
    mixer = jnp.concatenate([mixers[0], mixers[0], mixers[1]], axis=1)

    crit, attract, slope, covol = arrived("crit", "attract", "slope", "covol")
    for i in range(nc):
        root = jnp.sqrt(jnp.full((SUBLANES, LANES), attract[i], F32))
        kappa = jnp.full((SUBLANES, LANES), slope[i], F32)
        tc = jnp.full((SUBLANES, LANES), crit[i], F32)
        table_v[0, i] = root * (1.0 + kappa)
        table_v[1, i] = root * kappa / jnp.sqrt(tc)
        table_v[2, i] = jnp.full((SUBLANES, LANES), covol[i], F32)

    press, loc, member, place = arrived("press", "loc", "member", "place")
    row_hot, lane_hot = place_hots(loc[...], nx * ny)
    lane_hot = hot(lane_hot)

    def cells_of(field, count):
        found = mat_hot(field, lane_hot, count)
        return jnp.sum(jnp.where(row_hot, found, 0.0), axis=0, keepdims=True)

    p_cell = cells_of(press[...], 3)
    pcell_out[...] = p_cell
    slot_hot = slot_hot_of(member[...], place[...]).astype(BF16)
    (heat,) = arrived("heat")

    shape3 = (ny // SUBLANES, SUBLANES, LANES)
    root_t = [jnp.sqrt(heat[pl.ds(x * ny, ny)].reshape(shape3)) for x in range(nx)]
    for x in range(nx):
        span, lanes = pl.ds(x * ny, ny), pl.ds(x * LANES, LANES)
        total = jnp.zeros(shape3, F32)
        volume = jnp.zeros(shape3, F32)
        for i in range(nc):
            o = amount_v[i, span].reshape(shape3)
            v = jnp.abs(table_v[0, i] - table_v[1, i] * root_t[x]) * o
            total += o
            volume += table_v[2, i] * o
            high, low = pieces_of(v.reshape(ny, LANES), 2)
            split_v[pl.ds(i * ny, ny), lanes] = high
            split_v[pl.ds(size + i * ny, ny), lanes] = low
            split_v[pl.ds(2 * size + i * ny, ny), lanes] = high
        field_v[0, span] = total.reshape(ny, LANES)
        field_v[1, span] = volume.reshape(ny, LANES)
    for c in range(chunks):
        mixed = mat(mixer, split_v[:, pl.ds(c * per * LANES, per * LANES)])
        for k in range(per):
            x = c * per + k
            span = pl.ds(x * ny, ny)
            total = jnp.zeros(shape3, F32)
            for i in range(nc):
                m = mixed[i * ny : (i + 1) * ny, k * LANES : (k + 1) * LANES].reshape(shape3)
                psi = jnp.abs(table_v[0, i] - table_v[1, i] * root_t[x]) * m
                total += amount_v[i, span].reshape(shape3) * psi
                psi_v[i, span] = psi.reshape(ny, LANES)
            field_v[2, span] = total.reshape(ny, LANES)

    flag, visc, trans, inject = arrived("flag", "visc", "trans", "inject")
    states = []
    for h in range(2):
        span = pl.ds(h * half * rows, half * rows)
        p, t = press[span], heat[span]
        liquid = flag[span] == 1
        r = inverse(field_v[0, span])
        rt = inverse(t)
        ratio_pt = p * rt
        beta = field_v[1, span] * r
        gr = ratio_pt * rt * r
        big_a = gr * r * field_v[2, span]
        big_b = ratio_pt * beta
        z = jnp.where(liquid, big_b + 0.01, 1.0 + big_b)
        c1 = big_a - 3.0 * big_b * big_b - 2.0 * big_b
        c0 = big_b * big_b + big_b * big_b * big_b - big_a * big_b
        states.append([z, big_b, big_b + 0.01, big_b - 1.0, c1, c0])
        field_v[1, span] = inverse(beta)
        field_v[3, span] = r
        terms_out[0, span] = ratio_pt
        terms_out[1, span] = 0.5 * big_a
        terms_out[2, span] = gr
    for _ in range(NEWT):
        for state in states:
            z, _, floor, c2, c1, c0 = state
            near = z + c2
            value = (near * z + c1) * z + c0
            incline = (near + near + z) * z + c1
            state[0] = jnp.maximum(z - value * inverse(jnp.maximum(incline, 0.1)), floor)
    for h, (z, big_b, *_) in enumerate(states):
        span = pl.ds(h * half * rows, half * rows)
        ratio_pt, gr = terms_out[0, span], terms_out[2, span]
        log_ratio = jnp.log(
            (z + (1.0 + ROOT_TWO) * big_b) * inverse(z + (1.0 - ROOT_TWO) * big_b)
        )
        lb = log_ratio * inverse(ROOT_TWO * big_b)
        mob = ratio_pt * inverse(z * jnp.where(flag[span] == 1, visc[1], visc[0]))
        mob_out[span] = mob
        field_v[3, span] = mob * field_v[3, span]
        terms_out[0, span] = jnp.log(z - big_b)
        terms_out[1, span] = (z - 1.0 + terms_out[1, span] * lb) * field_v[1, span]
        terms_out[2, span] = gr * lb
    for x in range(nx):
        span = pl.ds(x * ny, ny)
        mr = field_v[3, span]
        for i in range(nc):
            carried_out[i, pl.ds(MARGIN + x * ny, ny)] = mr * amount_v[i, span]

    total = sum(inject[i] for i in range(nc))
    share = 1.0 / jnp.full((1, LANES), total, F32)
    numbers = [trans[0], trans[1], trans[2], visc[0], visc[1]]
    for i in range(nc):
        consts_out[pl.ds(i, 1)] = inject[i] * share
        consts_out[pl.ds(nc + 8 + i, 1)] = jnp.full((1, LANES), covol[i], F32)
    for i, number in enumerate(numbers):
        consts_out[pl.ds(nc + i, 1)] = jnp.full((1, LANES), number, F32)

    seg, strength, own_press, perm = arrived("seg", "strength", "own_press", "perm")
    weight = strength[...] * cells_of(mob_out[...], 2)
    segments = own_press.shape[1]
    place_of = iota((LANES, loc.shape[1]), 0)
    sums = jnp.where(place_of == seg[...], weight, 0.0)
    sums += jnp.where(place_of == seg[...] + segments, weight * (p_cell - 1.0), 0.0)
    shift = hot(iota((segments, LANES), 0) + 2 * segments == iota((segments, LANES), 1))
    part_out[...] = hot_mat_nt(slot_hot, sums, 2) + mat_hot(own_press[...], shift)

    odd_g = lax.axis_index(axes[0]) % 2 == 1
    odd_s = lax.axis_index(axes[1]) % 2 == 1
    for k in range(edge_x_out.shape[0]):
        at_low = odd_g if k == 0 else jnp.logical_not(odd_g)
        start = pl.multiple_of(jnp.where(at_low, 0, (nx - 1) * ny), ny)
        for i in range(nc):
            edge_x_out[k, i] = carried_out[i, pl.ds(start + MARGIN, ny)]
        edge_x_out[k, nc] = press[pl.ds(start, ny)]
        edge_x_out[k, nc + 1] = perm[pl.ds(start, ny)]
    for i in range(nc + 2):
        source = carried_out.at[i] if i < nc else press if i == nc else perm
        skip = MARGIN if i < nc else 0
        low = source[pl.ds(skip, nx, stride=ny)]
        high = source[pl.ds(skip + ny - 1, nx, stride=ny)]
        edge_ya_out[i] = jnp.where(odd_s, low, high)
        edge_yb_out[i] = jnp.where(odd_s, high, low)


def fugacity_kernel(ny, psi, terms, consts, lnphi_out, lnphi_v, sems):
    nc, rows, _ = psi.shape
    parts = sems.shape[0]
    stores = []
    for part in range(parts):
        for x in range(part * rows // parts // ny, (part + 1) * rows // parts // ny):
            span = pl.ds(x * ny, ny)
            e0, e1, e2 = (terms[k, span] for k in range(3))
            for i in range(nc):
                value = consts[pl.ds(nc + 8 + i, 1)] * e1 - e0 - psi[i, span] * e2
                lnphi_v[i, span] = value.astype(BF16)
        span = pl.ds(part * rows // parts, rows // parts)
        copy = pltpu.make_async_copy(lnphi_v.at[:, span], lnphi_out.at[:, span], sems.at[part])
        copy.start()
        stores.append(copy)
    for copy in stores:
        copy.wait()


def flux_kernel(
    nx,
    ny,
    axes,
    many_x,
    carried,
    press,
    perm,
    pore,
    flag,
    old_in,
    mob,
    edge_ya,
    edge_yb,
    well_rows,
    loc,
    member,
    seg,
    strength,
    place,
    pcell,
    consts,
    own_press,
    order,
    exit_press,
    friction,
    *rest,
):
    edge_x, rest = rest[:many_x], rest[many_x:]
    resid_out, well_out, old, y_v, res_v, in_sems, out_sems = rest
    nc = carried.shape[0]
    loads = []
    for k in range(2):
        span = pl.ds(k * nx * ny // 2, nx * ny // 2)
        copy = pltpu.make_async_copy(old_in.at[:, span], old.at[:, span], in_sems.at[k])
        copy.start()
        loads.append(copy)
    g, s = lax.axis_index(axes[0]), lax.axis_index(axes[1])
    ng, ns = lax.axis_size(axes[0]), lax.axis_size(axes[1])
    odd_g, odd_s = g % 2 == 1, s % 2 == 1
    has_low_y, has_high_y = s > 0, s < ns - 1
    has_low_x, has_high_x = g > 0, g < ng - 1

    for i in range(nc + 2):
        a, b = edge_ya[i], edge_yb[i]
        low, high = jnp.where(odd_s, a, b), jnp.where(odd_s, b, a)
        if i == nc + 1:
            low, high = jnp.where(has_low_y, low, 0.0), jnp.where(has_high_y, high, 0.0)
        y_v[0, i] = low
        y_v[1, i] = high

    def side_x(i, high):
        if many_x == 1:
            return edge_x[0][i]
        return jnp.where(odd_g != high, edge_x[0][i], edge_x[1][i])

    row_hot, lane_hot = place_hots(loc[...], nx * ny)
    slot_hot = slot_hot_of(member[...], place[...])
    segments = own_press.shape[1]
    gathered = well_rows[...]
    seg_hot = hot(iota((LANES, loc.shape[1]), 0) == seg[...] + 2 * segments)
    p_seg = jnp.sum(mat_hot(gathered, seg_hot) * slot_hot, axis=0, keepdims=True)
    push = strength[...] * (pcell[...] - p_seg)
    flows = jnp.concatenate(
        [
            jnp.where(lane_hot, jnp.maximum(push, 0.0), 0.0),
            jnp.where(lane_hot, jnp.minimum(push, 0.0), 0.0),
        ],
        axis=0,
    )
    spread = hot_mat_nt(hot(row_hot), flows, 2)

    own = jnp.sum(gathered, axis=0, keepdims=True)
    well_p = own_press[...]
    rate = own[:, segments : 2 * segments] - (well_p - 1.0) * own[:, :segments]
    order_hot = hot(iota((segments, segments), 0) == order[...])
    both = mat_hot(jnp.concatenate([rate, well_p], axis=0), order_hot)
    upper = hot(iota((segments, segments), 0) <= iota((segments, segments), 1))
    running = mat_hot(both[0:1], upper)
    press_ord = both[1:2]
    after = hot(iota((segments, segments), 0) == iota((segments, segments), 1) + 1)
    last = iota((1, segments), 1) == segments - 1
    nexts = jnp.where(last, exit_press[...], mat_hot(press_ord, after))
    res_ord = press_ord - nexts - friction[...] * running * jnp.abs(running)
    well_out[...] = sum(mat_nt(piece, order_hot) for piece in pieces_of(res_ord, 3))

    lane = iota((ny, LANES), 1)
    row = iota((ny, LANES), 0)
    first, final = row == 0, row == ny - 1

    def const(k):
        return jnp.broadcast_to(consts[pl.ds(k, 1)], (ny, LANES))

    stores = []
    for x in range(nx):
        if x * 2 % nx == 0:
            loads[x * 2 // nx].wait()
        rows = pl.ds(x * ny, ny)
        p_a, k_a = press[rows], perm[rows]
        twice_k = 2.0 * k_a

        def face(p_b, k_b, axis):
            t = const(nc + axis) * (twice_k * k_b) * inverse(k_a + k_b)
            flow = t * (p_a - p_b)
            return jnp.maximum(flow, 0.0), jnp.minimum(flow, 0.0)

        def other_x(field, i, high):
            at = x + 1 if high else x - 1
            return field[pl.ds(at * ny, ny)] if 0 <= at < nx else side_x(i, high)

        def other_y(field, i, high):
            if high:
                return jnp.where(final, y_v[1, i, pl.ds(x, 1)], pltpu.roll(field, ny - 1, 0))
            return jnp.where(first, y_v[0, i, pl.ds(x, 1)], pltpu.roll(field, 1, 0))

        centre = pore[rows] * jnp.where(flag[rows] == 1, const(nc + 4), const(nc + 3))
        centre += spread[x * ny : (x + 1) * ny, :LANES]
        ins = []
        for high in (True, False):
            p_b, k_b = other_x(press, nc, high), other_x(perm, nc + 1, high)
            if x == nx - 1 and high:
                k_b = jnp.where(has_high_x, k_b, 0.0)
            if x == 0 and not high:
                k_b = jnp.where(has_low_x, k_b, 0.0)
            ins.append(face(p_b, k_b, 0))
        for high in (True, False):
            ins.append(face(other_y(p_a, nc, high), other_y(k_a, nc + 1, high), 1))
        for shift, edge in ((LANES - 1, LANES - 1), (1, 0)):
            k_b = jnp.where(lane == edge, 0.0, pltpu.roll(k_a, shift, 1))
            ins.append(face(pltpu.roll(p_a, shift, 1), k_b, 2))
        for out, _ in ins:
            centre += out
        ins = [into for _, into in ins]
        pushed = mob[rows] * spread[x * ny : (x + 1) * ny, LANES:]
        for i in range(nc):
            base = MARGIN + x * ny
            c = carried[i, pl.ds(base, ny)]
            value = centre * c - old[i, rows] + const(i) * pushed
            for k, high in ((0, True), (1, False)):
                at = x + 1 if high else x - 1
                inside = 0 <= at < nx
                c_b = carried[i, pl.ds(MARGIN + at * ny, ny)] if inside else side_x(i, high)
                value += ins[k] * c_b
            up, down = carried[i, pl.ds(base + 1, ny)], carried[i, pl.ds(base - 1, ny)]
            value += ins[2] * jnp.where(final, y_v[1, i, pl.ds(x, 1)], up)
            value += ins[3] * jnp.where(first, y_v[0, i, pl.ds(x, 1)], down)
            value += ins[4] * pltpu.roll(c, LANES - 1, 1)
            value += ins[5] * pltpu.roll(c, 1, 1)
            res_v[i, rows] = value
        copy = pltpu.make_async_copy(res_v.at[:, rows], resid_out.at[:, rows], out_sems.at[x])
        copy.start()
        stores.append(copy)
    for copy in stores:
        copy.wait()


def swaps_of(count, other):
    pairs = [(i, i + 1) for i in range(1 if other else 0, count - 1, 2)]
    return pairs + [(b, a) for a, b in pairs]


def other_swaps_of(groups, count):
    swaps = [(g * count + a, g * count + b) for g in range(groups) for a, b in swaps_of(count, True)]
    ends = [(g * count + e, (g ^ 1) * count + e) for g in range(groups) for e in (0, count - 1)]
    return sorted(swaps + ends)


def per_device(
    amount,
    press,
    heat,
    flag,
    perm,
    pore,
    old,
    trans,
    visc,
    crit,
    attract,
    covol,
    slope,
    coupling,
    inject,
    locale,
    member,
    seg,
    strength,
    place,
    order,
    seg_press,
    exit_press,
    friction,
):
    axes = ("grp", "sub")
    nc, nx, ny, nz = amount.shape
    ng, ns = lax.axis_size("grp"), lax.axis_size("sub")
    rows = nx * ny
    perfs = locale.shape[0]
    wells, segments = place.shape[1], seg_press.shape[1]
    flat = lambda a: a.reshape(a.shape[:-3] + (rows, nz))
    line = lambda a: a.reshape(1, perfs)
    vm = pl.BlockSpec(memory_space=pltpu.VMEM)
    hbm = pl.BlockSpec(memory_space=pltpu.HBM)
    many_x = 1 if ng == 2 else 2

    amount, old = flat(amount), flat(old)
    press, heat, flag, perm, pore = (flat(a) for a in (press, heat, flag, perm, pore))
    locale, member, seg, strength = (line(a) for a in (locale, member, seg, strength))
    exit_press, friction = exit_press.reshape(1, 1), friction.reshape(1, 1)

    sources = (
        coupling, crit, attract, slope, covol, heat, press, locale, member, place,
        flag, visc, trans, inject, seg, strength, seg_press, perm,
    )
    kept = [
        pltpu.SMEM(a.shape, a.dtype) if a.ndim == 1 else pltpu.VMEM(a.shape, a.dtype)
        for a in sources
    ]
    in_hbm = lambda a: pltpu.with_memory_space_constraint(a, pltpu.HBM)

    psi, terms, carried, mob, edge_x, edge_ya, edge_yb, part, pcell, consts = pl.pallas_call(
        functools.partial(phase_kernel, nx, ny, axes),
        out_shape=(
            jax.ShapeDtypeStruct((nc, rows, nz), F32),
            jax.ShapeDtypeStruct((3, rows, nz), F32),
            jax.ShapeDtypeStruct((nc, rows + 2 * MARGIN, nz), F32),
            jax.ShapeDtypeStruct((rows, nz), F32),
            jax.ShapeDtypeStruct((many_x, nc + 2, ny, nz), F32),
            jax.ShapeDtypeStruct((nc + 2, nx, nz), F32),
            jax.ShapeDtypeStruct((nc + 2, nx, nz), F32),
            jax.ShapeDtypeStruct((wells, LANES), F32),
            jax.ShapeDtypeStruct((1, perfs), F32),
            jax.ShapeDtypeStruct((2 * nc + 8, LANES), F32),
        ),
        in_specs=[hbm] * (1 + len(sources)),
        out_specs=(vm,) * 10,
        scratch_shapes=[
            *kept,
            pltpu.VMEM((nc, rows, nz), F32),
            pltpu.VMEM((3 * nc * ny, nx * nz), BF16),
            pltpu.VMEM((4, rows, nz), F32),
            pltpu.VMEM((3, nc, SUBLANES, LANES), F32),
            pltpu.SemaphoreType.DMA((len(sources),)),
            pltpu.SemaphoreType.DMA((2,)),
        ],
        compiler_params=pltpu.CompilerParams(vmem_limit_bytes=VMEM_LIMIT),
        name="phase",
    )(in_hbm(amount), *(in_hbm(a) for a in sources))

    got_x = [lax.ppermute(edge_x[k], "grp", swaps_of(ng, k == 1)) for k in range(many_x)]
    got_yb = lax.ppermute(edge_yb, axes, other_swaps_of(ng, ns))
    got_ya = lax.ppermute(edge_ya, "sub", swaps_of(ns, False))
    backward = [list(range(ns))[::-1]]
    well_rows = lax.all_to_all(
        part, "sub", split_axis=0, concat_axis=0, axis_index_groups=backward, tiled=True
    )

    lnphi = pl.pallas_call(
        functools.partial(fugacity_kernel, ny),
        out_shape=jax.ShapeDtypeStruct((nc, rows, nz), BF16),
        in_specs=[vm] * 3,
        out_specs=hbm,
        scratch_shapes=[pltpu.VMEM((nc, rows, nz), BF16), pltpu.SemaphoreType.DMA((4,))],
        compiler_params=pltpu.CompilerParams(vmem_limit_bytes=VMEM_LIMIT),
        cost_estimate=pl.CostEstimate(
            flops=8 * nc * rows * nz, bytes_accessed=256 * nc * rows * nz, transcendentals=0
        ),
        name="fugacity",
    )(psi, terms, consts)

    resid, well = pl.pallas_call(
        functools.partial(flux_kernel, nx, ny, axes, many_x),
        out_shape=(
            jax.ShapeDtypeStruct((nc, rows, nz), F32),
            jax.ShapeDtypeStruct((1, segments), F32),
        ),
        in_specs=[vm] * 5 + [hbm] + [vm] * (15 + many_x),
        out_specs=(hbm, vm),
        scratch_shapes=[
            pltpu.VMEM((nc, rows, nz), F32),
            pltpu.VMEM((2, nc + 2, nx, nz), F32),
            pltpu.VMEM((nc, rows, nz), F32),
            pltpu.SemaphoreType.DMA((2,)),
            pltpu.SemaphoreType.DMA((nx,)),
        ],
        compiler_params=pltpu.CompilerParams(vmem_limit_bytes=VMEM_LIMIT),
        name="flux",
    )(
        carried, press, perm, pore, flag, in_hbm(old), mob, got_ya, got_yb, well_rows,
        locale, member, seg, strength, place, pcell,
        consts, seg_press, order, exit_press, friction, *got_x,
    )
    block = (nc, nx, ny, nz)
    return resid.reshape(block), lnphi.reshape(block), well


def solution(mesh):
    cells, parts = P("grp", "sub", None), P(None, "grp", "sub", None)
    listed = P(("grp", "sub"))
    row = P(("grp", "sub"), None)
    in_specs = (
        (parts,) + (cells,) * 5 + (parts,) + (P(),) * 8
        + (listed, row, listed, listed, P("grp", None), row, row, listed, listed)
    )
    return jax.shard_map(
        per_device, mesh=mesh, in_specs=in_specs, out_specs=(parts, parts, row), check_vma=False
    )
```

```python
import functools
import math

import jax
import jax.numpy as jnp
from jax import lax
from jax.experimental import pallas as pl
from jax.experimental.pallas import tpu as pltpu
from jax.sharding import PartitionSpec as P

NEWT = 8
ROOT_TWO = math.sqrt(2.0)
LANES = 128
SUBLANES = 8
F32 = jnp.float32
BF16 = jnp.bfloat16
VMEM_LIMIT = 48 * 1024 * 1024
MARGIN = 8
WHOLE = (
    "coupling", "crit", "attract", "slope", "covol", "heat", "press", "loc", "member", "place",
    "flag", "visc", "trans", "inject", "seg", "strength", "own_press", "perm",
)


def iota(shape, dim):
    return lax.broadcasted_iota(jnp.int32, shape, dim)


def pieces_of(x, count):
    out = []
    for _ in range(count):
        piece = x.astype(BF16)
        out.append(piece)
        x = x - piece.astype(F32)
    return out


def mat(a, b):
    return lax.dot_general(a, b, (((1,), (0,)), ((), ())), preferred_element_type=F32)


def mat_nt(a, b):
    return lax.dot_general(a, b, (((1,), (1,)), ((), ())), preferred_element_type=F32)


def mat_hot(x, hot, count=3):
    return sum(mat(piece, hot) for piece in pieces_of(x, count))


def hot_mat_nt(hot, x, count=3):
    return sum(mat_nt(hot, piece) for piece in pieces_of(x, count))


def inverse(x):
    r = pl.reciprocal(x, approx=True)
    return r * (2.0 - x * r)


def hot(cond):
    return jnp.where(cond, 1.0, 0.0).astype(BF16)


def place_hots(loc, rows):
    n = loc.shape[1]
    row_hot = iota((rows, n), 0) == loc // LANES
    lane_hot = iota((LANES, n), 0) == loc % LANES
    return row_hot, lane_hot


def slot_hot_of(member, place):
    wells = place.shape[1]
    slot_of = hot(iota((wells, wells), 0) == wells - 1 - place)
    member_hot = hot(iota((wells, member.shape[1]), 0) == member)
    return mat(slot_of, member_hot)


def phase_kernel(
    nx,
    ny,
    axes,
    amount,
    *rest,
):
    sources, rest = rest[: len(WHOLE)], rest[len(WHOLE) :]
    (
        psi_v,
        terms_out,
        carried_out,
        mob_out,
        edge_x_out,
        edge_ya_out,
        edge_yb_out,
        part_out,
        pcell_out,
        consts_out,
    ) = rest[:10]
    targets, rest = rest[10 : 10 + len(WHOLE)], rest[10 + len(WHOLE) :]
    amount_v, split_v, field_v, table_v, small_sems, in_sems = rest
    nc = amount.shape[0]
    per = 2
    chunks = nx // per
    half = chunks // 2
    rows = per * ny

    def go(source, target, sem):
        copy = pltpu.make_async_copy(source, target, sem)
        copy.start()
        return copy

    loads, copies = [], {}
    for k, name in enumerate(WHOLE):
        if name in ("press", "flag"):
            span = pl.ds(len(loads) * half * rows, half * rows)
            loads.append(go(amount.at[:, span], amount_v.at[:, span], in_sems.at[len(loads)]))
        copies[name] = go(sources[k], targets[k], small_sems.at[k])

    def arrived(*names):
        return [targets[WHOLE.index(name)] for name in names]

    for copy in [*copies.values(), *loads]:
        copy.wait()

    size = nc * ny
    spread = hot(iota((size, nc), 0) // ny == iota((size, nc), 1))
    same_row = iota((size, size), 0) % ny == iota((size, size), 1) % ny
    mixers = []
    (coupling,) = arrived("coupling")
    for piece in pieces_of(1.0 - coupling[...], 2):
        wide = mat(spread, piece).astype(BF16)
        mixers.append(jnp.where(same_row, mat_nt(wide, spread), 0.0).astype(BF16))
    mixer = jnp.concatenate([mixers[0], mixers[0], mixers[1]], axis=1)

    crit, attract, slope, covol = arrived("crit", "attract", "slope", "covol")
    for i in range(nc):
        root = jnp.sqrt(jnp.full((SUBLANES, LANES), attract[i], F32))
        kappa = jnp.full((SUBLANES, LANES), slope[i], F32)
        tc = jnp.full((SUBLANES, LANES), crit[i], F32)
        table_v[0, i] = root * (1.0 + kappa)
        table_v[1, i] = root * kappa / jnp.sqrt(tc)
        table_v[2, i] = jnp.full((SUBLANES, LANES), covol[i], F32)

    press, loc, member, place = arrived("press", "loc", "member", "place")
    row_hot, lane_hot = place_hots(loc[...], nx * ny)
    lane_hot = hot(lane_hot)

    def cells_of(field, count):
        found = mat_hot(field, lane_hot, count)
        return jnp.sum(jnp.where(row_hot, found, 0.0), axis=0, keepdims=True)

    p_cell = cells_of(press[...], 3)
    pcell_out[...] = p_cell
    slot_hot = slot_hot_of(member[...], place[...]).astype(BF16)
    (heat,) = arrived("heat")

    shape3 = (ny // SUBLANES, SUBLANES, LANES)
    root_t = [jnp.sqrt(heat[pl.ds(x * ny, ny)].reshape(shape3)) for x in range(nx)]
    for x in range(nx):
        span, lanes = pl.ds(x * ny, ny), pl.ds(x * LANES, LANES)
        total = jnp.zeros(shape3, F32)
        volume = jnp.zeros(shape3, F32)
        for i in range(nc):
            o = amount_v[i, span].reshape(shape3)
            v = jnp.abs(table_v[0, i] - table_v[1, i] * root_t[x]) * o
            total += o
            volume += table_v[2, i] * o
            high, low = pieces_of(v.reshape(ny, LANES), 2)
            split_v[pl.ds(i * ny, ny), lanes] = high
            split_v[pl.ds(size + i * ny, ny), lanes] = low
            split_v[pl.ds(2 * size + i * ny, ny), lanes] = high
        field_v[0, span] = total.reshape(ny, LANES)
        field_v[1, span] = volume.reshape(ny, LANES)
    for c in range(chunks):
        mixed = mat(mixer, split_v[:, pl.ds(c * per * LANES, per * LANES)])
        for k in range(per):
            x = c * per + k
            span = pl.ds(x * ny, ny)
            total = jnp.zeros(shape3, F32)
            for i in range(nc):
                m = mixed[i * ny : (i + 1) * ny, k * LANES : (k + 1) * LANES].reshape(shape3)
                psi = jnp.abs(table_v[0, i] - table_v[1, i] * root_t[x]) * m
                total += amount_v[i, span].reshape(shape3) * psi
                psi_v[i, span] = psi.reshape(ny, LANES)
            field_v[2, span] = total.reshape(ny, LANES)

    flag, visc, trans, inject = arrived("flag", "visc", "trans", "inject")
    states = []
    for h in range(2):
        span = pl.ds(h * half * rows, half * rows)
        p, t = press[span], heat[span]
        liquid = flag[span] == 1
        r = inverse(field_v[0, span])
        rt = inverse(t)
        ratio_pt = p * rt
        beta = field_v[1, span] * r
        gr = ratio_pt * rt * r
        big_a = gr * r * field_v[2, span]
        big_b = ratio_pt * beta
        z = jnp.where(liquid, big_b + 0.01, 1.0 + big_b)
        c1 = big_a - 3.0 * big_b * big_b - 2.0 * big_b
        c0 = big_b * big_b + big_b * big_b * big_b - big_a * big_b
        states.append([z, big_b, big_b + 0.01, big_b - 1.0, c1, c0])
        field_v[1, span] = inverse(beta)
        field_v[3, span] = r
        terms_out[0, span] = ratio_pt
        terms_out[1, span] = 0.5 * big_a
        terms_out[2, span] = gr
    for _ in range(NEWT):
        for state in states:
            z, _, floor, c2, c1, c0 = state
            near = z + c2
            value = (near * z + c1) * z + c0
            incline = (near + near + z) * z + c1
            state[0] = jnp.maximum(z - value * inverse(jnp.maximum(incline, 0.1)), floor)
    for h, (z, big_b, *_) in enumerate(states):
        span = pl.ds(h * half * rows, half * rows)
        ratio_pt, gr = terms_out[0, span], terms_out[2, span]
        log_ratio = jnp.log(
            (z + (1.0 + ROOT_TWO) * big_b) * inverse(z + (1.0 - ROOT_TWO) * big_b)
        )
        lb = log_ratio * inverse(ROOT_TWO * big_b)
        mob = ratio_pt * inverse(z * jnp.where(flag[span] == 1, visc[1], visc[0]))
        mob_out[span] = mob
        field_v[3, span] = mob * field_v[3, span]
        terms_out[0, span] = jnp.log(z - big_b)
        terms_out[1, span] = (z - 1.0 + terms_out[1, span] * lb) * field_v[1, span]
        terms_out[2, span] = gr * lb
    for x in range(nx):
        span = pl.ds(x * ny, ny)
        mr = field_v[3, span]
        for i in range(nc):
            carried_out[i, pl.ds(MARGIN + x * ny, ny)] = mr * amount_v[i, span]

    total = sum(inject[i] for i in range(nc))
    share = 1.0 / jnp.full((1, LANES), total, F32)
    numbers = [trans[0], trans[1], trans[2], visc[0], visc[1]]
    for i in range(nc):
        consts_out[pl.ds(i, 1)] = inject[i] * share
        consts_out[pl.ds(nc + 8 + i, 1)] = jnp.full((1, LANES), covol[i], F32)
    for i, number in enumerate(numbers):
        consts_out[pl.ds(nc + i, 1)] = jnp.full((1, LANES), number, F32)

    seg, strength, own_press, perm = arrived("seg", "strength", "own_press", "perm")
    weight = strength[...] * cells_of(mob_out[...], 2)
    segments = own_press.shape[1]
    place_of = iota((LANES, loc.shape[1]), 0)
    sums = jnp.where(place_of == seg[...], weight, 0.0)
    sums += jnp.where(place_of == seg[...] + segments, weight * (p_cell - 1.0), 0.0)
    shift = hot(iota((segments, LANES), 0) + 2 * segments == iota((segments, LANES), 1))
    part_out[...] = hot_mat_nt(slot_hot, sums, 2) + mat_hot(own_press[...], shift)

    odd_g = lax.axis_index(axes[0]) % 2 == 1
    odd_s = lax.axis_index(axes[1]) % 2 == 1
    for k in range(edge_x_out.shape[0]):
        at_low = odd_g if k == 0 else jnp.logical_not(odd_g)
        start = pl.multiple_of(jnp.where(at_low, 0, (nx - 1) * ny), ny)
        for i in range(nc):
            edge_x_out[k, i] = carried_out[i, pl.ds(start + MARGIN, ny)]
        edge_x_out[k, nc] = press[pl.ds(start, ny)]
        edge_x_out[k, nc + 1] = perm[pl.ds(start, ny)]
    for i in range(nc + 2):
        source = carried_out.at[i] if i < nc else press if i == nc else perm
        skip = MARGIN if i < nc else 0
        low = source[pl.ds(skip, nx, stride=ny)]
        high = source[pl.ds(skip + ny - 1, nx, stride=ny)]
        edge_ya_out[i] = jnp.where(odd_s, low, high)
        edge_yb_out[i] = jnp.where(odd_s, high, low)


def flux_kernel(
    nx,
    ny,
    axes,
    many_x,
    psi,
    terms,
    consts,
    carried,
    press,
    perm,
    pore,
    flag,
    old_in,
    edge_ya,
    edge_yb,
    *rest,
):
    edge_x, rest = rest[:many_x], rest[many_x:]
    lnphi_out, res_out, old, y_v, lnphi_v, in_sems, out_sems = rest
    nc = psi.shape[0]
    half = nx * ny // 2
    loads, stores = [], []
    for k in range(2):
        span = pl.ds(k * half, half)
        copy = pltpu.make_async_copy(old_in.at[:, span], old.at[:, span], in_sems.at[k])
        copy.start()
        loads.append(copy)

    def const(k):
        return jnp.broadcast_to(consts[pl.ds(k, 1)], (ny, LANES))

    for part in range(2):
        for x in range(part * nx // 2, (part + 1) * nx // 2):
            span = pl.ds(x * ny, ny)
            e0, e1, e2 = (terms[k, span] for k in range(3))
            for i in range(nc):
                value = const(nc + 8 + i) * e1 - e0 - psi[i, span] * e2
                lnphi_v[i, span] = value.astype(BF16)
        span = pl.ds(part * half, half)
        copy = pltpu.make_async_copy(
            lnphi_v.at[:, span], lnphi_out.at[:, span], out_sems.at[part]
        )
        copy.start()
        stores.append(copy)

    g, s = lax.axis_index(axes[0]), lax.axis_index(axes[1])
    ng, ns = lax.axis_size(axes[0]), lax.axis_size(axes[1])
    odd_g, odd_s = g % 2 == 1, s % 2 == 1
    has_low_y, has_high_y = s > 0, s < ns - 1
    has_low_x, has_high_x = g > 0, g < ng - 1

    for i in range(nc + 2):
        a, b = edge_ya[i], edge_yb[i]
        low, high = jnp.where(odd_s, a, b), jnp.where(odd_s, b, a)
        if i == nc + 1:
            low, high = jnp.where(has_low_y, low, 0.0), jnp.where(has_high_y, high, 0.0)
        y_v[0, i] = low
        y_v[1, i] = high

    def side_x(i, high):
        if many_x == 1:
            return edge_x[0][i]
        return jnp.where(odd_g != high, edge_x[0][i], edge_x[1][i])

    lane = iota((ny, LANES), 1)
    row = iota((ny, LANES), 0)
    first, final = row == 0, row == ny - 1
    factors = [const(nc + axis) for axis in range(3)]
    thin, thick = const(nc + 3), const(nc + 4)
    for x in range(nx):
        if x * 2 % nx == 0:
            loads[x * 2 // nx].wait()
        rows = pl.ds(x * ny, ny)
        p_a, k_a = press[rows], perm[rows]
        twice_k = 2.0 * k_a

        def face(p_b, k_b, axis):
            t = factors[axis] * (twice_k * k_b) * inverse(k_a + k_b)
            flow = t * (p_a - p_b)
            return jnp.maximum(flow, 0.0), jnp.minimum(flow, 0.0)

        def other_x(field, i, high):
            at = x + 1 if high else x - 1
            return field[pl.ds(at * ny, ny)] if 0 <= at < nx else side_x(i, high)

        def other_y(field, i, high):
            if high:
                return jnp.where(final, y_v[1, i, pl.ds(x, 1)], pltpu.roll(field, ny - 1, 0))
            return jnp.where(first, y_v[0, i, pl.ds(x, 1)], pltpu.roll(field, 1, 0))

        centre = pore[rows] * jnp.where(flag[rows] == 1, thick, thin)
        ins = []
        for high in (True, False):
            p_b, k_b = other_x(press, nc, high), other_x(perm, nc + 1, high)
            if x == nx - 1 and high:
                k_b = jnp.where(has_high_x, k_b, 0.0)
            if x == 0 and not high:
                k_b = jnp.where(has_low_x, k_b, 0.0)
            ins.append(face(p_b, k_b, 0))
        for high in (True, False):
            ins.append(face(other_y(p_a, nc, high), other_y(k_a, nc + 1, high), 1))
        for shift, edge in ((LANES - 1, LANES - 1), (1, 0)):
            k_b = jnp.where(lane == edge, 0.0, pltpu.roll(k_a, shift, 1))
            ins.append(face(pltpu.roll(p_a, shift, 1), k_b, 2))
        for out, _ in ins:
            centre += out
        ins = [into for _, into in ins]
        for i in range(nc):
            base = MARGIN + x * ny
            c = carried[i, pl.ds(base, ny)]
            value = centre * c - old[i, rows]
            for k, high in ((0, True), (1, False)):
                at = x + 1 if high else x - 1
                inside = 0 <= at < nx
                c_b = carried[i, pl.ds(MARGIN + at * ny, ny)] if inside else side_x(i, high)
                value += ins[k] * c_b
            up, down = carried[i, pl.ds(base + 1, ny)], carried[i, pl.ds(base - 1, ny)]
            value += ins[2] * jnp.where(final, y_v[1, i, pl.ds(x, 1)], up)
            value += ins[3] * jnp.where(first, y_v[0, i, pl.ds(x, 1)], down)
            value += ins[4] * pltpu.roll(c, LANES - 1, 1)
            value += ins[5] * pltpu.roll(c, 1, 1)
            res_out[i, rows] = value
    for copy in stores:
        copy.wait()


def well_kernel(
    nx,
    ny,
    axes,
    res,
    carried,
    mob,
    well_rows,
    loc,
    member,
    seg,
    strength,
    place,
    pcell,
    consts,
    own_press,
    order,
    exit_press,
    friction,
    resid_out,
    well_out,
    res_v,
    out_sems,
):
    nc = res.shape[0]
    s = lax.axis_index(axes[1])
    row_hot, lane_hot = place_hots(loc[...], nx * ny)
    slot_hot = slot_hot_of(member[...], place[...])
    segments = own_press.shape[1]
    gathered = well_rows[...]
    seg_hot = hot(iota((LANES, loc.shape[1]), 0) == seg[...] + 2 * segments)
    p_seg = jnp.sum(mat_hot(gathered, seg_hot) * slot_hot, axis=0, keepdims=True)
    push = strength[...] * (pcell[...] - p_seg)
    flows = jnp.concatenate(
        [
            jnp.where(lane_hot, jnp.maximum(push, 0.0), 0.0),
            jnp.where(lane_hot, jnp.minimum(push, 0.0), 0.0),
        ],
        axis=0,
    )
    spread = hot_mat_nt(hot(row_hot), flows, 2)
    stores = []
    for x in range(nx):
        rows = pl.ds(x * ny, ny)
        out = spread[x * ny : (x + 1) * ny, :LANES]
        pushed = mob[rows] * spread[x * ny : (x + 1) * ny, LANES:]
        for i in range(nc):
            c = carried[i, pl.ds(MARGIN + x * ny, ny)]
            share = jnp.broadcast_to(consts[pl.ds(i, 1)], (ny, LANES))
            res_v[i, rows] = res[i, rows] + out * c + share * pushed
        if x % 2 == 1:
            span = pl.ds((x - 1) * ny, 2 * ny)
            copy = pltpu.make_async_copy(
                res_v.at[:, span], resid_out.at[:, span], out_sems.at[x // 2]
            )
            copy.start()
            stores.append(copy)

    own = jnp.sum(gathered, axis=0, keepdims=True)
    well_p = own_press[...]
    rate = own[:, segments : 2 * segments] - (well_p - 1.0) * own[:, :segments]
    order_hot = hot(iota((segments, segments), 0) == order[...])
    both = mat_hot(jnp.concatenate([rate, well_p], axis=0), order_hot)
    upper = hot(iota((segments, segments), 0) <= iota((segments, segments), 1))
    running = mat_hot(both[0:1], upper)
    press_ord = both[1:2]
    after = hot(iota((segments, segments), 0) == iota((segments, segments), 1) + 1)
    last = iota((1, segments), 1) == segments - 1
    nexts = jnp.where(last, exit_press[0], mat_hot(press_ord, after))
    res_ord = press_ord - nexts - friction[0] * running * jnp.abs(running)
    well_out[...] = sum(mat_nt(piece, order_hot) for piece in pieces_of(res_ord, 3))
    for copy in stores:
        copy.wait()


def swaps_of(count, other):
    pairs = [(i, i + 1) for i in range(1 if other else 0, count - 1, 2)]
    return pairs + [(b, a) for a, b in pairs]


def other_swaps_of(groups, count):
    swaps = [(g * count + a, g * count + b) for g in range(groups) for a, b in swaps_of(count, True)]
    ends = [(g * count + e, (g ^ 1) * count + e) for g in range(groups) for e in (0, count - 1)]
    return sorted(swaps + ends)


def per_device(
    amount,
    press,
    heat,
    flag,
    perm,
    pore,
    old,
    trans,
    visc,
    crit,
    attract,
    covol,
    slope,
    coupling,
    inject,
    locale,
    member,
    seg,
    strength,
    place,
    order,
    seg_press,
    exit_press,
    friction,
):
    axes = ("grp", "sub")
    nc, nx, ny, nz = amount.shape
    ng, ns = lax.axis_size("grp"), lax.axis_size("sub")
    rows = nx * ny
    perfs = locale.shape[0]
    wells, segments = place.shape[1], seg_press.shape[1]
    flat = lambda a: a.reshape(a.shape[:-3] + (rows, nz))
    line = lambda a: a.reshape(1, perfs)
    vm = pl.BlockSpec(memory_space=pltpu.VMEM)
    sm = pl.BlockSpec(memory_space=pltpu.SMEM)
    hbm = pl.BlockSpec(memory_space=pltpu.HBM)
    many_x = 1 if ng == 2 else 2

    amount, old = flat(amount), flat(old)
    press, heat, flag, perm, pore = (flat(a) for a in (press, heat, flag, perm, pore))
    locale, member, seg, strength = (line(a) for a in (locale, member, seg, strength))

    sources = (
        coupling, crit, attract, slope, covol, heat, press, locale, member, place,
        flag, visc, trans, inject, seg, strength, seg_press, perm,
    )
    kept = [
        pltpu.SMEM(a.shape, a.dtype) if a.ndim == 1 else pltpu.VMEM(a.shape, a.dtype)
        for a in sources
    ]
    in_hbm = lambda a: pltpu.with_memory_space_constraint(a, pltpu.HBM)

    psi, terms, carried, mob, edge_x, edge_ya, edge_yb, part, pcell, consts = pl.pallas_call(
        functools.partial(phase_kernel, nx, ny, axes),
        out_shape=(
            jax.ShapeDtypeStruct((nc, rows, nz), F32),
            jax.ShapeDtypeStruct((3, rows, nz), F32),
            jax.ShapeDtypeStruct((nc, rows + 2 * MARGIN, nz), F32),
            jax.ShapeDtypeStruct((rows, nz), F32),
            jax.ShapeDtypeStruct((many_x, nc + 2, ny, nz), F32),
            jax.ShapeDtypeStruct((nc + 2, nx, nz), F32),
            jax.ShapeDtypeStruct((nc + 2, nx, nz), F32),
            jax.ShapeDtypeStruct((wells, LANES), F32),
            jax.ShapeDtypeStruct((1, perfs), F32),
            jax.ShapeDtypeStruct((2 * nc + 8, LANES), F32),
        ),
        in_specs=[hbm] * (1 + len(sources)),
        out_specs=(vm,) * 10,
        scratch_shapes=[
            *kept,
            pltpu.VMEM((nc, rows, nz), F32),
            pltpu.VMEM((3 * nc * ny, nx * nz), BF16),
            pltpu.VMEM((4, rows, nz), F32),
            pltpu.VMEM((3, nc, SUBLANES, LANES), F32),
            pltpu.SemaphoreType.DMA((len(sources),)),
            pltpu.SemaphoreType.DMA((2,)),
        ],
        compiler_params=pltpu.CompilerParams(vmem_limit_bytes=VMEM_LIMIT),
        name="phase",
    )(in_hbm(amount), *(in_hbm(a) for a in sources))

    got_x = [lax.ppermute(edge_x[k], "grp", swaps_of(ng, k == 1)) for k in range(many_x)]
    got_yb = lax.ppermute(edge_yb, axes, other_swaps_of(ng, ns))
    got_ya = lax.ppermute(edge_ya, "sub", swaps_of(ns, False))
    backward = [list(range(ns))[::-1]]
    well_rows = lax.all_to_all(
        part, "sub", split_axis=0, concat_axis=0, axis_index_groups=backward, tiled=True
    )

    lnphi, res = pl.pallas_call(
        functools.partial(flux_kernel, nx, ny, axes, many_x),
        out_shape=(
            jax.ShapeDtypeStruct((nc, rows, nz), BF16),
            jax.ShapeDtypeStruct((nc, rows, nz), F32),
        ),
        in_specs=[vm] * 8 + [hbm] + [vm] * (2 + many_x),
        out_specs=(hbm, vm),
        scratch_shapes=[
            pltpu.VMEM((nc, rows, nz), F32),
            pltpu.VMEM((2, nc + 2, nx, nz), F32),
            pltpu.VMEM((nc, rows, nz), BF16),
            pltpu.SemaphoreType.DMA((2,)),
            pltpu.SemaphoreType.DMA((2,)),
        ],
        compiler_params=pltpu.CompilerParams(vmem_limit_bytes=VMEM_LIMIT),
        cost_estimate=pl.CostEstimate(
            flops=32 * nc * rows * nz, bytes_accessed=64 * nc * rows * nz, transcendentals=0
        ),
        name="flux",
    )(
        psi, terms, consts, carried, press, perm, pore, flag, in_hbm(old), got_ya, got_yb, *got_x,
    )

    resid, well = pl.pallas_call(
        functools.partial(well_kernel, nx, ny, axes),
        out_shape=(
            jax.ShapeDtypeStruct((nc, rows, nz), F32),
            jax.ShapeDtypeStruct((1, segments), F32),
        ),
        in_specs=[vm] * 13 + [sm] * 2,
        out_specs=(hbm, vm),
        scratch_shapes=[
            pltpu.VMEM((nc, rows, nz), F32),
            pltpu.SemaphoreType.DMA((nx // 2,)),
        ],
        compiler_params=pltpu.CompilerParams(vmem_limit_bytes=VMEM_LIMIT),
        name="wells",
    )(
        res, carried, mob, well_rows, locale, member, seg, strength, place, pcell,
        consts, seg_press, order, exit_press, friction,
    )
    block = (nc, nx, ny, nz)
    return resid.reshape(block), lnphi.reshape(block), well


def solution(mesh):
    cells, parts = P("grp", "sub", None), P(None, "grp", "sub", None)
    listed = P(("grp", "sub"))
    row = P(("grp", "sub"), None)
    in_specs = (
        (parts,) + (cells,) * 5 + (parts,) + (P(),) * 8
        + (listed, row, listed, listed, P("grp", None), row, row, listed, listed)
    )
    return jax.shard_map(
        per_device, mesh=mesh, in_specs=in_specs, out_specs=(parts, parts, row), check_vma=False
    )
```

```python
import functools
import math

import jax
import jax.numpy as jnp
from jax import lax
from jax.experimental import pallas as pl
from jax.experimental.pallas import tpu as pltpu
from jax.sharding import PartitionSpec as P

NEWT = 8
ROOT_TWO = math.sqrt(2.0)
LANES = 128
SUBLANES = 8
F32 = jnp.float32
BF16 = jnp.bfloat16
VMEM_LIMIT = 48 * 1024 * 1024
MARGIN = 8
WHOLE = (
    "coupling", "crit", "attract", "slope", "covol", "heat", "press", "loc", "member", "place",
    "flag", "visc", "trans", "inject", "seg", "strength", "own_press", "perm",
)


def iota(shape, dim):
    return lax.broadcasted_iota(jnp.int32, shape, dim)


def pieces_of(x, count):
    out = []
    for _ in range(count):
        piece = x.astype(BF16)
        out.append(piece)
        x = x - piece.astype(F32)
    return out


def mat(a, b):
    return lax.dot_general(a, b, (((1,), (0,)), ((), ())), preferred_element_type=F32)


def mat_nt(a, b):
    return lax.dot_general(a, b, (((1,), (1,)), ((), ())), preferred_element_type=F32)


def mat_hot(x, hot, count=3):
    return sum(mat(piece, hot) for piece in pieces_of(x, count))


def hot_mat_nt(hot, x, count=3):
    return sum(mat_nt(hot, piece) for piece in pieces_of(x, count))


def inverse(x):
    r = pl.reciprocal(x, approx=True)
    return r * (2.0 - x * r)


def hot(cond):
    return jnp.where(cond, 1.0, 0.0).astype(BF16)


def place_hots(loc, rows):
    n = loc.shape[1]
    row_hot = iota((rows, n), 0) == loc // LANES
    lane_hot = iota((LANES, n), 0) == loc % LANES
    return row_hot, lane_hot


def slot_hot_of(member, place, own):
    wells = place.shape[1]
    half = wells // 2
    row = iota((wells, wells), 0)
    parity = jnp.where(row < half, own % 2, 1 - own % 2)
    slot_of = hot(wells - 2 - 2 * (row % half) + parity == place)
    member_hot = hot(iota((wells, member.shape[1]), 0) == member)
    return mat(slot_of, member_hot)


def phase_kernel(
    nx,
    ny,
    axes,
    amount,
    *rest,
):
    sources, rest = rest[: len(WHOLE)], rest[len(WHOLE) :]
    (
        lnphi_out,
        carried_out,
        mob_out,
        edge_x_out,
        edge_ya_out,
        edge_yb_out,
        part_out,
        pcell_out,
        consts_out,
    ) = rest[:9]
    targets, rest = rest[9 : 9 + len(WHOLE)], rest[9 + len(WHOLE) :]
    amount_v, split_v, psi_v, lnphi_v, field_v, terms_v, table_v, small_sems, in_sems, out_sems = rest
    nc = amount.shape[0]
    per = 2
    chunks = nx // per
    half = chunks // 2
    rows = per * ny

    def go(source, target, sem):
        copy = pltpu.make_async_copy(source, target, sem)
        copy.start()
        return copy

    loads, copies = [], {}
    for k, name in enumerate(WHOLE):
        if name in ("press", "flag"):
            span = pl.ds(len(loads) * half * rows, half * rows)
            loads.append(go(amount.at[:, span], amount_v.at[:, span], in_sems.at[len(loads)]))
        copies[name] = go(sources[k], targets[k], small_sems.at[k])

    def arrived(*names):
        return [targets[WHOLE.index(name)] for name in names]

    for copy in [*copies.values(), *loads]:
        copy.wait()

    size = nc * ny
    spread = hot(iota((size, nc), 0) // ny == iota((size, nc), 1))
    same_row = iota((size, size), 0) % ny == iota((size, size), 1) % ny
    mixers = []
    (coupling,) = arrived("coupling")
    for piece in pieces_of(1.0 - coupling[...], 2):
        wide = mat(spread, piece).astype(BF16)
        mixers.append(jnp.where(same_row, mat_nt(wide, spread), 0.0).astype(BF16))
    mixer = jnp.concatenate([mixers[0], mixers[0], mixers[1]], axis=1)

    crit, attract, slope, covol = arrived("crit", "attract", "slope", "covol")
    for i in range(nc):
        root = jnp.sqrt(jnp.full((SUBLANES, LANES), attract[i], F32))
        kappa = jnp.full((SUBLANES, LANES), slope[i], F32)
        tc = jnp.full((SUBLANES, LANES), crit[i], F32)
        table_v[0, i] = root * (1.0 + kappa)
        table_v[1, i] = root * kappa / jnp.sqrt(tc)
        table_v[2, i] = jnp.full((SUBLANES, LANES), covol[i], F32)

    press, loc, member, place = arrived("press", "loc", "member", "place")
    row_hot, lane_hot = place_hots(loc[...], nx * ny)
    lane_hot = hot(lane_hot)

    def cells_of(field, count):
        found = mat_hot(field, lane_hot, count)
        return jnp.sum(jnp.where(row_hot, found, 0.0), axis=0, keepdims=True)

    p_cell = cells_of(press[...], 3)
    pcell_out[...] = p_cell
    own_slot = lax.axis_index(axes[1])
    slot_hot = slot_hot_of(member[...], place[...], own_slot).astype(BF16)
    (heat,) = arrived("heat")

    shape3 = (ny // SUBLANES, SUBLANES, LANES)
    root_t = [jnp.sqrt(heat[pl.ds(x * ny, ny)].reshape(shape3)) for x in range(nx)]
    for x in range(nx):
        span, lanes = pl.ds(x * ny, ny), pl.ds(x * LANES, LANES)
        total = jnp.zeros(shape3, F32)
        volume = jnp.zeros(shape3, F32)
        for i in range(nc):
            o = amount_v[i, span].reshape(shape3)
            v = jnp.abs(table_v[0, i] - table_v[1, i] * root_t[x]) * o
            total += o
            volume += table_v[2, i] * o
            high, low = pieces_of(v.reshape(ny, LANES), 2)
            split_v[pl.ds(i * ny, ny), lanes] = high
            split_v[pl.ds(size + i * ny, ny), lanes] = low
            split_v[pl.ds(2 * size + i * ny, ny), lanes] = high
        field_v[0, span] = total.reshape(ny, LANES)
        field_v[1, span] = volume.reshape(ny, LANES)
    for c in range(chunks):
        mixed = mat(mixer, split_v[:, pl.ds(c * per * LANES, per * LANES)])
        for k in range(per):
            x = c * per + k
            span = pl.ds(x * ny, ny)
            total = jnp.zeros(shape3, F32)
            for i in range(nc):
                m = mixed[i * ny : (i + 1) * ny, k * LANES : (k + 1) * LANES].reshape(shape3)
                psi = jnp.abs(table_v[0, i] - table_v[1, i] * root_t[x]) * m
                total += amount_v[i, span].reshape(shape3) * psi
                psi_v[i, span] = psi.reshape(ny, LANES)
            field_v[2, span] = total.reshape(ny, LANES)

    flag, visc, trans, inject = arrived("flag", "visc", "trans", "inject")
    states = []
    for h in range(2):
        span = pl.ds(h * half * rows, half * rows)
        p, t = press[span], heat[span]
        liquid = flag[span] == 1
        r = inverse(field_v[0, span])
        rt = inverse(t)
        ratio_pt = p * rt
        beta = field_v[1, span] * r
        gr = ratio_pt * rt * r
        big_a = gr * r * field_v[2, span]
        big_b = ratio_pt * beta
        z = jnp.where(liquid, big_b + 0.01, 1.0 + big_b)
        c1 = big_a - 3.0 * big_b * big_b - 2.0 * big_b
        c0 = big_b * big_b + big_b * big_b * big_b - big_a * big_b
        states.append([z, big_b, big_b + 0.01, big_b - 1.0, c1, c0])
        field_v[1, span] = inverse(beta)
        field_v[3, span] = r
        terms_v[0, span] = ratio_pt
        terms_v[1, span] = 0.5 * big_a
        terms_v[2, span] = gr
    for _ in range(NEWT):
        for state in states:
            z, _, floor, c2, c1, c0 = state
            near = z + c2
            value = (near * z + c1) * z + c0
            incline = (near + near + z) * z + c1
            state[0] = jnp.maximum(z - value * inverse(jnp.maximum(incline, 0.1)), floor)
    for h, (z, big_b, *_) in enumerate(states):
        span = pl.ds(h * half * rows, half * rows)
        ratio_pt, gr = terms_v[0, span], terms_v[2, span]
        log_ratio = jnp.log(
            (z + (1.0 + ROOT_TWO) * big_b) * inverse(z + (1.0 - ROOT_TWO) * big_b)
        )
        lb = log_ratio * inverse(ROOT_TWO * big_b)
        mob = ratio_pt * inverse(z * jnp.where(flag[span] == 1, visc[1], visc[0]))
        mob_out[span] = mob
        field_v[3, span] = mob * field_v[3, span]
        terms_v[0, span] = jnp.log(z - big_b)
        terms_v[1, span] = (z - 1.0 + terms_v[1, span] * lb) * field_v[1, span]
        terms_v[2, span] = gr * lb
    stores = []
    for x in range(nx):
        span = pl.ds(x * ny, ny)
        e0, e1, e2, mr = (
            a.reshape(shape3)
            for a in (terms_v[0, span], terms_v[1, span], terms_v[2, span], field_v[3, span])
        )
        for i in range(nc):
            value = table_v[2, i] * e1 - e0 - psi_v[i, span].reshape(shape3) * e2
            lnphi_v[i, span] = value.reshape(ny, LANES).astype(BF16)
            carried = (mr * amount_v[i, span].reshape(shape3)).reshape(ny, LANES)
            carried_out[i, pl.ds(MARGIN + x * ny, ny)] = carried
        if (x + 1) * 2 % nx == 0:
            span = pl.ds((x + 1 - nx // 2) * ny, nx // 2 * ny)
            stores.append(go(lnphi_v.at[:, span], lnphi_out.at[:, span], out_sems.at[len(stores)]))

    total = sum(inject[i] for i in range(nc))
    share = 1.0 / jnp.full((SUBLANES, LANES), total, F32)
    numbers = [trans[0], trans[1], trans[2], visc[0], visc[1]]
    for i in range(nc):
        consts_out[i] = inject[i] * share
    for i, number in enumerate(numbers):
        consts_out[nc + i] = jnp.full((SUBLANES, LANES), number, F32)

    seg, strength, own_press, perm = arrived("seg", "strength", "own_press", "perm")
    weight = strength[...] * cells_of(mob_out[...], 2)
    segments = own_press.shape[1]
    place_of = iota((LANES, loc.shape[1]), 0)
    sums = jnp.where(place_of == seg[...], weight, 0.0)
    sums += jnp.where(place_of == seg[...] + segments, weight * (p_cell - 1.0), 0.0)
    sums = hot_mat_nt(slot_hot, sums, 2)
    half = sums.shape[0] // 2
    for k in range(2):
        shift = hot(iota((segments, LANES), 0) + (2 + k) * segments == iota((segments, LANES), 1))
        with_press = sums[k * half : (k + 1) * half] + mat_hot(own_press[...], shift)
        if k == 0:
            part_out[...] = with_press
        else:
            edge_ya_out[pl.ds(nc + 2, half // nx)] = with_press.reshape(half // nx, nx, LANES)

    odd_g = lax.axis_index(axes[0]) % 2 == 1
    odd_s = own_slot % 2 == 1
    for k in range(edge_x_out.shape[0]):
        at_low = odd_g if k == 0 else jnp.logical_not(odd_g)
        start = pl.multiple_of(jnp.where(at_low, 0, (nx - 1) * ny), ny)
        for i in range(nc):
            edge_x_out[k, i] = carried_out[i, pl.ds(start + MARGIN, ny)]
        edge_x_out[k, nc] = press[pl.ds(start, ny)]
        edge_x_out[k, nc + 1] = perm[pl.ds(start, ny)]
    for i in range(nc + 2):
        source = carried_out.at[i] if i < nc else press if i == nc else perm
        skip = MARGIN if i < nc else 0
        low = source[pl.ds(skip, nx, stride=ny)]
        high = source[pl.ds(skip + ny - 1, nx, stride=ny)]
        edge_ya_out[i] = jnp.where(odd_s, low, high)
        edge_yb_out[i] = jnp.where(odd_s, high, low)
    for copy in stores:
        copy.wait()


def flux_kernel(
    nx,
    ny,
    axes,
    many_x,
    carried,
    press,
    perm,
    pore,
    flag,
    old,
    mob,
    edge_ya,
    edge_yb,
    well_rows,
    loc,
    member,
    seg,
    strength,
    place,
    pcell,
    consts,
    own_press,
    order,
    exit_press,
    friction,
    *rest,
):
    edge_x, rest = rest[:many_x], rest[many_x:]
    resid_out, well_out, y_v, res_v, out_sems = rest
    nc = carried.shape[0]
    g, s = lax.axis_index(axes[0]), lax.axis_index(axes[1])
    ng, ns = lax.axis_size(axes[0]), lax.axis_size(axes[1])
    odd_g, odd_s = g % 2 == 1, s % 2 == 1
    has_low_y, has_high_y = s > 0, s < ns - 1
    has_low_x, has_high_x = g > 0, g < ng - 1

    for i in range(nc + 2):
        a, b = edge_ya[i], edge_yb[i]
        low, high = jnp.where(odd_s, a, b), jnp.where(odd_s, b, a)
        if i == nc + 1:
            low, high = jnp.where(has_low_y, low, 0.0), jnp.where(has_high_y, high, 0.0)
        y_v[0, i] = low
        y_v[1, i] = high

    def side_x(i, high):
        if many_x == 1:
            return edge_x[0][i]
        return jnp.where(odd_g != high, edge_x[0][i], edge_x[1][i])

    row_hot, lane_hot = place_hots(loc[...], nx * ny)
    slot_hot = slot_hot_of(member[...], place[...], s)
    segments = own_press.shape[1]
    gathered = well_rows[...]
    found = [
        mat_hot(gathered, hot(iota((LANES, loc.shape[1]), 0) == seg[...] + (2 + k) * segments))
        for k in range(2)
    ]
    p_seg = jnp.sum(jnp.concatenate(found, axis=0) * slot_hot, axis=0, keepdims=True)
    push = strength[...] * (pcell[...] - p_seg)
    flows = jnp.concatenate(
        [
            jnp.where(lane_hot, jnp.maximum(push, 0.0), 0.0),
            jnp.where(lane_hot, jnp.minimum(push, 0.0), 0.0),
        ],
        axis=0,
    )
    spread = hot_mat_nt(hot(row_hot), flows, 2)

    own = jnp.sum(gathered, axis=0, keepdims=True)
    well_p = own_press[...]
    rate = own[:, segments : 2 * segments] - (well_p - 1.0) * own[:, :segments]
    order_hot = hot(iota((segments, segments), 0) == order[...])
    both = mat_hot(jnp.concatenate([rate, well_p], axis=0), order_hot)
    upper = hot(iota((segments, segments), 0) <= iota((segments, segments), 1))
    running = mat_hot(both[0:1], upper)
    press_ord = both[1:2]
    after = hot(iota((segments, segments), 0) == iota((segments, segments), 1) + 1)
    last = iota((1, segments), 1) == segments - 1
    nexts = jnp.where(last, exit_press[0], mat_hot(press_ord, after))
    res_ord = press_ord - nexts - friction[0] * running * jnp.abs(running)
    well_out[...] = sum(mat_nt(piece, order_hot) for piece in pieces_of(res_ord, 3))

    lane = iota((ny, LANES), 1)
    row = iota((ny, LANES), 0)
    first, final = row == 0, row == ny - 1

    def const(k):
        return jnp.concatenate([consts[k]] * (ny // SUBLANES), axis=0)

    stores = []
    for x in range(nx):
        rows = pl.ds(x * ny, ny)
        p_a, k_a = press[rows], perm[rows]
        twice_k = 2.0 * k_a

        def face(p_b, k_b, axis):
            t = const(nc + axis) * (twice_k * k_b) * inverse(k_a + k_b)
            flow = t * (p_a - p_b)
            return jnp.maximum(flow, 0.0), jnp.minimum(flow, 0.0)

        def other_x(field, i, high):
            at = x + 1 if high else x - 1
            return field[pl.ds(at * ny, ny)] if 0 <= at < nx else side_x(i, high)

        def other_y(field, i, high):
            if high:
                return jnp.where(final, y_v[1, i, pl.ds(x, 1)], pltpu.roll(field, ny - 1, 0))
            return jnp.where(first, y_v[0, i, pl.ds(x, 1)], pltpu.roll(field, 1, 0))

        centre = pore[rows] * jnp.where(flag[rows] == 1, const(nc + 4), const(nc + 3))
        centre += spread[x * ny : (x + 1) * ny, :LANES]
        ins = []
        for high in (True, False):
            p_b, k_b = other_x(press, nc, high), other_x(perm, nc + 1, high)
            if x == nx - 1 and high:
                k_b = jnp.where(has_high_x, k_b, 0.0)
            if x == 0 and not high:
                k_b = jnp.where(has_low_x, k_b, 0.0)
            ins.append(face(p_b, k_b, 0))
        for high in (True, False):
            ins.append(face(other_y(p_a, nc, high), other_y(k_a, nc + 1, high), 1))
        for shift, edge in ((LANES - 1, LANES - 1), (1, 0)):
            k_b = jnp.where(lane == edge, 0.0, pltpu.roll(k_a, shift, 1))
            ins.append(face(pltpu.roll(p_a, shift, 1), k_b, 2))
        for out, _ in ins:
            centre += out
        ins = [into for _, into in ins]
        pushed = mob[rows] * spread[x * ny : (x + 1) * ny, LANES:]
        for i in range(nc):
            base = MARGIN + x * ny
            c = carried[i, pl.ds(base, ny)]
            value = centre * c - old[i, rows] + const(i) * pushed
            for k, high in ((0, True), (1, False)):
                at = x + 1 if high else x - 1
                inside = 0 <= at < nx
                c_b = carried[i, pl.ds(MARGIN + at * ny, ny)] if inside else side_x(i, high)
                value += ins[k] * c_b
            up, down = carried[i, pl.ds(base + 1, ny)], carried[i, pl.ds(base - 1, ny)]
            value += ins[2] * jnp.where(final, y_v[1, i, pl.ds(x, 1)], up)
            value += ins[3] * jnp.where(first, y_v[0, i, pl.ds(x, 1)], down)
            value += ins[4] * pltpu.roll(c, LANES - 1, 1)
            value += ins[5] * pltpu.roll(c, 1, 1)
            res_v[i, rows] = value
        copy = pltpu.make_async_copy(res_v.at[:, rows], resid_out.at[:, rows], out_sems.at[x])
        copy.start()
        stores.append(copy)
    for copy in stores:
        copy.wait()


def swaps_of(count, other):
    pairs = [(i, i + 1) for i in range(1 if other else 0, count - 1, 2)]
    return pairs + [(b, a) for a, b in pairs]


def other_swaps_of(groups, count):
    swaps = [(g * count + a, g * count + b) for g in range(groups) for a, b in swaps_of(count, True)]
    ends = [(g * count + e, (g ^ 1) * count + e) for g in range(groups) for e in (0, count - 1)]
    return sorted(swaps + ends)


def per_device(
    amount,
    press,
    heat,
    flag,
    perm,
    pore,
    old,
    trans,
    visc,
    crit,
    attract,
    covol,
    slope,
    coupling,
    inject,
    locale,
    member,
    seg,
    strength,
    place,
    order,
    seg_press,
    exit_press,
    friction,
):
    axes = ("grp", "sub")
    nc, nx, ny, nz = amount.shape
    ng, ns = lax.axis_size("grp"), lax.axis_size("sub")
    rows = nx * ny
    perfs = locale.shape[0]
    wells, segments = place.shape[1], seg_press.shape[1]
    flat = lambda a: a.reshape(a.shape[:-3] + (rows, nz))
    line = lambda a: a.reshape(1, perfs)
    vm = pl.BlockSpec(memory_space=pltpu.VMEM)
    sm = pl.BlockSpec(memory_space=pltpu.SMEM)
    hbm = pl.BlockSpec(memory_space=pltpu.HBM)
    many_x = 1 if ng == 2 else 2

    amount, old = flat(amount), flat(old)
    press, heat, flag, perm, pore = (flat(a) for a in (press, heat, flag, perm, pore))
    locale, member, seg, strength = (line(a) for a in (locale, member, seg, strength))

    sources = (
        coupling, crit, attract, slope, covol, heat, press, locale, member, place,
        flag, visc, trans, inject, seg, strength, seg_press, perm,
    )
    kept = [
        pltpu.SMEM(a.shape, a.dtype) if a.ndim == 1 else pltpu.VMEM(a.shape, a.dtype)
        for a in sources
    ]
    in_hbm = lambda a: pltpu.with_memory_space_constraint(a, pltpu.HBM)

    lnphi, carried, mob, edge_x, edge_ya, edge_yb, part, pcell, consts = pl.pallas_call(
        functools.partial(phase_kernel, nx, ny, axes),
        out_shape=(
            jax.ShapeDtypeStruct((nc, rows, nz), BF16),
            jax.ShapeDtypeStruct((nc, rows + 2 * MARGIN, nz), F32),
            jax.ShapeDtypeStruct((rows, nz), F32),
            jax.ShapeDtypeStruct((many_x, nc + 2, ny, nz), F32),
            jax.ShapeDtypeStruct((nc + 2 + wells // 2 // nx, nx, nz), F32),
            jax.ShapeDtypeStruct((nc + 2, nx, nz), F32),
            jax.ShapeDtypeStruct((wells // 2, LANES), F32),
            jax.ShapeDtypeStruct((1, perfs), F32),
            jax.ShapeDtypeStruct((nc + 8, SUBLANES, LANES), F32),
        ),
        in_specs=[hbm] * (1 + len(sources)),
        out_specs=(hbm,) + (vm,) * 8,
        scratch_shapes=[
            *kept,
            pltpu.VMEM((nc, rows, nz), F32),
            pltpu.VMEM((3 * nc * ny, nx * nz), BF16),
            pltpu.VMEM((nc, rows, nz), F32),
            pltpu.VMEM((nc, rows, nz), BF16),
            pltpu.VMEM((4, rows, nz), F32),
            pltpu.VMEM((3, rows, nz), F32),
            pltpu.VMEM((3, nc, SUBLANES, LANES), F32),
            pltpu.SemaphoreType.DMA((len(sources),)),
            pltpu.SemaphoreType.DMA((2,)),
            pltpu.SemaphoreType.DMA((2,)),
        ],
        compiler_params=pltpu.CompilerParams(vmem_limit_bytes=VMEM_LIMIT),
        name="phase",
    )(in_hbm(amount), *(in_hbm(a) for a in sources))

    got_ya = lax.ppermute(edge_ya, "sub", swaps_of(ns, False))
    got_x = [lax.ppermute(edge_x[k], "grp", swaps_of(ng, k == 1)) for k in range(many_x)]
    got_yb = lax.ppermute(edge_yb, axes, other_swaps_of(ng, ns))
    part = part + got_ya[nc + 2 :].reshape(part.shape)
    same_parity = [list(range(ns - 1 - k, -1, -2)) for k in range(2)]
    well_rows = lax.all_to_all(
        part, "sub", split_axis=0, concat_axis=0, axis_index_groups=same_parity, tiled=True
    )

    resid, well = pl.pallas_call(
        functools.partial(flux_kernel, nx, ny, axes, many_x),
        out_shape=(
            jax.ShapeDtypeStruct((nc, rows, nz), F32),
            jax.ShapeDtypeStruct((1, segments), F32),
        ),
        in_specs=[vm] * 19 + [sm] * 2 + [vm] * many_x,
        out_specs=(hbm, vm),
        scratch_shapes=[
            pltpu.VMEM((2, nc + 2, nx, nz), F32),
            pltpu.VMEM((nc, rows, nz), F32),
            pltpu.SemaphoreType.DMA((nx,)),
        ],
        compiler_params=pltpu.CompilerParams(vmem_limit_bytes=VMEM_LIMIT),
        name="flux",
    )(
        carried, press, perm, pore, flag, old, mob, got_ya, got_yb, well_rows,
        locale, member, seg, strength, place, pcell,
        consts, seg_press, order, exit_press, friction, *got_x,
    )
    block = (nc, nx, ny, nz)
    return resid.reshape(block), lnphi.reshape(block), well


def solution(mesh):
    cells, parts = P("grp", "sub", None), P(None, "grp", "sub", None)
    listed = P(("grp", "sub"))
    row = P(("grp", "sub"), None)
    in_specs = (
        (parts,) + (cells,) * 5 + (parts,) + (P(),) * 8
        + (listed, row, listed, listed, P("grp", None), row, row, listed, listed)
    )
    return jax.shard_map(
        per_device, mesh=mesh, in_specs=in_specs, out_specs=(parts, parts, row), check_vma=False
    )
```

```python
import functools
import math

import jax
import jax.numpy as jnp
from jax import lax
from jax.experimental import pallas as pl
from jax.experimental.pallas import tpu as pltpu
from jax.sharding import PartitionSpec as P

NEWT = 8
ROOT_TWO = math.sqrt(2.0)
LANES = 128
SUBLANES = 8
F32 = jnp.float32
BF16 = jnp.bfloat16
VMEM_LIMIT = 48 * 1024 * 1024
MARGIN = 8
WHOLE = (
    "coupling", "crit", "attract", "slope", "covol", "heat", "press", "loc", "member", "place",
    "flag", "visc", "trans", "inject", "seg", "strength", "own_press", "perm",
)


def iota(shape, dim):
    return lax.broadcasted_iota(jnp.int32, shape, dim)


def pieces_of(x, count):
    out = []
    for _ in range(count):
        piece = x.astype(BF16)
        out.append(piece)
        x = x - piece.astype(F32)
    return out


def mat(a, b):
    return lax.dot_general(a, b, (((1,), (0,)), ((), ())), preferred_element_type=F32)


def mat_nt(a, b):
    return lax.dot_general(a, b, (((1,), (1,)), ((), ())), preferred_element_type=F32)


def mat_hot(x, hot, count=3):
    return sum(mat(piece, hot) for piece in pieces_of(x, count))


def inverse(x):
    r = pl.reciprocal(x, approx=True)
    return r * (2.0 - x * r)


def hot(cond):
    return jnp.where(cond, 1.0, 0.0).astype(BF16)


def place_hots(loc, rows):
    n = loc.shape[1]
    row_hot = iota((rows, n), 0) == loc // LANES
    lane_hot = iota((LANES, n), 0) == loc % LANES
    return row_hot, lane_hot


def slot_hot_of(member, place):
    wells = place.shape[1]
    slot_of = hot(iota((wells, wells), 0) == wells - 1 - place)
    member_hot = hot(iota((wells, member.shape[1]), 0) == member)
    return mat(slot_of, member_hot)


def phase_kernel(
    nx,
    ny,
    axes,
    amount,
    *rest,
):
    sources, rest = rest[: len(WHOLE)], rest[len(WHOLE) :]
    (
        lnphi_out,
        carried_out,
        mob_out,
        edge_x_out,
        edge_ya_out,
        edge_yb_out,
        part_out,
        pcell_out,
        consts_out,
    ) = rest[:9]
    targets, rest = rest[9 : 9 + len(WHOLE)], rest[9 + len(WHOLE) :]
    amount_v, split_v, psi_v, lnphi_v, field_v, terms_v, table_v, small_sems, in_sems, out_sems = rest
    nc = amount.shape[0]
    per = 2
    chunks = nx // per
    half = chunks // 2
    rows = per * ny

    def go(source, target, sem):
        copy = pltpu.make_async_copy(source, target, sem)
        copy.start()
        return copy

    loads, copies = [], {}
    for k, name in enumerate(WHOLE):
        if name in ("press", "flag"):
            span = pl.ds(len(loads) * half * rows, half * rows)
            loads.append(go(amount.at[:, span], amount_v.at[:, span], in_sems.at[len(loads)]))
        copies[name] = go(sources[k], targets[k], small_sems.at[k])

    def arrived(*names):
        return [targets[WHOLE.index(name)] for name in names]

    for copy in [*copies.values(), *loads]:
        copy.wait()

    size = nc * ny
    spread = hot(iota((size, nc), 0) // ny == iota((size, nc), 1))
    same_row = iota((size, size), 0) % ny == iota((size, size), 1) % ny
    mixers = []
    (coupling,) = arrived("coupling")
    for piece in pieces_of(1.0 - coupling[...], 2):
        wide = mat(spread, piece).astype(BF16)
        mixers.append(jnp.where(same_row, mat_nt(wide, spread), 0.0).astype(BF16))
    mixer = jnp.concatenate([mixers[0], mixers[0], mixers[1]], axis=1)

    crit, attract, slope, covol = arrived("crit", "attract", "slope", "covol")
    for i in range(nc):
        root = jnp.sqrt(jnp.full((SUBLANES, LANES), attract[i], F32))
        kappa = jnp.full((SUBLANES, LANES), slope[i], F32)
        tc = jnp.full((SUBLANES, LANES), crit[i], F32)
        table_v[0, i] = root * (1.0 + kappa)
        table_v[1, i] = root * kappa / jnp.sqrt(tc)
        table_v[2, i] = jnp.full((SUBLANES, LANES), covol[i], F32)

    press, loc, member, place = arrived("press", "loc", "member", "place")
    row_hot, lane_hot = place_hots(loc[...], nx * ny)
    lane_hot = hot(lane_hot)

    def cells_of(field, count):
        found = mat_hot(field, lane_hot, count)
        return jnp.sum(jnp.where(row_hot, found, 0.0), axis=0, keepdims=True)

    p_cell = cells_of(press[...], 3)
    pcell_out[...] = p_cell
    slot_hot = slot_hot_of(member[...], place[...])
    (heat,) = arrived("heat")

    shape3 = (ny // SUBLANES, SUBLANES, LANES)
    root_t = [jnp.sqrt(heat[pl.ds(x * ny, ny)].reshape(shape3)) for x in range(nx)]
    for x in range(nx):
        span, lanes = pl.ds(x * ny, ny), pl.ds(x * LANES, LANES)
        total = jnp.zeros(shape3, F32)
        volume = jnp.zeros(shape3, F32)
        for i in range(nc):
            o = amount_v[i, span].reshape(shape3)
            v = jnp.abs(table_v[0, i] - table_v[1, i] * root_t[x]) * o
            total += o
            volume += table_v[2, i] * o
            high, low = pieces_of(v.reshape(ny, LANES), 2)
            split_v[pl.ds(i * ny, ny), lanes] = high
            split_v[pl.ds(size + i * ny, ny), lanes] = low
            split_v[pl.ds(2 * size + i * ny, ny), lanes] = high
        field_v[0, span] = total.reshape(ny, LANES)
        field_v[1, span] = volume.reshape(ny, LANES)
    for c in range(chunks):
        mixed = mat(mixer, split_v[:, pl.ds(c * per * LANES, per * LANES)])
        for k in range(per):
            x = c * per + k
            span = pl.ds(x * ny, ny)
            total = jnp.zeros(shape3, F32)
            for i in range(nc):
                m = mixed[i * ny : (i + 1) * ny, k * LANES : (k + 1) * LANES].reshape(shape3)
                psi = jnp.abs(table_v[0, i] - table_v[1, i] * root_t[x]) * m
                total += amount_v[i, span].reshape(shape3) * psi
                psi_v[i, span] = psi.reshape(ny, LANES)
            field_v[2, span] = total.reshape(ny, LANES)

    flag, visc, trans, inject = arrived("flag", "visc", "trans", "inject")
    states = []
    for h in range(2):
        span = pl.ds(h * half * rows, half * rows)
        p, t = press[span], heat[span]
        liquid = flag[span] == 1
        r = inverse(field_v[0, span])
        rt = inverse(t)
        ratio_pt = p * rt
        beta = field_v[1, span] * r
        gr = ratio_pt * rt * r
        big_a = gr * r * field_v[2, span]
        big_b = ratio_pt * beta
        z = jnp.where(liquid, big_b + 0.01, 1.0 + big_b)
        c1 = big_a - 3.0 * big_b * big_b - 2.0 * big_b
        c0 = big_b * big_b + big_b * big_b * big_b - big_a * big_b
        states.append([z, big_b, big_b + 0.01, big_b - 1.0, c1, c0])
        field_v[1, span] = inverse(beta)
        field_v[3, span] = r
        terms_v[0, span] = ratio_pt
        terms_v[1, span] = 0.5 * big_a
        terms_v[2, span] = gr
    for _ in range(NEWT):
        for state in states:
            z, _, floor, c2, c1, c0 = state
            near = z + c2
            value = (near * z + c1) * z + c0
            incline = (near + near + z) * z + c1
            state[0] = jnp.maximum(z - value * inverse(jnp.maximum(incline, 0.1)), floor)
    for h, (z, big_b, *_) in enumerate(states):
        span = pl.ds(h * half * rows, half * rows)
        ratio_pt, gr = terms_v[0, span], terms_v[2, span]
        log_ratio = jnp.log(
            (z + (1.0 + ROOT_TWO) * big_b) * inverse(z + (1.0 - ROOT_TWO) * big_b)
        )
        lb = log_ratio * inverse(ROOT_TWO * big_b)
        mob = ratio_pt * inverse(z * jnp.where(flag[span] == 1, visc[1], visc[0]))
        mob_out[span] = mob
        field_v[3, span] = mob * field_v[3, span]
        terms_v[0, span] = jnp.log(z - big_b)
        terms_v[1, span] = (z - 1.0 + terms_v[1, span] * lb) * field_v[1, span]
        terms_v[2, span] = gr * lb
    stores = []
    for x in range(nx):
        span = pl.ds(x * ny, ny)
        e0, e1, e2 = (terms_v[k, span].reshape(shape3) for k in range(3))
        for i in range(nc):
            value = table_v[2, i] * e1 - e0 - psi_v[i, span].reshape(shape3) * e2
            lnphi_v[i, span] = value.reshape(ny, LANES).astype(BF16)
        if (x + 1) * 2 % nx == 0:
            span = pl.ds((x + 1 - nx // 2) * ny, nx // 2 * ny)
            stores.append(go(lnphi_v.at[:, span], lnphi_out.at[:, span], out_sems.at[len(stores)]))
    for x in range(nx):
        span = pl.ds(x * ny, ny)
        mr = field_v[3, span]
        for i in range(nc):
            carried_out[i, pl.ds(MARGIN + x * ny, ny)] = mr * amount_v[i, span]

    total = sum(inject[i] for i in range(nc))
    share = 1.0 / jnp.full((SUBLANES, LANES), total, F32)
    numbers = [trans[0], trans[1], trans[2], visc[0], visc[1]]
    for i in range(nc):
        consts_out[i] = inject[i] * share
    for i, number in enumerate(numbers):
        consts_out[nc + i] = jnp.full((SUBLANES, LANES), number, F32)

    seg, strength, own_press, perm = arrived("seg", "strength", "own_press", "perm")
    weight = strength[...] * cells_of(mob_out[...], 2)
    segments = own_press.shape[1]
    lanes = iota((LANES, loc.shape[1]), 0)
    shift = hot(iota((segments, LANES), 0) + 2 * segments == iota((segments, LANES), 1))
    sums = mat_hot(own_press[...], shift)
    for k, value in enumerate((weight, weight * (p_cell - 1.0))):
        seg_hot = hot(lanes == seg[...] + k * segments)
        for piece in pieces_of(slot_hot * value, 2):
            sums += mat_nt(piece, seg_hot)
    part_out[...] = sums

    odd_g = lax.axis_index(axes[0]) % 2 == 1
    odd_s = lax.axis_index(axes[1]) % 2 == 1
    for k in range(edge_x_out.shape[0]):
        at_low = odd_g if k == 0 else jnp.logical_not(odd_g)
        start = pl.multiple_of(jnp.where(at_low, 0, (nx - 1) * ny), ny)
        for i in range(nc):
            edge_x_out[k, i] = carried_out[i, pl.ds(start + MARGIN, ny)]
        edge_x_out[k, nc] = press[pl.ds(start, ny)]
        edge_x_out[k, nc + 1] = perm[pl.ds(start, ny)]
    for i in range(nc + 2):
        source = carried_out.at[i] if i < nc else press if i == nc else perm
        skip = MARGIN if i < nc else 0
        low = source[pl.ds(skip, nx, stride=ny)]
        high = source[pl.ds(skip + ny - 1, nx, stride=ny)]
        edge_ya_out[i] = jnp.where(odd_s, low, high)
        edge_yb_out[i] = jnp.where(odd_s, high, low)
    for copy in stores:
        copy.wait()


def flux_kernel(
    nx,
    ny,
    axes,
    many_x,
    carried,
    press,
    perm,
    pore,
    flag,
    old,
    mob,
    edge_ya,
    edge_yb,
    well_rows,
    loc,
    member,
    seg,
    strength,
    place,
    pcell,
    consts,
    own_press,
    order,
    exit_press,
    friction,
    *rest,
):
    edge_x, rest = rest[:many_x], rest[many_x:]
    resid_out, well_out, y_v, res_v, out_sems = rest
    nc = carried.shape[0]
    g, s = lax.axis_index(axes[0]), lax.axis_index(axes[1])
    ng, ns = lax.axis_size(axes[0]), lax.axis_size(axes[1])
    odd_g, odd_s = g % 2 == 1, s % 2 == 1
    has_low_y, has_high_y = s > 0, s < ns - 1
    has_low_x, has_high_x = g > 0, g < ng - 1

    for i in range(nc + 2):
        a, b = edge_ya[i], edge_yb[i]
        low, high = jnp.where(odd_s, a, b), jnp.where(odd_s, b, a)
        if i == nc + 1:
            low, high = jnp.where(has_low_y, low, 0.0), jnp.where(has_high_y, high, 0.0)
        y_v[0, i] = low
        y_v[1, i] = high

    def side_x(i, high):
        if many_x == 1:
            return edge_x[0][i]
        return jnp.where(odd_g != high, edge_x[0][i], edge_x[1][i])

    row_hot, lane_hot = place_hots(loc[...], nx * ny)
    slot_hot = slot_hot_of(member[...], place[...])
    segments = own_press.shape[1]
    gathered = well_rows[...]
    seg_hot = hot(iota((LANES, loc.shape[1]), 0) == seg[...] + 2 * segments)
    p_seg = jnp.sum(mat_hot(gathered, seg_hot) * slot_hot, axis=0, keepdims=True)
    push = strength[...] * (pcell[...] - p_seg)
    flows = jnp.concatenate(
        [
            jnp.where(row_hot, jnp.maximum(push, 0.0), 0.0),
            jnp.where(row_hot, jnp.minimum(push, 0.0), 0.0),
        ],
        axis=0,
    )
    lane_hot = hot(lane_hot)
    spread = sum(mat_nt(piece, lane_hot) for piece in pieces_of(flows, 2))

    own = jnp.sum(gathered, axis=0, keepdims=True)
    well_p = own_press[...]
    rate = own[:, segments : 2 * segments] - (well_p - 1.0) * own[:, :segments]
    order_hot = hot(iota((segments, segments), 0) == order[...])
    both = mat_hot(jnp.concatenate([rate, well_p], axis=0), order_hot)
    upper = hot(iota((segments, segments), 0) <= iota((segments, segments), 1))
    running = mat_hot(both[0:1], upper)
    press_ord = both[1:2]
    after = hot(iota((segments, segments), 0) == iota((segments, segments), 1) + 1)
    last = iota((1, segments), 1) == segments - 1
    nexts = jnp.where(last, exit_press[0], mat_hot(press_ord, after))
    res_ord = press_ord - nexts - friction[0] * running * jnp.abs(running)
    well_out[...] = sum(mat_nt(piece, order_hot) for piece in pieces_of(res_ord, 3))

    lane = iota((ny, LANES), 1)
    row = iota((ny, LANES), 0)
    first, final = row == 0, row == ny - 1

    def const(k):
        return jnp.concatenate([consts[k]] * (ny // SUBLANES), axis=0)

    stores = []
    for x in range(nx):
        rows = pl.ds(x * ny, ny)
        p_a, k_a = press[rows], perm[rows]
        twice_k = 2.0 * k_a

        def face(p_b, k_b, axis):
            t = const(nc + axis) * (twice_k * k_b) * inverse(k_a + k_b)
            flow = t * (p_a - p_b)
            return jnp.maximum(flow, 0.0), jnp.minimum(flow, 0.0)

        def other_x(field, i, high):
            at = x + 1 if high else x - 1
            return field[pl.ds(at * ny, ny)] if 0 <= at < nx else side_x(i, high)

        def other_y(field, i, high):
            if high:
                return jnp.where(final, y_v[1, i, pl.ds(x, 1)], pltpu.roll(field, ny - 1, 0))
            return jnp.where(first, y_v[0, i, pl.ds(x, 1)], pltpu.roll(field, 1, 0))

        centre = pore[rows] * jnp.where(flag[rows] == 1, const(nc + 4), const(nc + 3))
        centre += spread[x * ny : (x + 1) * ny]
        ins = []
        for high in (True, False):
            p_b, k_b = other_x(press, nc, high), other_x(perm, nc + 1, high)
            if x == nx - 1 and high:
                k_b = jnp.where(has_high_x, k_b, 0.0)
            if x == 0 and not high:
                k_b = jnp.where(has_low_x, k_b, 0.0)
            ins.append(face(p_b, k_b, 0))
        for high in (True, False):
            ins.append(face(other_y(p_a, nc, high), other_y(k_a, nc + 1, high), 1))
        for shift, edge in ((LANES - 1, LANES - 1), (1, 0)):
            k_b = jnp.where(lane == edge, 0.0, pltpu.roll(k_a, shift, 1))
            ins.append(face(pltpu.roll(p_a, shift, 1), k_b, 2))
        for out, _ in ins:
            centre += out
        ins = [into for _, into in ins]
        pushed = mob[rows] * spread[(nx + x) * ny : (nx + x + 1) * ny]
        for i in range(nc):
            base = MARGIN + x * ny
            c = carried[i, pl.ds(base, ny)]
            value = centre * c - old[i, rows] + const(i) * pushed
            for k, high in ((0, True), (1, False)):
                at = x + 1 if high else x - 1
                inside = 0 <= at < nx
                c_b = carried[i, pl.ds(MARGIN + at * ny, ny)] if inside else side_x(i, high)
                value += ins[k] * c_b
            up, down = carried[i, pl.ds(base + 1, ny)], carried[i, pl.ds(base - 1, ny)]
            value += ins[2] * jnp.where(final, y_v[1, i, pl.ds(x, 1)], up)
            value += ins[3] * jnp.where(first, y_v[0, i, pl.ds(x, 1)], down)
            value += ins[4] * pltpu.roll(c, LANES - 1, 1)
            value += ins[5] * pltpu.roll(c, 1, 1)
            res_v[i, rows] = value
        copy = pltpu.make_async_copy(res_v.at[:, rows], resid_out.at[:, rows], out_sems.at[x])
        copy.start()
        stores.append(copy)
    for copy in stores:
        copy.wait()


def swaps_of(count, other):
    pairs = [(i, i + 1) for i in range(1 if other else 0, count - 1, 2)]
    return pairs + [(b, a) for a, b in pairs]


def other_swaps_of(groups, count):
    swaps = [(g * count + a, g * count + b) for g in range(groups) for a, b in swaps_of(count, True)]
    ends = [(g * count + e, (g ^ 1) * count + e) for g in range(groups) for e in (0, count - 1)]
    return sorted(swaps + ends)


def per_device(
    amount,
    press,
    heat,
    flag,
    perm,
    pore,
    old,
    trans,
    visc,
    crit,
    attract,
    covol,
    slope,
    coupling,
    inject,
    locale,
    member,
    seg,
    strength,
    place,
    order,
    seg_press,
    exit_press,
    friction,
):
    axes = ("grp", "sub")
    nc, nx, ny, nz = amount.shape
    ng, ns = lax.axis_size("grp"), lax.axis_size("sub")
    rows = nx * ny
    perfs = locale.shape[0]
    wells, segments = place.shape[1], seg_press.shape[1]
    flat = lambda a: a.reshape(a.shape[:-3] + (rows, nz))
    line = lambda a: a.reshape(1, perfs)
    vm = pl.BlockSpec(memory_space=pltpu.VMEM)
    sm = pl.BlockSpec(memory_space=pltpu.SMEM)
    hbm = pl.BlockSpec(memory_space=pltpu.HBM)
    many_x = 1 if ng == 2 else 2

    amount, old = flat(amount), flat(old)
    press, heat, flag, perm, pore = (flat(a) for a in (press, heat, flag, perm, pore))
    locale, member, seg, strength = (line(a) for a in (locale, member, seg, strength))

    sources = (
        coupling, crit, attract, slope, covol, heat, press, locale, member, place,
        flag, visc, trans, inject, seg, strength, seg_press, perm,
    )
    kept = [
        pltpu.SMEM(a.shape, a.dtype) if a.ndim == 1 else pltpu.VMEM(a.shape, a.dtype)
        for a in sources
    ]
    in_hbm = lambda a: pltpu.with_memory_space_constraint(a, pltpu.HBM)

    lnphi, carried, mob, edge_x, edge_ya, edge_yb, part, pcell, consts = pl.pallas_call(
        functools.partial(phase_kernel, nx, ny, axes),
        out_shape=(
            jax.ShapeDtypeStruct((nc, rows, nz), BF16),
            jax.ShapeDtypeStruct((nc, rows + 2 * MARGIN, nz), F32),
            jax.ShapeDtypeStruct((rows, nz), F32),
            jax.ShapeDtypeStruct((many_x, nc + 2, ny, nz), F32),
            jax.ShapeDtypeStruct((nc + 2, nx, nz), F32),
            jax.ShapeDtypeStruct((nc + 2, nx, nz), F32),
            jax.ShapeDtypeStruct((wells, LANES), F32),
            jax.ShapeDtypeStruct((1, perfs), F32),
            jax.ShapeDtypeStruct((nc + 8, SUBLANES, LANES), F32),
        ),
        in_specs=[hbm] * (1 + len(sources)),
        out_specs=(hbm,) + (vm,) * 8,
        scratch_shapes=[
            *kept,
            pltpu.VMEM((nc, rows, nz), F32),
            pltpu.VMEM((3 * nc * ny, nx * nz), BF16),
            pltpu.VMEM((nc, rows, nz), F32),
            pltpu.VMEM((nc, rows, nz), BF16),
            pltpu.VMEM((4, rows, nz), F32),
            pltpu.VMEM((3, rows, nz), F32),
            pltpu.VMEM((3, nc, SUBLANES, LANES), F32),
            pltpu.SemaphoreType.DMA((len(sources),)),
            pltpu.SemaphoreType.DMA((2,)),
            pltpu.SemaphoreType.DMA((2,)),
        ],
        compiler_params=pltpu.CompilerParams(vmem_limit_bytes=VMEM_LIMIT),
        name="phase",
    )(in_hbm(amount), *(in_hbm(a) for a in sources))

    got_ya = lax.ppermute(edge_ya, "sub", swaps_of(ns, False))
    got_x = [lax.ppermute(edge_x[k], "grp", swaps_of(ng, k == 1)) for k in range(many_x)]
    got_yb = lax.ppermute(edge_yb, axes, other_swaps_of(ng, ns))
    backward = [list(range(ns))[::-1]]
    well_rows = lax.all_to_all(
        part, "sub", split_axis=0, concat_axis=0, axis_index_groups=backward, tiled=True
    )

    resid, well = pl.pallas_call(
        functools.partial(flux_kernel, nx, ny, axes, many_x),
        out_shape=(
            jax.ShapeDtypeStruct((nc, rows, nz), F32),
            jax.ShapeDtypeStruct((1, segments), F32),
        ),
        in_specs=[vm] * 19 + [sm] * 2 + [vm] * many_x,
        out_specs=(hbm, vm),
        scratch_shapes=[
            pltpu.VMEM((2, nc + 2, nx, nz), F32),
            pltpu.VMEM((nc, rows, nz), F32),
            pltpu.SemaphoreType.DMA((nx,)),
        ],
        compiler_params=pltpu.CompilerParams(vmem_limit_bytes=VMEM_LIMIT),
        name="flux",
    )(
        carried, press, perm, pore, flag, old, mob, got_ya, got_yb, well_rows,
        locale, member, seg, strength, place, pcell,
        consts, seg_press, order, exit_press, friction, *got_x,
    )
    block = (nc, nx, ny, nz)
    return resid.reshape(block), lnphi.reshape(block), well


def solution(mesh):
    cells, parts = P("grp", "sub", None), P(None, "grp", "sub", None)
    listed = P(("grp", "sub"))
    row = P(("grp", "sub"), None)
    in_specs = (
        (parts,) + (cells,) * 5 + (parts,) + (P(),) * 8
        + (listed, row, listed, listed, P("grp", None), row, row, listed, listed)
    )
    return jax.shard_map(
        per_device, mesh=mesh, in_specs=in_specs, out_specs=(parts, parts, row), check_vma=False
    )
```

```python
import functools
import math

import jax
import jax.numpy as jnp
from jax import lax
from jax.experimental import pallas as pl
from jax.experimental.pallas import tpu as pltpu
from jax.sharding import PartitionSpec as P

NEWT = 8
ROOT_TWO = math.sqrt(2.0)
LANES = 128
SUBLANES = 8
F32 = jnp.float32
BF16 = jnp.bfloat16
VMEM_LIMIT = 48 * 1024 * 1024
MARGIN = 8
WHOLE = (
    "coupling", "crit", "attract", "slope", "covol", "heat", "press", "loc", "member", "place",
    "flag", "visc", "trans", "inject", "seg", "strength", "own_press", "perm",
)


def iota(shape, dim):
    return lax.broadcasted_iota(jnp.int32, shape, dim)


def pieces_of(x, count):
    out = []
    for _ in range(count):
        piece = x.astype(BF16)
        out.append(piece)
        x = x - piece.astype(F32)
    return out


def mat(a, b):
    return lax.dot_general(a, b, (((1,), (0,)), ((), ())), preferred_element_type=F32)


def mat_nt(a, b):
    return lax.dot_general(a, b, (((1,), (1,)), ((), ())), preferred_element_type=F32)


def mat_hot(x, hot, count=3):
    return sum(mat(piece, hot) for piece in pieces_of(x, count))


def inverse(x):
    r = pl.reciprocal(x, approx=True)
    return r * (2.0 - x * r)


def hot(cond):
    return jnp.where(cond, 1.0, 0.0).astype(BF16)


def place_hots(loc, rows):
    n = loc.shape[1]
    row_hot = iota((rows, n), 0) == loc // LANES
    lane_hot = iota((LANES, n), 0) == loc % LANES
    return row_hot, lane_hot


def slot_hot_of(member, place):
    wells = place.shape[1]
    slot_of = hot(iota((wells, wells), 0) == wells - 1 - place)
    member_hot = hot(iota((wells, member.shape[1]), 0) == member)
    return mat(slot_of, member_hot)


def phase_kernel(
    nx,
    ny,
    axes,
    amount,
    *rest,
):
    sources, rest = rest[: len(WHOLE)], rest[len(WHOLE) :]
    (
        lnphi_out,
        carried_out,
        mob_out,
        edge_x_out,
        edge_ya_out,
        edge_yb_out,
        part_out,
        pcell_out,
        consts_out,
    ) = rest[:9]
    targets, rest = rest[9 : 9 + len(WHOLE)], rest[9 + len(WHOLE) :]
    amount_v, split_v, psi_v, lnphi_v, field_v, terms_v, table_v, small_sems, in_sems, out_sems = rest
    nc = amount.shape[0]
    per = 2
    chunks = nx // per
    half = chunks // 2
    rows = per * ny

    def go(source, target, sem):
        copy = pltpu.make_async_copy(source, target, sem)
        copy.start()
        return copy

    loads, copies = [], {}
    for k, name in enumerate(WHOLE):
        if name in ("press", "flag"):
            span = pl.ds(len(loads) * half * rows, half * rows)
            loads.append(go(amount.at[:, span], amount_v.at[:, span], in_sems.at[len(loads)]))
        copies[name] = go(sources[k], targets[k], small_sems.at[k])

    def arrived(*names):
        return [targets[WHOLE.index(name)] for name in names]

    for copy in [*copies.values(), *loads]:
        copy.wait()

    size = nc * ny
    spread = hot(iota((size, nc), 0) // ny == iota((size, nc), 1))
    same_row = iota((size, size), 0) % ny == iota((size, size), 1) % ny
    mixers = []
    (coupling,) = arrived("coupling")
    for piece in pieces_of(1.0 - coupling[...], 2):
        wide = mat(spread, piece).astype(BF16)
        mixers.append(jnp.where(same_row, mat_nt(wide, spread), 0.0).astype(BF16))
    mixer = jnp.concatenate([mixers[0], mixers[0], mixers[1]], axis=1)

    crit, attract, slope, covol = arrived("crit", "attract", "slope", "covol")
    for i in range(nc):
        root = jnp.sqrt(jnp.full((SUBLANES, LANES), attract[i], F32))
        kappa = jnp.full((SUBLANES, LANES), slope[i], F32)
        tc = jnp.full((SUBLANES, LANES), crit[i], F32)
        table_v[0, i] = root * (1.0 + kappa)
        table_v[1, i] = root * kappa / jnp.sqrt(tc)
        table_v[2, i] = jnp.full((SUBLANES, LANES), covol[i], F32)

    press, loc, member, place = arrived("press", "loc", "member", "place")
    row_hot, lane_hot = place_hots(loc[...], nx * ny)
    lane_hot = hot(lane_hot)

    def cells_of(field, count):
        found = mat_hot(field, lane_hot, count)
        return jnp.sum(jnp.where(row_hot, found, 0.0), axis=0, keepdims=True)

    p_cell = cells_of(press[...], 3)
    pcell_out[...] = p_cell
    slot_hot = slot_hot_of(member[...], place[...])
    (heat,) = arrived("heat")

    shape3 = (ny // SUBLANES, SUBLANES, LANES)
    root_t = [jnp.sqrt(heat[pl.ds(x * ny, ny)].reshape(shape3)) for x in range(nx)]
    for x in range(nx):
        span, lanes = pl.ds(x * ny, ny), pl.ds(x * LANES, LANES)
        total = jnp.zeros(shape3, F32)
        volume = jnp.zeros(shape3, F32)
        for i in range(nc):
            o = amount_v[i, span].reshape(shape3)
            v = jnp.abs(table_v[0, i] - table_v[1, i] * root_t[x]) * o
            total += o
            volume += table_v[2, i] * o
            high, low = pieces_of(v.reshape(ny, LANES), 2)
            split_v[pl.ds(i * ny, ny), lanes] = high
            split_v[pl.ds(size + i * ny, ny), lanes] = low
            split_v[pl.ds(2 * size + i * ny, ny), lanes] = high
        field_v[0, span] = total.reshape(ny, LANES)
        field_v[1, span] = volume.reshape(ny, LANES)
    for c in range(chunks):
        mixed = mat(mixer, split_v[:, pl.ds(c * per * LANES, per * LANES)])
        for k in range(per):
            x = c * per + k
            span = pl.ds(x * ny, ny)
            total = jnp.zeros(shape3, F32)
            for i in range(nc):
                m = mixed[i * ny : (i + 1) * ny, k * LANES : (k + 1) * LANES].reshape(shape3)
                psi = jnp.abs(table_v[0, i] - table_v[1, i] * root_t[x]) * m
                total += amount_v[i, span].reshape(shape3) * psi
                psi_v[i, span] = psi.reshape(ny, LANES)
            field_v[2, span] = total.reshape(ny, LANES)

    flag, visc, trans, inject = arrived("flag", "visc", "trans", "inject")
    states = []
    for h in range(2):
        span = pl.ds(h * half * rows, half * rows)
        p, t = press[span], heat[span]
        liquid = flag[span] == 1
        r = inverse(field_v[0, span])
        rt = inverse(t)
        ratio_pt = p * rt
        beta = field_v[1, span] * r
        gr = ratio_pt * rt * r
        big_a = gr * r * field_v[2, span]
        big_b = ratio_pt * beta
        z = jnp.where(liquid, big_b + 0.01, 1.0 + big_b)
        c1 = big_a - 3.0 * big_b * big_b - 2.0 * big_b
        c0 = big_b * big_b + big_b * big_b * big_b - big_a * big_b
        states.append([z, big_b, big_b + 0.01, big_b - 1.0, c1, c0])
        field_v[1, span] = inverse(beta)
        field_v[3, span] = r
        terms_v[0, span] = ratio_pt
        terms_v[1, span] = 0.5 * big_a
        terms_v[2, span] = gr
    for _ in range(NEWT):
        for state in states:
            z, _, floor, c2, c1, c0 = state
            near = z + c2
            value = (near * z + c1) * z + c0
            incline = (near + near + z) * z + c1
            state[0] = jnp.maximum(z - value * inverse(jnp.maximum(incline, 0.1)), floor)
    for h, (z, big_b, *_) in enumerate(states):
        span = pl.ds(h * half * rows, half * rows)
        ratio_pt, gr = terms_v[0, span], terms_v[2, span]
        log_ratio = jnp.log(
            (z + (1.0 + ROOT_TWO) * big_b) * inverse(z + (1.0 - ROOT_TWO) * big_b)
        )
        lb = log_ratio * inverse(ROOT_TWO * big_b)
        mob = ratio_pt * inverse(z * jnp.where(flag[span] == 1, visc[1], visc[0]))
        mob_out[span] = mob
        field_v[3, span] = mob * field_v[3, span]
        terms_v[0, span] = jnp.log(z - big_b)
        terms_v[1, span] = (z - 1.0 + terms_v[1, span] * lb) * field_v[1, span]
        terms_v[2, span] = gr * lb
    seg, strength, own_press, perm = arrived("seg", "strength", "own_press", "perm")
    weight = strength[...] * cells_of(mob_out[...], 2)
    segments = own_press.shape[1]
    lanes = iota((LANES, loc.shape[1]), 0)
    shift = hot(iota((segments, LANES), 0) + 2 * segments == iota((segments, LANES), 1))
    sums = mat_hot(own_press[...], shift)
    for k, value in enumerate((weight, weight * (p_cell - 1.0))):
        seg_hot = hot(lanes == seg[...] + k * segments)
        for piece in pieces_of(slot_hot * value, 2):
            sums += mat_nt(piece, seg_hot)
    part_out[...] = sums

    total = sum(inject[i] for i in range(nc))
    share = 1.0 / jnp.full((SUBLANES, LANES), total, F32)
    numbers = [trans[0], trans[1], trans[2], visc[0], visc[1]]
    for i in range(nc):
        consts_out[i] = inject[i] * share
    for i, number in enumerate(numbers):
        consts_out[nc + i] = jnp.full((SUBLANES, LANES), number, F32)

    stores = []
    for x in range(nx):
        span = pl.ds(x * ny, ny)
        e0, e1, e2 = (terms_v[k, span].reshape(shape3) for k in range(3))
        mr = field_v[3, span].reshape(shape3)
        for i in range(nc):
            value = table_v[2, i] * e1 - e0 - psi_v[i, span].reshape(shape3) * e2
            lnphi_v[i, span] = value.reshape(ny, LANES).astype(BF16)
            carried = (mr * amount_v[i, span].reshape(shape3)).reshape(ny, LANES)
            carried_out[i, pl.ds(MARGIN + x * ny, ny)] = carried
        if (x + 1) * 2 % nx == 0:
            span = pl.ds((x + 1 - nx // 2) * ny, nx // 2 * ny)
            stores.append(go(lnphi_v.at[:, span], lnphi_out.at[:, span], out_sems.at[len(stores)]))

    odd_g = lax.axis_index(axes[0]) % 2 == 1
    odd_s = lax.axis_index(axes[1]) % 2 == 1
    for k in range(edge_x_out.shape[0]):
        at_low = odd_g if k == 0 else jnp.logical_not(odd_g)
        start = pl.multiple_of(jnp.where(at_low, 0, (nx - 1) * ny), ny)
        for i in range(nc):
            edge_x_out[k, i] = carried_out[i, pl.ds(start + MARGIN, ny)]
        edge_x_out[k, nc] = press[pl.ds(start, ny)]
        edge_x_out[k, nc + 1] = perm[pl.ds(start, ny)]
    for i in range(nc + 2):
        source = carried_out.at[i] if i < nc else press if i == nc else perm
        skip = MARGIN if i < nc else 0
        low = source[pl.ds(skip, nx, stride=ny)]
        high = source[pl.ds(skip + ny - 1, nx, stride=ny)]
        edge_ya_out[i] = jnp.where(odd_s, low, high)
        edge_yb_out[i] = jnp.where(odd_s, high, low)
    for copy in stores:
        copy.wait()


def flux_kernel(
    nx,
    ny,
    axes,
    many_x,
    carried,
    press,
    perm,
    pore,
    flag,
    old,
    mob,
    edge_ya,
    edge_yb,
    well_rows,
    loc,
    member,
    seg,
    strength,
    place,
    pcell,
    consts,
    own_press,
    order,
    exit_press,
    friction,
    *rest,
):
    edge_x, rest = rest[:many_x], rest[many_x:]
    resid_out, well_out, y_v, res_v, out_sems = rest
    nc = carried.shape[0]
    g, s = lax.axis_index(axes[0]), lax.axis_index(axes[1])
    ng, ns = lax.axis_size(axes[0]), lax.axis_size(axes[1])
    odd_g, odd_s = g % 2 == 1, s % 2 == 1
    has_low_y, has_high_y = s > 0, s < ns - 1
    has_low_x, has_high_x = g > 0, g < ng - 1

    for i in range(nc + 2):
        a, b = edge_ya[i], edge_yb[i]
        low, high = jnp.where(odd_s, a, b), jnp.where(odd_s, b, a)
        if i == nc + 1:
            low, high = jnp.where(has_low_y, low, 0.0), jnp.where(has_high_y, high, 0.0)
        y_v[0, i] = low
        y_v[1, i] = high

    def side_x(i, high):
        if many_x == 1:
            return edge_x[0][i]
        return jnp.where(odd_g != high, edge_x[0][i], edge_x[1][i])

    row_hot, lane_hot = place_hots(loc[...], nx * ny)
    slot_hot = slot_hot_of(member[...], place[...])
    segments = own_press.shape[1]
    gathered = well_rows[...]
    seg_hot = hot(iota((LANES, loc.shape[1]), 0) == seg[...] + 2 * segments)
    p_seg = jnp.sum(mat_hot(gathered, seg_hot) * slot_hot, axis=0, keepdims=True)
    push = strength[...] * (pcell[...] - p_seg)
    flows = jnp.concatenate(
        [
            jnp.where(row_hot, jnp.maximum(push, 0.0), 0.0),
            jnp.where(row_hot, jnp.minimum(push, 0.0), 0.0),
        ],
        axis=0,
    )
    lane_hot = hot(lane_hot)
    spread = sum(mat_nt(piece, lane_hot) for piece in pieces_of(flows, 2))

    own = jnp.sum(gathered, axis=0, keepdims=True)
    well_p = own_press[...]
    rate = own[:, segments : 2 * segments] - (well_p - 1.0) * own[:, :segments]
    order_hot = hot(iota((segments, segments), 0) == order[...])
    both = mat_hot(jnp.concatenate([rate, well_p], axis=0), order_hot)
    upper = hot(iota((segments, segments), 0) <= iota((segments, segments), 1))
    running = mat_hot(both[0:1], upper)
    press_ord = both[1:2]
    after = hot(iota((segments, segments), 0) == iota((segments, segments), 1) + 1)
    last = iota((1, segments), 1) == segments - 1
    nexts = jnp.where(last, exit_press[0], mat_hot(press_ord, after))
    res_ord = press_ord - nexts - friction[0] * running * jnp.abs(running)
    well_out[...] = sum(mat_nt(piece, order_hot) for piece in pieces_of(res_ord, 3))

    lane = iota((ny, LANES), 1)
    row = iota((ny, LANES), 0)
    first, final = row == 0, row == ny - 1

    def const(k):
        return jnp.concatenate([consts[k]] * (ny // SUBLANES), axis=0)

    stores = []
    for x in range(nx):
        rows = pl.ds(x * ny, ny)
        p_a, k_a = press[rows], perm[rows]
        twice_k = 2.0 * k_a

        def face(p_b, k_b, axis):
            t = const(nc + axis) * (twice_k * k_b) * inverse(k_a + k_b)
            flow = t * (p_a - p_b)
            return jnp.maximum(flow, 0.0), jnp.minimum(flow, 0.0)

        def other_x(field, i, high):
            at = x + 1 if high else x - 1
            return field[pl.ds(at * ny, ny)] if 0 <= at < nx else side_x(i, high)

        def other_y(field, i, high):
            if high:
                return jnp.where(final, y_v[1, i, pl.ds(x, 1)], pltpu.roll(field, ny - 1, 0))
            return jnp.where(first, y_v[0, i, pl.ds(x, 1)], pltpu.roll(field, 1, 0))

        centre = pore[rows] * jnp.where(flag[rows] == 1, const(nc + 4), const(nc + 3))
        centre += spread[x * ny : (x + 1) * ny]
        ins = []
        for high in (True, False):
            p_b, k_b = other_x(press, nc, high), other_x(perm, nc + 1, high)
            if x == nx - 1 and high:
                k_b = jnp.where(has_high_x, k_b, 0.0)
            if x == 0 and not high:
                k_b = jnp.where(has_low_x, k_b, 0.0)
            ins.append(face(p_b, k_b, 0))
        for high in (True, False):
            ins.append(face(other_y(p_a, nc, high), other_y(k_a, nc + 1, high), 1))
        for shift, edge in ((LANES - 1, LANES - 1), (1, 0)):
            k_b = jnp.where(lane == edge, 0.0, pltpu.roll(k_a, shift, 1))
            ins.append(face(pltpu.roll(p_a, shift, 1), k_b, 2))
        for out, _ in ins:
            centre += out
        ins = [into for _, into in ins]
        pushed = mob[rows] * spread[(nx + x) * ny : (nx + x + 1) * ny]
        for i in range(nc):
            base = MARGIN + x * ny
            c = carried[i, pl.ds(base, ny)]
            value = centre * c - old[i, rows] + const(i) * pushed
            for k, high in ((0, True), (1, False)):
                at = x + 1 if high else x - 1
                inside = 0 <= at < nx
                c_b = carried[i, pl.ds(MARGIN + at * ny, ny)] if inside else side_x(i, high)
                value += ins[k] * c_b
            up, down = carried[i, pl.ds(base + 1, ny)], carried[i, pl.ds(base - 1, ny)]
            value += ins[2] * jnp.where(final, y_v[1, i, pl.ds(x, 1)], up)
            value += ins[3] * jnp.where(first, y_v[0, i, pl.ds(x, 1)], down)
            value += ins[4] * pltpu.roll(c, LANES - 1, 1)
            value += ins[5] * pltpu.roll(c, 1, 1)
            res_v[i, rows] = value
        copy = pltpu.make_async_copy(res_v.at[:, rows], resid_out.at[:, rows], out_sems.at[x])
        copy.start()
        stores.append(copy)
    for copy in stores:
        copy.wait()


def swaps_of(count, other):
    pairs = [(i, i + 1) for i in range(1 if other else 0, count - 1, 2)]
    return pairs + [(b, a) for a, b in pairs]


def other_swaps_of(groups, count):
    swaps = [(g * count + a, g * count + b) for g in range(groups) for a, b in swaps_of(count, True)]
    ends = [(g * count + e, (g ^ 1) * count + e) for g in range(groups) for e in (0, count - 1)]
    return sorted(swaps + ends)


def per_device(
    amount,
    press,
    heat,
    flag,
    perm,
    pore,
    old,
    trans,
    visc,
    crit,
    attract,
    covol,
    slope,
    coupling,
    inject,
    locale,
    member,
    seg,
    strength,
    place,
    order,
    seg_press,
    exit_press,
    friction,
):
    axes = ("grp", "sub")
    nc, nx, ny, nz = amount.shape
    ng, ns = lax.axis_size("grp"), lax.axis_size("sub")
    rows = nx * ny
    perfs = locale.shape[0]
    wells, segments = place.shape[1], seg_press.shape[1]
    flat = lambda a: a.reshape(a.shape[:-3] + (rows, nz))
    line = lambda a: a.reshape(1, perfs)
    vm = pl.BlockSpec(memory_space=pltpu.VMEM)
    sm = pl.BlockSpec(memory_space=pltpu.SMEM)
    hbm = pl.BlockSpec(memory_space=pltpu.HBM)
    many_x = 1 if ng == 2 else 2

    amount, old = flat(amount), flat(old)
    press, heat, flag, perm, pore = (flat(a) for a in (press, heat, flag, perm, pore))
    locale, member, seg, strength = (line(a) for a in (locale, member, seg, strength))

    sources = (
        coupling, crit, attract, slope, covol, heat, press, locale, member, place,
        flag, visc, trans, inject, seg, strength, seg_press, perm,
    )
    kept = [
        pltpu.SMEM(a.shape, a.dtype) if a.ndim == 1 else pltpu.VMEM(a.shape, a.dtype)
        for a in sources
    ]
    in_hbm = lambda a: pltpu.with_memory_space_constraint(a, pltpu.HBM)

    lnphi, carried, mob, edge_x, edge_ya, edge_yb, part, pcell, consts = pl.pallas_call(
        functools.partial(phase_kernel, nx, ny, axes),
        out_shape=(
            jax.ShapeDtypeStruct((nc, rows, nz), BF16),
            jax.ShapeDtypeStruct((nc, rows + 2 * MARGIN, nz), F32),
            jax.ShapeDtypeStruct((rows, nz), F32),
            jax.ShapeDtypeStruct((many_x, nc + 2, ny, nz), F32),
            jax.ShapeDtypeStruct((nc + 2, nx, nz), F32),
            jax.ShapeDtypeStruct((nc + 2, nx, nz), F32),
            jax.ShapeDtypeStruct((wells, LANES), F32),
            jax.ShapeDtypeStruct((1, perfs), F32),
            jax.ShapeDtypeStruct((nc + 8, SUBLANES, LANES), F32),
        ),
        in_specs=[hbm] * (1 + len(sources)),
        out_specs=(hbm,) + (vm,) * 8,
        scratch_shapes=[
            *kept,
            pltpu.VMEM((nc, rows, nz), F32),
            pltpu.VMEM((3 * nc * ny, nx * nz), BF16),
            pltpu.VMEM((nc, rows, nz), F32),
            pltpu.VMEM((nc, rows, nz), BF16),
            pltpu.VMEM((4, rows, nz), F32),
            pltpu.VMEM((3, rows, nz), F32),
            pltpu.VMEM((3, nc, SUBLANES, LANES), F32),
            pltpu.SemaphoreType.DMA((len(sources),)),
            pltpu.SemaphoreType.DMA((2,)),
            pltpu.SemaphoreType.DMA((2,)),
        ],
        compiler_params=pltpu.CompilerParams(vmem_limit_bytes=VMEM_LIMIT),
        name="phase",
    )(in_hbm(amount), *(in_hbm(a) for a in sources))

    got_ya = lax.ppermute(edge_ya, "sub", swaps_of(ns, False))
    got_x = [lax.ppermute(edge_x[k], "grp", swaps_of(ng, k == 1)) for k in range(many_x)]
    got_yb = lax.ppermute(edge_yb, axes, other_swaps_of(ng, ns))
    backward = [list(range(ns))[::-1]]
    well_rows = lax.all_to_all(
        part, "sub", split_axis=0, concat_axis=0, axis_index_groups=backward, tiled=True
    )

    resid, well = pl.pallas_call(
        functools.partial(flux_kernel, nx, ny, axes, many_x),
        out_shape=(
            jax.ShapeDtypeStruct((nc, rows, nz), F32),
            jax.ShapeDtypeStruct((1, segments), F32),
        ),
        in_specs=[vm] * 19 + [sm] * 2 + [vm] * many_x,
        out_specs=(hbm, vm),
        scratch_shapes=[
            pltpu.VMEM((2, nc + 2, nx, nz), F32),
            pltpu.VMEM((nc, rows, nz), F32),
            pltpu.SemaphoreType.DMA((nx,)),
        ],
        compiler_params=pltpu.CompilerParams(vmem_limit_bytes=VMEM_LIMIT),
        name="flux",
    )(
        carried, press, perm, pore, flag, old, mob, got_ya, got_yb, well_rows,
        locale, member, seg, strength, place, pcell,
        consts, seg_press, order, exit_press, friction, *got_x,
    )
    block = (nc, nx, ny, nz)
    return resid.reshape(block), lnphi.reshape(block), well


def solution(mesh):
    cells, parts = P("grp", "sub", None), P(None, "grp", "sub", None)
    listed = P(("grp", "sub"))
    row = P(("grp", "sub"), None)
    in_specs = (
        (parts,) + (cells,) * 5 + (parts,) + (P(),) * 8
        + (listed, row, listed, listed, P("grp", None), row, row, listed, listed)
    )
    return jax.shard_map(
        per_device, mesh=mesh, in_specs=in_specs, out_specs=(parts, parts, row), check_vma=False
    )
```

```python
import functools
import math

import jax
import jax.numpy as jnp
from jax import lax
from jax.experimental import pallas as pl
from jax.experimental.pallas import tpu as pltpu
from jax.sharding import PartitionSpec as P

NEWT = 8
ROOT_TWO = math.sqrt(2.0)
LANES = 128
SUBLANES = 8
F32 = jnp.float32
BF16 = jnp.bfloat16
VMEM_LIMIT = 48 * 1024 * 1024
MARGIN = 8
WHOLE = (
    "coupling", "crit", "attract", "slope", "covol", "heat", "press", "loc", "member", "place",
    "flag", "visc", "trans", "inject", "seg", "strength", "own_press", "perm", "pore",
)


def iota(shape, dim):
    return lax.broadcasted_iota(jnp.int32, shape, dim)


def pieces_of(x, count):
    out = []
    for _ in range(count):
        piece = x.astype(BF16)
        out.append(piece)
        x = x - piece.astype(F32)
    return out


def mat(a, b):
    return lax.dot_general(a, b, (((1,), (0,)), ((), ())), preferred_element_type=F32)


def mat_nt(a, b):
    return lax.dot_general(a, b, (((1,), (1,)), ((), ())), preferred_element_type=F32)


def mat_hot(x, hot, count=3):
    return sum(mat(piece, hot) for piece in pieces_of(x, count))


def inverse(x):
    r = pl.reciprocal(x, approx=True)
    return r * (2.0 - x * r)


def hot(cond):
    return jnp.where(cond, 1.0, 0.0).astype(BF16)


def place_hots(loc, rows):
    n = loc.shape[1]
    row_hot = iota((rows, n), 0) == loc // LANES
    lane_hot = iota((LANES, n), 0) == loc % LANES
    return row_hot, lane_hot


def slot_hot_of(member, place):
    wells = place.shape[1]
    slot_of = hot(iota((wells, wells), 0) == wells - 1 - place)
    member_hot = hot(iota((wells, member.shape[1]), 0) == member)
    return mat(slot_of, member_hot)


def phase_kernel(
    nx,
    ny,
    axes,
    amount,
    *rest,
):
    sources, rest = rest[: len(WHOLE)], rest[len(WHOLE) :]
    (
        psi_v,
        terms_v,
        carried_out,
        mob_out,
        store_out,
        edge_x_out,
        edge_ya_out,
        edge_yb_out,
        part_out,
        pcell_out,
        consts_out,
        covol_out,
    ) = rest[:12]
    targets, rest = rest[12 : 12 + len(WHOLE)], rest[12 + len(WHOLE) :]
    amount_v, split_v, field_v, table_v, part_v, small_sems, in_sems, out_sems = rest
    nc = amount.shape[0]
    per = 2
    chunks = nx // per
    half = chunks // 2
    rows = per * ny

    def go(source, target, sem):
        copy = pltpu.make_async_copy(source, target, sem)
        copy.start()
        return copy

    loads, copies = [], {}
    for k, name in enumerate(WHOLE):
        if name in ("press", "flag"):
            span = pl.ds(len(loads) * half * rows, half * rows)
            loads.append(go(amount.at[:, span], amount_v.at[:, span], in_sems.at[len(loads)]))
        copies[name] = go(sources[k], targets[k], small_sems.at[k])

    def arrived(*names):
        return [targets[WHOLE.index(name)] for name in names]

    for copy in [*copies.values(), *loads]:
        copy.wait()

    size = nc * ny
    spread = hot(iota((size, nc), 0) // ny == iota((size, nc), 1))
    same_row = iota((size, size), 0) % ny == iota((size, size), 1) % ny
    mixers = []
    (coupling,) = arrived("coupling")
    for piece in pieces_of(1.0 - coupling[...], 2):
        wide = mat(spread, piece).astype(BF16)
        mixers.append(jnp.where(same_row, mat_nt(wide, spread), 0.0).astype(BF16))
    mixer = jnp.concatenate([mixers[0], mixers[0], mixers[1]], axis=1)

    crit, attract, slope, covol = arrived("crit", "attract", "slope", "covol")
    for i in range(nc):
        root = jnp.sqrt(jnp.full((SUBLANES, LANES), attract[i], F32))
        kappa = jnp.full((SUBLANES, LANES), slope[i], F32)
        tc = jnp.full((SUBLANES, LANES), crit[i], F32)
        table_v[0, i] = root * (1.0 + kappa)
        table_v[1, i] = root * kappa / jnp.sqrt(tc)
        table_v[2, i] = jnp.full((SUBLANES, LANES), covol[i], F32)

    press, loc, member, place = arrived("press", "loc", "member", "place")
    row_hot, lane_hot = place_hots(loc[...], nx * ny)
    lane_hot = hot(lane_hot)

    def cells_of(field, count):
        found = mat_hot(field, lane_hot, count)
        return jnp.sum(jnp.where(row_hot, found, 0.0), axis=0, keepdims=True)

    p_cell = cells_of(press[...], 3)
    pcell_out[...] = p_cell
    slot_hot = slot_hot_of(member[...], place[...])
    (heat,) = arrived("heat")

    shape3 = (ny // SUBLANES, SUBLANES, LANES)
    root_t = [jnp.sqrt(heat[pl.ds(x * ny, ny)].reshape(shape3)) for x in range(nx)]
    for x in range(nx):
        span, lanes = pl.ds(x * ny, ny), pl.ds(x * LANES, LANES)
        total = jnp.zeros(shape3, F32)
        volume = jnp.zeros(shape3, F32)
        for i in range(nc):
            o = amount_v[i, span].reshape(shape3)
            v = jnp.abs(table_v[0, i] - table_v[1, i] * root_t[x]) * o
            total += o
            volume += table_v[2, i] * o
            high, low = pieces_of(v.reshape(ny, LANES), 2)
            split_v[pl.ds(i * ny, ny), lanes] = high
            split_v[pl.ds(size + i * ny, ny), lanes] = low
            split_v[pl.ds(2 * size + i * ny, ny), lanes] = high
        field_v[0, span] = total.reshape(ny, LANES)
        field_v[1, span] = volume.reshape(ny, LANES)
    for c in range(chunks):
        mixed = mat(mixer, split_v[:, pl.ds(c * per * LANES, per * LANES)])
        for k in range(per):
            x = c * per + k
            span = pl.ds(x * ny, ny)
            total = jnp.zeros(shape3, F32)
            for i in range(nc):
                m = mixed[i * ny : (i + 1) * ny, k * LANES : (k + 1) * LANES].reshape(shape3)
                psi = jnp.abs(table_v[0, i] - table_v[1, i] * root_t[x]) * m
                total += amount_v[i, span].reshape(shape3) * psi
                psi_v[i, span] = psi.reshape(ny, LANES)
            field_v[2, span] = total.reshape(ny, LANES)

    flag, visc, trans, inject = arrived("flag", "visc", "trans", "inject")
    states = []
    for h in range(2):
        span = pl.ds(h * half * rows, half * rows)
        p, t = press[span], heat[span]
        liquid = flag[span] == 1
        r = inverse(field_v[0, span])
        rt = inverse(t)
        ratio_pt = p * rt
        beta = field_v[1, span] * r
        gr = ratio_pt * rt * r
        big_a = gr * r * field_v[2, span]
        big_b = ratio_pt * beta
        z = jnp.where(liquid, big_b + 0.01, 1.0 + big_b)
        c1 = big_a - 3.0 * big_b * big_b - 2.0 * big_b
        c0 = big_b * big_b + big_b * big_b * big_b - big_a * big_b
        states.append([z, big_b, big_b + 0.01, big_b - 1.0, c1, c0])
        field_v[1, span] = inverse(beta)
        field_v[3, span] = r
        terms_v[0, span] = ratio_pt
        terms_v[1, span] = 0.5 * big_a
        terms_v[2, span] = gr
    for _ in range(NEWT):
        for state in states:
            z, _, floor, c2, c1, c0 = state
            near = z + c2
            value = (near * z + c1) * z + c0
            incline = (near + near + z) * z + c1
            state[0] = jnp.maximum(z - value * inverse(jnp.maximum(incline, 0.1)), floor)
    for h, (z, big_b, *_) in enumerate(states):
        span = pl.ds(h * half * rows, half * rows)
        ratio_pt, gr = terms_v[0, span], terms_v[2, span]
        log_ratio = jnp.log(
            (z + (1.0 + ROOT_TWO) * big_b) * inverse(z + (1.0 - ROOT_TWO) * big_b)
        )
        lb = log_ratio * inverse(ROOT_TWO * big_b)
        mob = ratio_pt * inverse(z * jnp.where(flag[span] == 1, visc[1], visc[0]))
        mob_out[span] = mob
        field_v[3, span] = mob * field_v[3, span]
        terms_v[0, span] = jnp.log(z - big_b)
        terms_v[1, span] = (z - 1.0 + terms_v[1, span] * lb) * field_v[1, span]
        terms_v[2, span] = gr * lb
    seg, strength, own_press, perm = arrived("seg", "strength", "own_press", "perm")
    weight = strength[...] * cells_of(mob_out[...], 2)
    segments = own_press.shape[1]
    lanes = iota((LANES, loc.shape[1]), 0)
    shift = hot(iota((segments, LANES), 0) + 2 * segments == iota((segments, LANES), 1))
    sums = mat_hot(own_press[...], shift)
    for k, value in enumerate((weight, weight * (p_cell - 1.0))):
        seg_hot = hot(lanes == seg[...] + k * segments)
        for piece in pieces_of(slot_hot * value, 2):
            sums += mat_nt(piece, seg_hot)
    part_v[...] = sums
    part_copy = go(part_v, part_out, out_sems.at[0])

    (pore,) = arrived("pore")
    store_out[...] = pore[...] * jnp.where(flag[...] == 1, visc[1], visc[0])
    for x in range(nx):
        span = pl.ds(x * ny, ny)
        mr = field_v[3, span]
        for i in range(nc):
            carried_out[i, pl.ds(MARGIN + x * ny, ny)] = mr * amount_v[i, span]

    total = sum(inject[i] for i in range(nc))
    share = 1.0 / jnp.full((SUBLANES, LANES), total, F32)
    for i in range(nc):
        consts_out[i] = inject[i] * share
        covol_out[pl.ds(i, 1)] = jnp.full((1, LANES), covol[i], F32)
    for k in range(3):
        consts_out[nc + k] = jnp.full((SUBLANES, LANES), trans[k], F32)

    odd_g = lax.axis_index(axes[0]) % 2 == 1
    odd_s = lax.axis_index(axes[1]) % 2 == 1
    for k in range(edge_x_out.shape[0]):
        at_low = odd_g if k == 0 else jnp.logical_not(odd_g)
        start = pl.multiple_of(jnp.where(at_low, 0, (nx - 1) * ny), ny)
        for i in range(nc):
            edge_x_out[k, i] = carried_out[i, pl.ds(start + MARGIN, ny)]
        edge_x_out[k, nc] = press[pl.ds(start, ny)]
        edge_x_out[k, nc + 1] = perm[pl.ds(start, ny)]
    for i in range(nc + 2):
        source = carried_out.at[i] if i < nc else press if i == nc else perm
        skip = MARGIN if i < nc else 0
        low = source[pl.ds(skip, nx, stride=ny)]
        high = source[pl.ds(skip + ny - 1, nx, stride=ny)]
        edge_ya_out[i] = jnp.where(odd_s, low, high)
        edge_yb_out[i] = jnp.where(odd_s, high, low)
    part_copy.wait()


def fugacity_kernel(ny, psi, terms, covol, lnphi_out, lnphi_v, sems):
    nc, rows, _ = psi.shape
    parts = sems.shape[0]
    stores = []
    for part in range(parts):
        for x in range(part * rows // parts // ny, (part + 1) * rows // parts // ny):
            span = pl.ds(x * ny, ny)
            e0, e1, e2 = (terms[k, span] for k in range(3))
            for i in range(nc):
                value = covol[pl.ds(i, 1)] * e1 - e0 - psi[i, span] * e2
                lnphi_v[i, span] = value.astype(BF16)
        span = pl.ds(part * rows // parts, rows // parts)
        copy = pltpu.make_async_copy(lnphi_v.at[:, span], lnphi_out.at[:, span], sems.at[part])
        copy.start()
        stores.append(copy)
    for copy in stores:
        copy.wait()


def flux_kernel(
    nx,
    ny,
    axes,
    many_x,
    carried,
    press,
    perm,
    store,
    old_in,
    mob,
    edge_ya,
    edge_yb,
    well_rows,
    loc,
    member,
    seg,
    strength,
    place,
    pcell,
    consts,
    own_press,
    order,
    exit_press,
    friction,
    *rest,
):
    edge_x, rest = rest[:many_x], rest[many_x:]
    resid_out, well_out, old, y_v, res_v, well_v, in_sems, out_sems = rest
    nc = carried.shape[0]
    loads = []
    for x in range(nx):
        span = pl.ds(x * ny, ny)
        copy = pltpu.make_async_copy(old_in.at[:, span], old.at[:, span], in_sems.at[x])
        copy.start()
        loads.append(copy)
    g, s = lax.axis_index(axes[0]), lax.axis_index(axes[1])
    ng, ns = lax.axis_size(axes[0]), lax.axis_size(axes[1])
    odd_g, odd_s = g % 2 == 1, s % 2 == 1
    has_low_y, has_high_y = s > 0, s < ns - 1
    has_low_x, has_high_x = g > 0, g < ng - 1

    for i in range(nc + 2):
        a, b = edge_ya[i], edge_yb[i]
        low, high = jnp.where(odd_s, a, b), jnp.where(odd_s, b, a)
        if i == nc + 1:
            low, high = jnp.where(has_low_y, low, 0.0), jnp.where(has_high_y, high, 0.0)
        y_v[0, i] = low
        y_v[1, i] = high

    def side_x(i, high):
        if many_x == 1:
            return edge_x[0][i]
        return jnp.where(odd_g != high, edge_x[0][i], edge_x[1][i])

    row_hot, lane_hot = place_hots(loc[...], nx * ny)
    slot_hot = slot_hot_of(member[...], place[...])
    segments = own_press.shape[1]
    gathered = well_rows[...]
    seg_hot = hot(iota((LANES, loc.shape[1]), 0) == seg[...] + 2 * segments)
    p_seg = jnp.sum(mat_hot(gathered, seg_hot) * slot_hot, axis=0, keepdims=True)
    push = strength[...] * (pcell[...] - p_seg)
    flows = jnp.concatenate(
        [
            jnp.where(row_hot, jnp.maximum(push, 0.0), 0.0),
            jnp.where(row_hot, jnp.minimum(push, 0.0), 0.0),
        ],
        axis=0,
    )
    lane_hot = hot(lane_hot)
    spread = sum(mat_nt(piece, lane_hot) for piece in pieces_of(flows, 2))

    own = jnp.sum(gathered, axis=0, keepdims=True)
    well_p = own_press[...]
    rate = own[:, segments : 2 * segments] - (well_p - 1.0) * own[:, :segments]
    order_hot = hot(iota((segments, segments), 0) == order[...])
    both = mat_hot(jnp.concatenate([rate, well_p], axis=0), order_hot)
    upper = hot(iota((segments, segments), 0) <= iota((segments, segments), 1))
    running = mat_hot(both[0:1], upper)
    press_ord = both[1:2]
    after = hot(iota((segments, segments), 0) == iota((segments, segments), 1) + 1)
    last = iota((1, segments), 1) == segments - 1
    nexts = jnp.where(last, exit_press[0], mat_hot(press_ord, after))
    res_ord = press_ord - nexts - friction[0] * running * jnp.abs(running)
    well_v[...] = sum(mat_nt(piece, order_hot) for piece in pieces_of(res_ord, 3))
    stores = [pltpu.make_async_copy(well_v, well_out, out_sems.at[nx])]
    stores[0].start()

    lane = iota((ny, LANES), 1)
    row = iota((ny, LANES), 0)
    first, final = row == 0, row == ny - 1

    def const(k):
        return jnp.concatenate([consts[k]] * (ny // SUBLANES), axis=0)

    for x in range(nx):
        rows = pl.ds(x * ny, ny)
        p_a, k_a = press[rows], perm[rows]
        twice_k = 2.0 * k_a

        def face(p_b, k_b, axis):
            t = const(nc + axis) * (twice_k * k_b) * inverse(k_a + k_b)
            flow = t * (p_a - p_b)
            return jnp.maximum(flow, 0.0), jnp.minimum(flow, 0.0)

        def other_x(field, i, high):
            at = x + 1 if high else x - 1
            return field[pl.ds(at * ny, ny)] if 0 <= at < nx else side_x(i, high)

        def other_y(field, i, high):
            if high:
                return jnp.where(final, y_v[1, i, pl.ds(x, 1)], pltpu.roll(field, ny - 1, 0))
            return jnp.where(first, y_v[0, i, pl.ds(x, 1)], pltpu.roll(field, 1, 0))

        centre = store[rows] + spread[x * ny : (x + 1) * ny]
        ins = []
        for high in (True, False):
            p_b, k_b = other_x(press, nc, high), other_x(perm, nc + 1, high)
            if x == nx - 1 and high:
                k_b = jnp.where(has_high_x, k_b, 0.0)
            if x == 0 and not high:
                k_b = jnp.where(has_low_x, k_b, 0.0)
            ins.append(face(p_b, k_b, 0))
        for high in (True, False):
            ins.append(face(other_y(p_a, nc, high), other_y(k_a, nc + 1, high), 1))
        for shift, edge in ((LANES - 1, LANES - 1), (1, 0)):
            k_b = jnp.where(lane == edge, 0.0, pltpu.roll(k_a, shift, 1))
            ins.append(face(pltpu.roll(p_a, shift, 1), k_b, 2))
        for out, _ in ins:
            centre += out
        ins = [into for _, into in ins]
        pushed = mob[rows] * spread[(nx + x) * ny : (nx + x + 1) * ny]
        loads[x].wait()
        for i in range(nc):
            base = MARGIN + x * ny
            c = carried[i, pl.ds(base, ny)]
            value = centre * c - old[i, rows] + const(i) * pushed
            for k, high in ((0, True), (1, False)):
                at = x + 1 if high else x - 1
                inside = 0 <= at < nx
                c_b = carried[i, pl.ds(MARGIN + at * ny, ny)] if inside else side_x(i, high)
                value += ins[k] * c_b
            up, down = carried[i, pl.ds(base + 1, ny)], carried[i, pl.ds(base - 1, ny)]
            value += ins[2] * jnp.where(final, y_v[1, i, pl.ds(x, 1)], up)
            value += ins[3] * jnp.where(first, y_v[0, i, pl.ds(x, 1)], down)
            value += ins[4] * pltpu.roll(c, LANES - 1, 1)
            value += ins[5] * pltpu.roll(c, 1, 1)
            res_v[i, rows] = value
        copy = pltpu.make_async_copy(res_v.at[:, rows], resid_out.at[:, rows], out_sems.at[x])
        copy.start()
        stores.append(copy)
    for copy in stores:
        copy.wait()


def swaps_of(count, other):
    pairs = [(i, i + 1) for i in range(1 if other else 0, count - 1, 2)]
    return pairs + [(b, a) for a, b in pairs]


def other_swaps_of(groups, count):
    swaps = [(g * count + a, g * count + b) for g in range(groups) for a, b in swaps_of(count, True)]
    ends = [(g * count + e, (g ^ 1) * count + e) for g in range(groups) for e in (0, count - 1)]
    return sorted(swaps + ends)


def per_device(
    amount,
    press,
    heat,
    flag,
    perm,
    pore,
    old,
    trans,
    visc,
    crit,
    attract,
    covol,
    slope,
    coupling,
    inject,
    locale,
    member,
    seg,
    strength,
    place,
    order,
    seg_press,
    exit_press,
    friction,
):
    axes = ("grp", "sub")
    nc, nx, ny, nz = amount.shape
    ng, ns = lax.axis_size("grp"), lax.axis_size("sub")
    rows = nx * ny
    perfs = locale.shape[0]
    wells, segments = place.shape[1], seg_press.shape[1]
    flat = lambda a: a.reshape(a.shape[:-3] + (rows, nz))
    line = lambda a: a.reshape(1, perfs)
    vm = pl.BlockSpec(memory_space=pltpu.VMEM)
    sm = pl.BlockSpec(memory_space=pltpu.SMEM)
    hbm = pl.BlockSpec(memory_space=pltpu.HBM)
    many_x = 1 if ng == 2 else 2

    amount, old = flat(amount), flat(old)
    press, heat, flag, perm, pore = (flat(a) for a in (press, heat, flag, perm, pore))
    locale, member, seg, strength = (line(a) for a in (locale, member, seg, strength))

    sources = (
        coupling, crit, attract, slope, covol, heat, press, locale, member, place,
        flag, visc, trans, inject, seg, strength, seg_press, perm, pore,
    )
    kept = [
        pltpu.SMEM(a.shape, a.dtype) if a.ndim == 1 else pltpu.VMEM(a.shape, a.dtype)
        for a in sources
    ]
    in_hbm = lambda a: pltpu.with_memory_space_constraint(a, pltpu.HBM)

    psi, terms, carried, mob, store, edge_x, edge_ya, edge_yb, part, pcell, consts, covols = pl.pallas_call(
        functools.partial(phase_kernel, nx, ny, axes),
        out_shape=(
            jax.ShapeDtypeStruct((nc, rows, nz), F32),
            jax.ShapeDtypeStruct((3, rows, nz), F32),
            jax.ShapeDtypeStruct((nc, rows + 2 * MARGIN, nz), F32),
            jax.ShapeDtypeStruct((rows, nz), F32),
            jax.ShapeDtypeStruct((rows, nz), F32),
            jax.ShapeDtypeStruct((many_x, nc + 2, ny, nz), F32),
            jax.ShapeDtypeStruct((nc + 2, nx, nz), F32),
            jax.ShapeDtypeStruct((nc + 2, nx, nz), F32),
            jax.ShapeDtypeStruct((wells, LANES), F32),
            jax.ShapeDtypeStruct((1, perfs), F32),
            jax.ShapeDtypeStruct((nc + 3, SUBLANES, LANES), F32),
            jax.ShapeDtypeStruct((nc, LANES), F32),
        ),
        in_specs=[hbm] * (1 + len(sources)),
        out_specs=(vm,) * 8 + (hbm,) + (vm,) * 3,
        scratch_shapes=[
            *kept,
            pltpu.VMEM((nc, rows, nz), F32),
            pltpu.VMEM((3 * nc * ny, nx * nz), BF16),
            pltpu.VMEM((4, rows, nz), F32),
            pltpu.VMEM((3, nc, SUBLANES, LANES), F32),
            pltpu.VMEM((wells, LANES), F32),
            pltpu.SemaphoreType.DMA((len(sources),)),
            pltpu.SemaphoreType.DMA((2,)),
            pltpu.SemaphoreType.DMA((1,)),
        ],
        compiler_params=pltpu.CompilerParams(vmem_limit_bytes=VMEM_LIMIT),
        name="phase",
    )(in_hbm(amount), *(in_hbm(a) for a in sources))

    got_ya = lax.ppermute(edge_ya, "sub", swaps_of(ns, False))
    got_x = [lax.ppermute(edge_x[k], "grp", swaps_of(ng, k == 1)) for k in range(many_x)]
    got_yb = lax.ppermute(edge_yb, axes, other_swaps_of(ng, ns))
    backward = [list(range(ns))[::-1]]
    well_rows = lax.all_to_all(
        part, "sub", split_axis=0, concat_axis=0, axis_index_groups=backward, tiled=True
    )

    lnphi = pl.pallas_call(
        functools.partial(fugacity_kernel, ny),
        out_shape=jax.ShapeDtypeStruct((nc, rows, nz), BF16),
        in_specs=[vm] * 3,
        out_specs=hbm,
        scratch_shapes=[pltpu.VMEM((nc, rows, nz), BF16), pltpu.SemaphoreType.DMA((4,))],
        compiler_params=pltpu.CompilerParams(vmem_limit_bytes=VMEM_LIMIT),
        cost_estimate=pl.CostEstimate(
            flops=8 * nc * rows * nz, bytes_accessed=256 * nc * rows * nz, transcendentals=0
        ),
        name="fugacity",
    )(psi, terms, covols)

    resid, well = pl.pallas_call(
        functools.partial(flux_kernel, nx, ny, axes, many_x),
        out_shape=(
            jax.ShapeDtypeStruct((nc, rows, nz), F32),
            jax.ShapeDtypeStruct((1, segments), F32),
        ),
        in_specs=[vm] * 4 + [hbm] + [vm] * 13 + [sm] * 2 + [vm] * many_x,
        out_specs=(hbm, hbm),
        scratch_shapes=[
            pltpu.VMEM((nc, rows, nz), F32),
            pltpu.VMEM((2, nc + 2, nx, nz), F32),
            pltpu.VMEM((nc, rows, nz), F32),
            pltpu.VMEM((1, segments), F32),
            pltpu.SemaphoreType.DMA((nx,)),
            pltpu.SemaphoreType.DMA((nx + 1,)),
        ],
        compiler_params=pltpu.CompilerParams(vmem_limit_bytes=VMEM_LIMIT),
        name="flux",
    )(
        carried, press, perm, store, in_hbm(old), mob, got_ya, got_yb, well_rows,
        locale, member, seg, strength, place, pcell,
        consts, seg_press, order, exit_press, friction, *got_x,
    )
    block = (nc, nx, ny, nz)
    return resid.reshape(block), lnphi.reshape(block), well


def solution(mesh):
    cells, parts = P("grp", "sub", None), P(None, "grp", "sub", None)
    listed = P(("grp", "sub"))
    row = P(("grp", "sub"), None)
    in_specs = (
        (parts,) + (cells,) * 5 + (parts,) + (P(),) * 8
        + (listed, row, listed, listed, P("grp", None), row, row, listed, listed)
    )
    return jax.shard_map(
        per_device, mesh=mesh, in_specs=in_specs, out_specs=(parts, parts, row), check_vma=False
    )
```

```python
import functools
import math

import jax
import jax.numpy as jnp
from jax import lax
from jax.experimental import pallas as pl
from jax.experimental.pallas import tpu as pltpu
from jax.sharding import PartitionSpec as P

NEWT = 8
ROOT_TWO = math.sqrt(2.0)
LANES = 128
SUBLANES = 8
F32 = jnp.float32
BF16 = jnp.bfloat16
VMEM_LIMIT = 48 * 1024 * 1024
MARGIN = 8
WHOLE = (
    "coupling", "crit", "attract", "slope", "covol", "heat", "press", "loc", "member", "place",
    "flag", "visc", "trans", "inject", "seg", "strength", "own_press", "perm", "pore",
)


def iota(shape, dim):
    return lax.broadcasted_iota(jnp.int32, shape, dim)


def pieces_of(x, count):
    out = []
    for _ in range(count):
        piece = x.astype(BF16)
        out.append(piece)
        x = x - piece.astype(F32)
    return out


def mat(a, b):
    return lax.dot_general(a, b, (((1,), (0,)), ((), ())), preferred_element_type=F32)


def mat_nt(a, b):
    return lax.dot_general(a, b, (((1,), (1,)), ((), ())), preferred_element_type=F32)


def mat_hot(x, hot, count=3):
    return sum(mat(piece, hot) for piece in pieces_of(x, count))


def inverse(x):
    r = pl.reciprocal(x, approx=True)
    return r * (2.0 - x * r)


def hot(cond):
    return jnp.where(cond, 1.0, 0.0).astype(BF16)


def place_hots(loc, rows):
    n = loc.shape[1]
    row_hot = iota((rows, n), 0) == loc // LANES
    lane_hot = iota((LANES, n), 0) == loc % LANES
    return row_hot, lane_hot


def slot_hot_of(member, place):
    wells = place.shape[1]
    slot_of = hot(iota((wells, wells), 0) == wells - 1 - place)
    member_hot = hot(iota((wells, member.shape[1]), 0) == member)
    return mat(slot_of, member_hot)


def phase_kernel(
    nx,
    ny,
    axes,
    amount,
    *rest,
):
    sources, rest = rest[: len(WHOLE)], rest[len(WHOLE) :]
    (
        psi_v,
        terms_v,
        carried_out,
        mob_out,
        store_out,
        edge_x_out,
        edge_ya_out,
        edge_yb_out,
        part_out,
        pcell_out,
        consts_out,
        covol_out,
    ) = rest[:12]
    targets, rest = rest[12 : 12 + len(WHOLE)], rest[12 + len(WHOLE) :]
    amount_v, split_v, field_v, table_v, part_v, small_sems, in_sems, out_sems = rest
    nc = amount.shape[0]
    per = 2
    chunks = nx // per
    half = chunks // 2
    rows = per * ny

    def go(source, target, sem):
        copy = pltpu.make_async_copy(source, target, sem)
        copy.start()
        return copy

    loads, copies = [], {}
    for k, name in enumerate(WHOLE):
        if name in ("press", "flag"):
            span = pl.ds(len(loads) * half * rows, half * rows)
            loads.append(go(amount.at[:, span], amount_v.at[:, span], in_sems.at[len(loads)]))
        copies[name] = go(sources[k], targets[k], small_sems.at[k])

    def arrived(*names):
        return [targets[WHOLE.index(name)] for name in names]

    for copy in [*copies.values(), *loads]:
        copy.wait()

    size = nc * ny
    spread = hot(iota((size, nc), 0) // ny == iota((size, nc), 1))
    same_row = iota((size, size), 0) % ny == iota((size, size), 1) % ny
    mixers = []
    (coupling,) = arrived("coupling")
    for piece in pieces_of(1.0 - coupling[...], 2):
        wide = mat(spread, piece).astype(BF16)
        mixers.append(jnp.where(same_row, mat_nt(wide, spread), 0.0).astype(BF16))
    mixer = jnp.concatenate([mixers[0], mixers[0], mixers[1]], axis=1)

    crit, attract, slope, covol = arrived("crit", "attract", "slope", "covol")
    for i in range(nc):
        root = jnp.sqrt(jnp.full((SUBLANES, LANES), attract[i], F32))
        kappa = jnp.full((SUBLANES, LANES), slope[i], F32)
        tc = jnp.full((SUBLANES, LANES), crit[i], F32)
        table_v[0, i] = root * (1.0 + kappa)
        table_v[1, i] = root * kappa / jnp.sqrt(tc)
        table_v[2, i] = jnp.full((SUBLANES, LANES), covol[i], F32)

    press, loc, member, place = arrived("press", "loc", "member", "place")
    row_hot, lane_hot = place_hots(loc[...], nx * ny)
    lane_hot = hot(lane_hot)

    def cells_of(field, count):
        found = mat_hot(field, lane_hot, count)
        return jnp.sum(jnp.where(row_hot, found, 0.0), axis=0, keepdims=True)

    p_cell = cells_of(press[...], 3)
    pcell_out[...] = p_cell
    slot_hot = slot_hot_of(member[...], place[...]).astype(BF16)
    (heat,) = arrived("heat")

    shape3 = (ny // SUBLANES, SUBLANES, LANES)
    root_t = [jnp.sqrt(heat[pl.ds(x * ny, ny)].reshape(shape3)) for x in range(nx)]
    for x in range(nx):
        span, lanes = pl.ds(x * ny, ny), pl.ds(x * LANES, LANES)
        total = jnp.zeros(shape3, F32)
        volume = jnp.zeros(shape3, F32)
        for i in range(nc):
            o = amount_v[i, span].reshape(shape3)
            v = jnp.abs(table_v[0, i] - table_v[1, i] * root_t[x]) * o
            total += o
            volume += table_v[2, i] * o
            high, low = pieces_of(v.reshape(ny, LANES), 2)
            split_v[pl.ds(i * ny, ny), lanes] = high
            split_v[pl.ds(size + i * ny, ny), lanes] = low
            split_v[pl.ds(2 * size + i * ny, ny), lanes] = high
        field_v[0, span] = total.reshape(ny, LANES)
        field_v[1, span] = volume.reshape(ny, LANES)
    for c in range(chunks):
        mixed = mat(mixer, split_v[:, pl.ds(c * per * LANES, per * LANES)])
        for k in range(per):
            x = c * per + k
            span = pl.ds(x * ny, ny)
            total = jnp.zeros(shape3, F32)
            for i in range(nc):
                m = mixed[i * ny : (i + 1) * ny, k * LANES : (k + 1) * LANES].reshape(shape3)
                psi = jnp.abs(table_v[0, i] - table_v[1, i] * root_t[x]) * m
                total += amount_v[i, span].reshape(shape3) * psi
                psi_v[i, span] = psi.reshape(ny, LANES)
            field_v[2, span] = total.reshape(ny, LANES)

    flag, visc, trans, inject = arrived("flag", "visc", "trans", "inject")
    states = []
    for h in range(2):
        span = pl.ds(h * half * rows, half * rows)
        p, t = press[span], heat[span]
        liquid = flag[span] == 1
        r = inverse(field_v[0, span])
        rt = inverse(t)
        ratio_pt = p * rt
        beta = field_v[1, span] * r
        gr = ratio_pt * rt * r
        big_a = gr * r * field_v[2, span]
        big_b = ratio_pt * beta
        z = jnp.where(liquid, big_b + 0.01, 1.0 + big_b)
        c1 = big_a - 3.0 * big_b * big_b - 2.0 * big_b
        c0 = big_b * big_b + big_b * big_b * big_b - big_a * big_b
        states.append([z, big_b, big_b + 0.01, big_b - 1.0, c1, c0])
        field_v[1, span] = inverse(beta)
        field_v[3, span] = r
        terms_v[0, span] = ratio_pt
        terms_v[1, span] = 0.5 * big_a
        terms_v[2, span] = gr
    for _ in range(NEWT):
        for state in states:
            z, _, floor, c2, c1, c0 = state
            near = z + c2
            value = (near * z + c1) * z + c0
            incline = (near + near + z) * z + c1
            state[0] = jnp.maximum(z - value * inverse(jnp.maximum(incline, 0.1)), floor)
    for h, (z, big_b, *_) in enumerate(states):
        span = pl.ds(h * half * rows, half * rows)
        ratio_pt, gr = terms_v[0, span], terms_v[2, span]
        log_ratio = jnp.log(
            (z + (1.0 + ROOT_TWO) * big_b) * inverse(z + (1.0 - ROOT_TWO) * big_b)
        )
        lb = log_ratio * inverse(ROOT_TWO * big_b)
        mob = ratio_pt * inverse(z * jnp.where(flag[span] == 1, visc[1], visc[0]))
        mob_out[span] = mob
        field_v[3, span] = mob * field_v[3, span]
        terms_v[0, span] = jnp.log(z - big_b)
        terms_v[1, span] = (z - 1.0 + terms_v[1, span] * lb) * field_v[1, span]
        terms_v[2, span] = gr * lb
    seg, strength, own_press, perm = arrived("seg", "strength", "own_press", "perm")
    weight = strength[...] * cells_of(mob_out[...], 2)
    segments = own_press.shape[1]
    lanes = iota((LANES, loc.shape[1]), 0)
    shift = hot(iota((segments, LANES), 0) + 2 * segments == iota((segments, LANES), 1))
    sums = jnp.where(lanes == seg[...], weight, 0.0)
    sums += jnp.where(lanes == seg[...] + segments, weight * (p_cell - 1.0), 0.0)
    sums = sum(mat_nt(slot_hot, piece) for piece in pieces_of(sums, 2))
    sums += mat_hot(own_press[...], shift)
    part_v[...] = sums
    part_copy = go(part_v, part_out, out_sems.at[0])

    (pore,) = arrived("pore")
    store_out[...] = pore[...] * jnp.where(flag[...] == 1, visc[1], visc[0])
    for x in range(nx):
        span = pl.ds(x * ny, ny)
        mr = field_v[3, span]
        for i in range(nc):
            carried_out[i, pl.ds(MARGIN + x * ny, ny)] = mr * amount_v[i, span]

    total = sum(inject[i] for i in range(nc))
    share = 1.0 / jnp.full((SUBLANES, LANES), total, F32)
    for i in range(nc):
        consts_out[i] = inject[i] * share
        covol_out[pl.ds(i, 1)] = jnp.full((1, LANES), covol[i], F32)
    for k in range(3):
        consts_out[nc + k] = jnp.full((SUBLANES, LANES), trans[k], F32)

    odd_g = lax.axis_index(axes[0]) % 2 == 1
    odd_s = lax.axis_index(axes[1]) % 2 == 1
    for k in range(edge_x_out.shape[0]):
        at_low = odd_g if k == 0 else jnp.logical_not(odd_g)
        start = pl.multiple_of(jnp.where(at_low, 0, (nx - 1) * ny), ny)
        for i in range(nc):
            edge_x_out[k, i] = carried_out[i, pl.ds(start + MARGIN, ny)]
        edge_x_out[k, nc] = press[pl.ds(start, ny)]
        edge_x_out[k, nc + 1] = perm[pl.ds(start, ny)]
    for i in range(nc + 2):
        source = carried_out.at[i] if i < nc else press if i == nc else perm
        skip = MARGIN if i < nc else 0
        low = source[pl.ds(skip, nx, stride=ny)]
        high = source[pl.ds(skip + ny - 1, nx, stride=ny)]
        edge_ya_out[i] = jnp.where(odd_s, low, high)
        edge_yb_out[i] = jnp.where(odd_s, high, low)
    part_copy.wait()


def fugacity_kernel(ny, psi, terms, covol, lnphi_out, lnphi_v, sems):
    nc, rows, _ = psi.shape
    parts = sems.shape[0]
    stores = []
    for part in range(parts):
        for x in range(part * rows // parts // ny, (part + 1) * rows // parts // ny):
            span = pl.ds(x * ny, ny)
            e0, e1, e2 = (terms[k, span] for k in range(3))
            for i in range(nc):
                value = covol[pl.ds(i, 1)] * e1 - e0 - psi[i, span] * e2
                lnphi_v[i, span] = value.astype(BF16)
        span = pl.ds(part * rows // parts, rows // parts)
        copy = pltpu.make_async_copy(lnphi_v.at[:, span], lnphi_out.at[:, span], sems.at[part])
        copy.start()
        stores.append(copy)
    for copy in stores:
        copy.wait()


def flux_kernel(
    nx,
    ny,
    axes,
    many_x,
    carried,
    press,
    perm,
    store,
    old_in,
    mob,
    edge_ya,
    edge_yb,
    well_rows,
    loc,
    member,
    seg,
    strength,
    place,
    pcell,
    consts,
    own_press,
    order,
    exit_press,
    friction,
    *rest,
):
    edge_x, rest = rest[:many_x], rest[many_x:]
    resid_out, well_out, old, y_v, res_v, well_v, in_sems, out_sems = rest
    nc = carried.shape[0]
    loads = []
    for x in range(nx):
        span = pl.ds(x * ny, ny)
        copy = pltpu.make_async_copy(old_in.at[:, span], old.at[:, span], in_sems.at[x])
        copy.start()
        loads.append(copy)

    def send(x):
        rows = pl.ds(x * ny, ny)
        copy = pltpu.make_async_copy(res_v.at[:, rows], resid_out.at[:, rows], out_sems.at[x])
        copy.start()
        stores.append(copy)
    g, s = lax.axis_index(axes[0]), lax.axis_index(axes[1])
    ng, ns = lax.axis_size(axes[0]), lax.axis_size(axes[1])
    odd_g, odd_s = g % 2 == 1, s % 2 == 1
    has_low_y, has_high_y = s > 0, s < ns - 1
    has_low_x, has_high_x = g > 0, g < ng - 1

    for i in range(nc + 2):
        a, b = edge_ya[i], edge_yb[i]
        low, high = jnp.where(odd_s, a, b), jnp.where(odd_s, b, a)
        if i == nc + 1:
            low, high = jnp.where(has_low_y, low, 0.0), jnp.where(has_high_y, high, 0.0)
        y_v[0, i] = low
        y_v[1, i] = high

    def side_x(i, high):
        if many_x == 1:
            return edge_x[0][i]
        return jnp.where(odd_g != high, edge_x[0][i], edge_x[1][i])

    row_hot, lane_hot = place_hots(loc[...], nx * ny)
    slot_hot = slot_hot_of(member[...], place[...])
    segments = own_press.shape[1]
    gathered = well_rows[...]
    seg_hot = hot(iota((LANES, loc.shape[1]), 0) == seg[...] + 2 * segments)
    p_seg = jnp.sum(mat_hot(gathered, seg_hot) * slot_hot, axis=0, keepdims=True)
    push = strength[...] * (pcell[...] - p_seg)
    flows = jnp.concatenate(
        [
            jnp.where(row_hot, jnp.maximum(push, 0.0), 0.0),
            jnp.where(row_hot, jnp.minimum(push, 0.0), 0.0),
        ],
        axis=0,
    )
    lane_hot = hot(lane_hot)
    spread = sum(mat_nt(piece, lane_hot) for piece in pieces_of(flows, 2))

    own = jnp.sum(gathered, axis=0, keepdims=True)
    well_p = own_press[...]
    rate = own[:, segments : 2 * segments] - (well_p - 1.0) * own[:, :segments]
    order_hot = hot(iota((segments, segments), 0) == order[...])
    both = mat_hot(jnp.concatenate([rate, well_p], axis=0), order_hot)
    upper = hot(iota((segments, segments), 0) <= iota((segments, segments), 1))
    running = mat_hot(both[0:1], upper)
    press_ord = both[1:2]
    after = hot(iota((segments, segments), 0) == iota((segments, segments), 1) + 1)
    last = iota((1, segments), 1) == segments - 1
    nexts = jnp.where(last, exit_press[0], mat_hot(press_ord, after))
    res_ord = press_ord - nexts - friction[0] * running * jnp.abs(running)
    well_v[...] = sum(mat_nt(piece, order_hot) for piece in pieces_of(res_ord, 3))
    stores = [pltpu.make_async_copy(well_v, well_out, out_sems.at[nx])]
    stores[0].start()

    lane = iota((ny, LANES), 1)
    row = iota((ny, LANES), 0)
    first, final = row == 0, row == ny - 1

    def const(k):
        return jnp.concatenate([consts[k]] * (ny // SUBLANES), axis=0)

    for x in range(nx):
        rows = pl.ds(x * ny, ny)
        p_a, k_a = press[rows], perm[rows]
        twice_k = 2.0 * k_a

        def face(p_b, k_b, axis):
            t = const(nc + axis) * (twice_k * k_b) * inverse(k_a + k_b)
            flow = t * (p_a - p_b)
            return jnp.maximum(flow, 0.0), jnp.minimum(flow, 0.0)

        def other_x(field, i, high):
            at = x + 1 if high else x - 1
            return field[pl.ds(at * ny, ny)] if 0 <= at < nx else side_x(i, high)

        def other_y(field, i, high):
            if high:
                return jnp.where(final, y_v[1, i, pl.ds(x, 1)], pltpu.roll(field, ny - 1, 0))
            return jnp.where(first, y_v[0, i, pl.ds(x, 1)], pltpu.roll(field, 1, 0))

        centre = store[rows] + spread[x * ny : (x + 1) * ny]
        ins = []
        for high in (True, False):
            p_b, k_b = other_x(press, nc, high), other_x(perm, nc + 1, high)
            if x == nx - 1 and high:
                k_b = jnp.where(has_high_x, k_b, 0.0)
            if x == 0 and not high:
                k_b = jnp.where(has_low_x, k_b, 0.0)
            ins.append(face(p_b, k_b, 0))
        for high in (True, False):
            ins.append(face(other_y(p_a, nc, high), other_y(k_a, nc + 1, high), 1))
        for shift, edge in ((LANES - 1, LANES - 1), (1, 0)):
            k_b = jnp.where(lane == edge, 0.0, pltpu.roll(k_a, shift, 1))
            ins.append(face(pltpu.roll(p_a, shift, 1), k_b, 2))
        for out, _ in ins:
            centre += out
        ins = [into for _, into in ins]
        pushed = mob[rows] * spread[(nx + x) * ny : (nx + x + 1) * ny]
        if x == nx // 2:
            for load in loads:
                load.wait()
            for before in range(x):
                span = pl.ds(before * ny, ny)
                for i in range(nc):
                    res_v[i, span] = res_v[i, span] - old[i, span]
                send(before)
        for i in range(nc):
            base = MARGIN + x * ny
            c = carried[i, pl.ds(base, ny)]
            value = centre * c + const(i) * pushed
            if x >= nx // 2:
                value -= old[i, rows]
            for k, high in ((0, True), (1, False)):
                at = x + 1 if high else x - 1
                inside = 0 <= at < nx
                c_b = carried[i, pl.ds(MARGIN + at * ny, ny)] if inside else side_x(i, high)
                value += ins[k] * c_b
            up, down = carried[i, pl.ds(base + 1, ny)], carried[i, pl.ds(base - 1, ny)]
            value += ins[2] * jnp.where(final, y_v[1, i, pl.ds(x, 1)], up)
            value += ins[3] * jnp.where(first, y_v[0, i, pl.ds(x, 1)], down)
            value += ins[4] * pltpu.roll(c, LANES - 1, 1)
            value += ins[5] * pltpu.roll(c, 1, 1)
            res_v[i, rows] = value
        if x >= nx // 2:
            send(x)
    for copy in stores:
        copy.wait()


def swaps_of(count, other):
    pairs = [(i, i + 1) for i in range(1 if other else 0, count - 1, 2)]
    return pairs + [(b, a) for a, b in pairs]


def other_swaps_of(groups, count):
    swaps = [(g * count + a, g * count + b) for g in range(groups) for a, b in swaps_of(count, True)]
    ends = [(g * count + e, (g ^ 1) * count + e) for g in range(groups) for e in (0, count - 1)]
    return sorted(swaps + ends)


def per_device(
    amount,
    press,
    heat,
    flag,
    perm,
    pore,
    old,
    trans,
    visc,
    crit,
    attract,
    covol,
    slope,
    coupling,
    inject,
    locale,
    member,
    seg,
    strength,
    place,
    order,
    seg_press,
    exit_press,
    friction,
):
    axes = ("grp", "sub")
    nc, nx, ny, nz = amount.shape
    ng, ns = lax.axis_size("grp"), lax.axis_size("sub")
    rows = nx * ny
    perfs = locale.shape[0]
    wells, segments = place.shape[1], seg_press.shape[1]
    flat = lambda a: a.reshape(a.shape[:-3] + (rows, nz))
    line = lambda a: a.reshape(1, perfs)
    vm = pl.BlockSpec(memory_space=pltpu.VMEM)
    sm = pl.BlockSpec(memory_space=pltpu.SMEM)
    hbm = pl.BlockSpec(memory_space=pltpu.HBM)
    many_x = 1 if ng == 2 else 2

    amount, old = flat(amount), flat(old)
    press, heat, flag, perm, pore = (flat(a) for a in (press, heat, flag, perm, pore))
    locale, member, seg, strength = (line(a) for a in (locale, member, seg, strength))

    sources = (
        coupling, crit, attract, slope, covol, heat, press, locale, member, place,
        flag, visc, trans, inject, seg, strength, seg_press, perm, pore,
    )
    kept = [
        pltpu.SMEM(a.shape, a.dtype) if a.ndim == 1 else pltpu.VMEM(a.shape, a.dtype)
        for a in sources
    ]
    in_hbm = lambda a: pltpu.with_memory_space_constraint(a, pltpu.HBM)

    psi, terms, carried, mob, store, edge_x, edge_ya, edge_yb, part, pcell, consts, covols = pl.pallas_call(
        functools.partial(phase_kernel, nx, ny, axes),
        out_shape=(
            jax.ShapeDtypeStruct((nc, rows, nz), F32),
            jax.ShapeDtypeStruct((3, rows, nz), F32),
            jax.ShapeDtypeStruct((nc, rows + 2 * MARGIN, nz), F32),
            jax.ShapeDtypeStruct((rows, nz), F32),
            jax.ShapeDtypeStruct((rows, nz), F32),
            jax.ShapeDtypeStruct((many_x, nc + 2, ny, nz), F32),
            jax.ShapeDtypeStruct((nc + 2, nx, nz), F32),
            jax.ShapeDtypeStruct((nc + 2, nx, nz), F32),
            jax.ShapeDtypeStruct((wells, LANES), F32),
            jax.ShapeDtypeStruct((1, perfs), F32),
            jax.ShapeDtypeStruct((nc + 3, SUBLANES, LANES), F32),
            jax.ShapeDtypeStruct((nc, LANES), F32),
        ),
        in_specs=[hbm] * (1 + len(sources)),
        out_specs=(vm,) * 8 + (hbm,) + (vm,) * 3,
        scratch_shapes=[
            *kept,
            pltpu.VMEM((nc, rows, nz), F32),
            pltpu.VMEM((3 * nc * ny, nx * nz), BF16),
            pltpu.VMEM((4, rows, nz), F32),
            pltpu.VMEM((3, nc, SUBLANES, LANES), F32),
            pltpu.VMEM((wells, LANES), F32),
            pltpu.SemaphoreType.DMA((len(sources),)),
            pltpu.SemaphoreType.DMA((2,)),
            pltpu.SemaphoreType.DMA((1,)),
        ],
        compiler_params=pltpu.CompilerParams(vmem_limit_bytes=VMEM_LIMIT),
        name="phase",
    )(in_hbm(amount), *(in_hbm(a) for a in sources))

    got_ya = lax.ppermute(edge_ya, "sub", swaps_of(ns, False))
    got_x = [lax.ppermute(edge_x[k], "grp", swaps_of(ng, k == 1)) for k in range(many_x)]
    got_yb = lax.ppermute(edge_yb, axes, other_swaps_of(ng, ns))
    backward = [list(range(ns))[::-1]]
    well_rows = lax.all_to_all(
        part, "sub", split_axis=0, concat_axis=0, axis_index_groups=backward, tiled=True
    )

    lnphi = pl.pallas_call(
        functools.partial(fugacity_kernel, ny),
        out_shape=jax.ShapeDtypeStruct((nc, rows, nz), BF16),
        in_specs=[vm] * 3,
        out_specs=hbm,
        scratch_shapes=[pltpu.VMEM((nc, rows, nz), BF16), pltpu.SemaphoreType.DMA((4,))],
        compiler_params=pltpu.CompilerParams(vmem_limit_bytes=VMEM_LIMIT),
        cost_estimate=pl.CostEstimate(
            flops=8 * nc * rows * nz, bytes_accessed=256 * nc * rows * nz, transcendentals=0
        ),
        name="fugacity",
    )(psi, terms, covols)

    resid, well = pl.pallas_call(
        functools.partial(flux_kernel, nx, ny, axes, many_x),
        out_shape=(
            jax.ShapeDtypeStruct((nc, rows, nz), F32),
            jax.ShapeDtypeStruct((1, segments), F32),
        ),
        in_specs=[vm] * 4 + [hbm] + [vm] * 13 + [sm] * 2 + [vm] * many_x,
        out_specs=(hbm, hbm),
        scratch_shapes=[
            pltpu.VMEM((nc, rows, nz), F32),
            pltpu.VMEM((2, nc + 2, nx, nz), F32),
            pltpu.VMEM((nc, rows, nz), F32),
            pltpu.VMEM((1, segments), F32),
            pltpu.SemaphoreType.DMA((nx,)),
            pltpu.SemaphoreType.DMA((nx + 1,)),
        ],
        compiler_params=pltpu.CompilerParams(vmem_limit_bytes=VMEM_LIMIT),
        name="flux",
    )(
        carried, press, perm, store, in_hbm(old), mob, got_ya, got_yb, well_rows,
        locale, member, seg, strength, place, pcell,
        consts, seg_press, order, exit_press, friction, *got_x,
    )
    block = (nc, nx, ny, nz)
    return resid.reshape(block), lnphi.reshape(block), well


def solution(mesh):
    cells, parts = P("grp", "sub", None), P(None, "grp", "sub", None)
    listed = P(("grp", "sub"))
    row = P(("grp", "sub"), None)
    in_specs = (
        (parts,) + (cells,) * 5 + (parts,) + (P(),) * 8
        + (listed, row, listed, listed, P("grp", None), row, row, listed, listed)
    )
    return jax.shard_map(
        per_device, mesh=mesh, in_specs=in_specs, out_specs=(parts, parts, row), check_vma=False
    )
```

```python
import functools
import math

import jax
import jax.numpy as jnp
from jax import lax
from jax.experimental import pallas as pl
from jax.experimental.pallas import tpu as pltpu
from jax.sharding import PartitionSpec as P

NEWT = 8
ROOT_TWO = math.sqrt(2.0)
LANES = 128
SUBLANES = 8
F32 = jnp.float32
BF16 = jnp.bfloat16
VMEM_LIMIT = 48 * 1024 * 1024
MARGIN = 8
WHOLE = (
    "coupling", "crit", "attract", "slope", "covol", "heat", "press", "loc", "member", "place",
    "flag", "visc", "trans", "inject", "seg", "strength", "own_press", "perm", "pore",
)


def iota(shape, dim):
    return lax.broadcasted_iota(jnp.int32, shape, dim)


def pieces_of(x, count):
    out = []
    for _ in range(count):
        piece = x.astype(BF16)
        out.append(piece)
        x = x - piece.astype(F32)
    return out


def mat(a, b):
    return lax.dot_general(a, b, (((1,), (0,)), ((), ())), preferred_element_type=F32)


def mat_nt(a, b):
    return lax.dot_general(a, b, (((1,), (1,)), ((), ())), preferred_element_type=F32)


def mat_hot(x, hot, count=3):
    return sum(mat(piece, hot) for piece in pieces_of(x, count))


def inverse(x):
    r = pl.reciprocal(x, approx=True)
    return r * (2.0 - x * r)


def hot(cond):
    return jnp.where(cond, 1.0, 0.0).astype(BF16)


def place_hots(loc, rows):
    n = loc.shape[1]
    row_hot = iota((rows, n), 0) == loc // LANES
    lane_hot = iota((LANES, n), 0) == loc % LANES
    return row_hot, lane_hot


def member_at(row, count):
    return (count - 1 - row) ^ 2


def slot_hot_of(member, place):
    wells = place.shape[1]
    slot_of = hot(member_at(iota((wells, wells), 0), wells) == place)
    member_hot = hot(iota((wells, member.shape[1]), 0) == member)
    return mat(slot_of, member_hot)


def phase_kernel(
    nx,
    ny,
    axes,
    amount,
    *rest,
):
    sources, rest = rest[: len(WHOLE)], rest[len(WHOLE) :]
    (
        psi_v,
        terms_v,
        carried_out,
        mob_out,
        store_out,
        edge_x_out,
        edge_ya_out,
        edge_yb_out,
        part_out,
        pcell_out,
        consts_out,
        covol_out,
    ) = rest[:12]
    targets, rest = rest[12 : 12 + len(WHOLE)], rest[12 + len(WHOLE) :]
    amount_v, split_v, field_v, table_v, part_v, small_sems, in_sems, out_sems = rest
    nc = amount.shape[0]
    per = 2
    chunks = nx // per
    half = chunks // 2
    rows = per * ny

    def go(source, target, sem):
        copy = pltpu.make_async_copy(source, target, sem)
        copy.start()
        return copy

    loads, copies = [], {}
    for k, name in enumerate(WHOLE):
        if name in ("press", "flag"):
            span = pl.ds(len(loads) * half * rows, half * rows)
            loads.append(go(amount.at[:, span], amount_v.at[:, span], in_sems.at[len(loads)]))
        copies[name] = go(sources[k], targets[k], small_sems.at[k])

    def arrived(*names):
        return [targets[WHOLE.index(name)] for name in names]

    for copy in [*copies.values(), *loads]:
        copy.wait()

    size = nc * ny
    spread = hot(iota((size, nc), 0) // ny == iota((size, nc), 1))
    same_row = iota((size, size), 0) % ny == iota((size, size), 1) % ny
    mixers = []
    (coupling,) = arrived("coupling")
    for piece in pieces_of(1.0 - coupling[...], 2):
        wide = mat(spread, piece).astype(BF16)
        mixers.append(jnp.where(same_row, mat_nt(wide, spread), 0.0).astype(BF16))
    mixer = jnp.concatenate([mixers[0], mixers[0], mixers[1]], axis=1)

    crit, attract, slope, covol = arrived("crit", "attract", "slope", "covol")
    for i in range(nc):
        root = jnp.sqrt(jnp.full((SUBLANES, LANES), attract[i], F32))
        kappa = jnp.full((SUBLANES, LANES), slope[i], F32)
        tc = jnp.full((SUBLANES, LANES), crit[i], F32)
        table_v[0, i] = root * (1.0 + kappa)
        table_v[1, i] = root * kappa / jnp.sqrt(tc)
        table_v[2, i] = jnp.full((SUBLANES, LANES), covol[i], F32)

    press, loc, member, place = arrived("press", "loc", "member", "place")
    row_hot, lane_hot = place_hots(loc[...], nx * ny)
    lane_hot = hot(lane_hot)

    def cells_of(field, count):
        found = mat_hot(field, lane_hot, count)
        return jnp.sum(jnp.where(row_hot, found, 0.0), axis=0, keepdims=True)

    p_cell = cells_of(press[...], 3)
    pcell_out[...] = p_cell
    slot_hot = slot_hot_of(member[...], place[...])
    (heat,) = arrived("heat")

    shape3 = (ny // SUBLANES, SUBLANES, LANES)
    root_t = [jnp.sqrt(heat[pl.ds(x * ny, ny)].reshape(shape3)) for x in range(nx)]
    for x in range(nx):
        span, lanes = pl.ds(x * ny, ny), pl.ds(x * LANES, LANES)
        total = jnp.zeros(shape3, F32)
        volume = jnp.zeros(shape3, F32)
        for i in range(nc):
            o = amount_v[i, span].reshape(shape3)
            v = jnp.abs(table_v[0, i] - table_v[1, i] * root_t[x]) * o
            total += o
            volume += table_v[2, i] * o
            high, low = pieces_of(v.reshape(ny, LANES), 2)
            split_v[pl.ds(i * ny, ny), lanes] = high
            split_v[pl.ds(size + i * ny, ny), lanes] = low
            split_v[pl.ds(2 * size + i * ny, ny), lanes] = high
        field_v[0, span] = total.reshape(ny, LANES)
        field_v[1, span] = volume.reshape(ny, LANES)
    for c in range(chunks):
        mixed = mat(mixer, split_v[:, pl.ds(c * per * LANES, per * LANES)])
        for k in range(per):
            x = c * per + k
            span = pl.ds(x * ny, ny)
            total = jnp.zeros(shape3, F32)
            for i in range(nc):
                m = mixed[i * ny : (i + 1) * ny, k * LANES : (k + 1) * LANES].reshape(shape3)
                psi = jnp.abs(table_v[0, i] - table_v[1, i] * root_t[x]) * m
                total += amount_v[i, span].reshape(shape3) * psi
                psi_v[i, span] = psi.reshape(ny, LANES)
            field_v[2, span] = total.reshape(ny, LANES)

    flag, visc, trans, inject = arrived("flag", "visc", "trans", "inject")
    states = []
    for h in range(2):
        span = pl.ds(h * half * rows, half * rows)
        p, t = press[span], heat[span]
        liquid = flag[span] == 1
        r = inverse(field_v[0, span])
        rt = inverse(t)
        ratio_pt = p * rt
        beta = field_v[1, span] * r
        gr = ratio_pt * rt * r
        big_a = gr * r * field_v[2, span]
        big_b = ratio_pt * beta
        z = jnp.where(liquid, big_b + 0.01, 1.0 + big_b)
        c1 = big_a - 3.0 * big_b * big_b - 2.0 * big_b
        c0 = big_b * big_b + big_b * big_b * big_b - big_a * big_b
        states.append([z, big_b, big_b + 0.01, big_b - 1.0, c1, c0])
        field_v[1, span] = inverse(beta)
        field_v[3, span] = r
        terms_v[0, span] = ratio_pt
        terms_v[1, span] = 0.5 * big_a
        terms_v[2, span] = gr
    for _ in range(NEWT):
        for state in states:
            z, _, floor, c2, c1, c0 = state
            near = z + c2
            value = (near * z + c1) * z + c0
            incline = (near + near + z) * z + c1
            state[0] = jnp.maximum(z - value * inverse(jnp.maximum(incline, 0.1)), floor)
    for h, (z, big_b, *_) in enumerate(states):
        span = pl.ds(h * half * rows, half * rows)
        ratio_pt, gr = terms_v[0, span], terms_v[2, span]
        log_ratio = jnp.log(
            (z + (1.0 + ROOT_TWO) * big_b) * inverse(z + (1.0 - ROOT_TWO) * big_b)
        )
        lb = log_ratio * inverse(ROOT_TWO * big_b)
        mob = ratio_pt * inverse(z * jnp.where(flag[span] == 1, visc[1], visc[0]))
        mob_out[span] = mob
        field_v[3, span] = mob * field_v[3, span]
        terms_v[0, span] = jnp.log(z - big_b)
        terms_v[1, span] = (z - 1.0 + terms_v[1, span] * lb) * field_v[1, span]
        terms_v[2, span] = gr * lb
    seg, strength, own_press, perm = arrived("seg", "strength", "own_press", "perm")
    weight = strength[...] * cells_of(mob_out[...], 2)
    segments = own_press.shape[1]
    lanes = iota((LANES, loc.shape[1]), 0)
    shift = hot(iota((segments, LANES), 0) + 2 * segments == iota((segments, LANES), 1))
    sums = mat_hot(own_press[...], shift)
    for k, value in enumerate((weight, weight * (p_cell - 1.0))):
        seg_hot = hot(lanes == seg[...] + k * segments)
        for piece in pieces_of(slot_hot * value, 2):
            sums += mat_nt(piece, seg_hot)
    part_v[...] = sums
    part_copy = go(part_v, part_out, out_sems.at[0])

    (pore,) = arrived("pore")
    store_out[...] = pore[...] * jnp.where(flag[...] == 1, visc[1], visc[0])
    for x in range(nx):
        span = pl.ds(x * ny, ny)
        mr = field_v[3, span]
        for i in range(nc):
            carried_out[i, pl.ds(MARGIN + x * ny, ny)] = mr * amount_v[i, span]

    total = sum(inject[i] for i in range(nc))
    share = 1.0 / jnp.full((SUBLANES, LANES), total, F32)
    for i in range(nc):
        consts_out[i] = inject[i] * share
        covol_out[pl.ds(i, 1)] = jnp.full((1, LANES), covol[i], F32)
    for k in range(3):
        consts_out[nc + k] = jnp.full((SUBLANES, LANES), trans[k], F32)

    odd_g = lax.axis_index(axes[0]) % 2 == 1
    odd_s = lax.axis_index(axes[1]) % 2 == 1
    for k in range(edge_x_out.shape[0]):
        at_low = odd_g if k == 0 else jnp.logical_not(odd_g)
        start = pl.multiple_of(jnp.where(at_low, 0, (nx - 1) * ny), ny)
        for i in range(nc):
            edge_x_out[k, i] = carried_out[i, pl.ds(start + MARGIN, ny)]
        edge_x_out[k, nc] = press[pl.ds(start, ny)]
        edge_x_out[k, nc + 1] = perm[pl.ds(start, ny)]
    for i in range(nc + 2):
        source = carried_out.at[i] if i < nc else press if i == nc else perm
        skip = MARGIN if i < nc else 0
        low = source[pl.ds(skip, nx, stride=ny)]
        high = source[pl.ds(skip + ny - 1, nx, stride=ny)]
        edge_ya_out[i] = jnp.where(odd_s, low, high)
        edge_yb_out[i] = jnp.where(odd_s, high, low)
    part_copy.wait()


def fugacity_kernel(ny, psi, terms, covol, lnphi_out, lnphi_v, sems):
    nc, rows, _ = psi.shape
    parts = sems.shape[0]
    stores = []
    for part in range(parts):
        for x in range(part * rows // parts // ny, (part + 1) * rows // parts // ny):
            span = pl.ds(x * ny, ny)
            e0, e1, e2 = (terms[k, span] for k in range(3))
            for i in range(nc):
                value = covol[pl.ds(i, 1)] * e1 - e0 - psi[i, span] * e2
                lnphi_v[i, span] = value.astype(BF16)
        span = pl.ds(part * rows // parts, rows // parts)
        copy = pltpu.make_async_copy(lnphi_v.at[:, span], lnphi_out.at[:, span], sems.at[part])
        copy.start()
        stores.append(copy)
    for copy in stores:
        copy.wait()


def flux_kernel(
    nx,
    ny,
    axes,
    many_x,
    carried,
    press,
    perm,
    store,
    old_in,
    mob,
    edge_ya,
    edge_yb,
    well_rows,
    loc,
    member,
    seg,
    strength,
    place,
    pcell,
    consts,
    own_press,
    order,
    exit_press,
    friction,
    *rest,
):
    edge_x, rest = rest[:many_x], rest[many_x:]
    resid_out, well_out, old, y_v, res_v, well_v, in_sems, out_sems = rest
    nc = carried.shape[0]
    loads = []
    for x in range(nx):
        span = pl.ds(x * ny, ny)
        copy = pltpu.make_async_copy(old_in.at[:, span], old.at[:, span], in_sems.at[x])
        copy.start()
        loads.append(copy)
    g, s = lax.axis_index(axes[0]), lax.axis_index(axes[1])
    ng, ns = lax.axis_size(axes[0]), lax.axis_size(axes[1])
    odd_g, odd_s = g % 2 == 1, s % 2 == 1
    has_low_y, has_high_y = s > 0, s < ns - 1
    has_low_x, has_high_x = g > 0, g < ng - 1

    for i in range(nc + 2):
        a, b = edge_ya[i], edge_yb[i]
        low, high = jnp.where(odd_s, a, b), jnp.where(odd_s, b, a)
        if i == nc + 1:
            low, high = jnp.where(has_low_y, low, 0.0), jnp.where(has_high_y, high, 0.0)
        y_v[0, i] = low
        y_v[1, i] = high

    def side_x(i, high):
        if many_x == 1:
            return edge_x[0][i]
        return jnp.where(odd_g != high, edge_x[0][i], edge_x[1][i])

    row_hot, lane_hot = place_hots(loc[...], nx * ny)
    slot_hot = slot_hot_of(member[...], place[...])
    segments = own_press.shape[1]
    gathered = well_rows[...]
    seg_hot = hot(iota((LANES, loc.shape[1]), 0) == seg[...] + 2 * segments)
    p_seg = jnp.sum(mat_hot(gathered, seg_hot) * slot_hot, axis=0, keepdims=True)
    push = strength[...] * (pcell[...] - p_seg)
    flows = jnp.concatenate(
        [
            jnp.where(row_hot, jnp.maximum(push, 0.0), 0.0),
            jnp.where(row_hot, jnp.minimum(push, 0.0), 0.0),
        ],
        axis=0,
    )
    lane_hot = hot(lane_hot)
    spread = sum(mat_nt(piece, lane_hot) for piece in pieces_of(flows, 2))

    own = jnp.sum(gathered, axis=0, keepdims=True)
    well_p = own_press[...]
    rate = own[:, segments : 2 * segments] - (well_p - 1.0) * own[:, :segments]
    order_hot = hot(iota((segments, segments), 0) == order[...])
    both = mat_hot(jnp.concatenate([rate, well_p], axis=0), order_hot)
    upper = hot(iota((segments, segments), 0) <= iota((segments, segments), 1))
    running = mat_hot(both[0:1], upper)
    press_ord = both[1:2]
    after = hot(iota((segments, segments), 0) == iota((segments, segments), 1) + 1)
    last = iota((1, segments), 1) == segments - 1
    nexts = jnp.where(last, exit_press[0], mat_hot(press_ord, after))
    res_ord = press_ord - nexts - friction[0] * running * jnp.abs(running)
    well_v[...] = sum(mat_nt(piece, order_hot) for piece in pieces_of(res_ord, 3))
    stores = [pltpu.make_async_copy(well_v, well_out, out_sems.at[nx])]
    stores[0].start()

    lane = iota((ny, LANES), 1)
    row = iota((ny, LANES), 0)
    first, final = row == 0, row == ny - 1

    def const(k):
        return jnp.concatenate([consts[k]] * (ny // SUBLANES), axis=0)

    for x in range(nx):
        rows = pl.ds(x * ny, ny)
        p_a, k_a = press[rows], perm[rows]
        twice_k = 2.0 * k_a

        def face(p_b, k_b, axis):
            t = const(nc + axis) * (twice_k * k_b) * inverse(k_a + k_b)
            flow = t * (p_a - p_b)
            return jnp.maximum(flow, 0.0), jnp.minimum(flow, 0.0)

        def other_x(field, i, high):
            at = x + 1 if high else x - 1
            return field[pl.ds(at * ny, ny)] if 0 <= at < nx else side_x(i, high)

        def other_y(field, i, high):
            if high:
                return jnp.where(final, y_v[1, i, pl.ds(x, 1)], pltpu.roll(field, ny - 1, 0))
            return jnp.where(first, y_v[0, i, pl.ds(x, 1)], pltpu.roll(field, 1, 0))

        centre = store[rows] + spread[x * ny : (x + 1) * ny]
        ins = []
        for high in (True, False):
            p_b, k_b = other_x(press, nc, high), other_x(perm, nc + 1, high)
            if x == nx - 1 and high:
                k_b = jnp.where(has_high_x, k_b, 0.0)
            if x == 0 and not high:
                k_b = jnp.where(has_low_x, k_b, 0.0)
            ins.append(face(p_b, k_b, 0))
        for high in (True, False):
            ins.append(face(other_y(p_a, nc, high), other_y(k_a, nc + 1, high), 1))
        for shift, edge in ((LANES - 1, LANES - 1), (1, 0)):
            k_b = jnp.where(lane == edge, 0.0, pltpu.roll(k_a, shift, 1))
            ins.append(face(pltpu.roll(p_a, shift, 1), k_b, 2))
        for out, _ in ins:
            centre += out
        ins = [into for _, into in ins]
        pushed = mob[rows] * spread[(nx + x) * ny : (nx + x + 1) * ny]
        loads[x].wait()
        for i in range(nc):
            base = MARGIN + x * ny
            c = carried[i, pl.ds(base, ny)]
            value = centre * c - old[i, rows] + const(i) * pushed
            for k, high in ((0, True), (1, False)):
                at = x + 1 if high else x - 1
                inside = 0 <= at < nx
                c_b = carried[i, pl.ds(MARGIN + at * ny, ny)] if inside else side_x(i, high)
                value += ins[k] * c_b
            up, down = carried[i, pl.ds(base + 1, ny)], carried[i, pl.ds(base - 1, ny)]
            value += ins[2] * jnp.where(final, y_v[1, i, pl.ds(x, 1)], up)
            value += ins[3] * jnp.where(first, y_v[0, i, pl.ds(x, 1)], down)
            value += ins[4] * pltpu.roll(c, LANES - 1, 1)
            value += ins[5] * pltpu.roll(c, 1, 1)
            res_v[i, rows] = value
        copy = pltpu.make_async_copy(res_v.at[:, rows], resid_out.at[:, rows], out_sems.at[x])
        copy.start()
        stores.append(copy)
    for copy in stores:
        copy.wait()


def swaps_of(count, other):
    pairs = [(i, i + 1) for i in range(1 if other else 0, count - 1, 2)]
    return pairs + [(b, a) for a, b in pairs]


def other_swaps_of(groups, count):
    swaps = [(g * count + a, g * count + b) for g in range(groups) for a, b in swaps_of(count, True)]
    ends = [(g * count + e, (g ^ 1) * count + e) for g in range(groups) for e in (0, count - 1)]
    return sorted(swaps + ends)


def per_device(
    amount,
    press,
    heat,
    flag,
    perm,
    pore,
    old,
    trans,
    visc,
    crit,
    attract,
    covol,
    slope,
    coupling,
    inject,
    locale,
    member,
    seg,
    strength,
    place,
    order,
    seg_press,
    exit_press,
    friction,
):
    axes = ("grp", "sub")
    nc, nx, ny, nz = amount.shape
    ng, ns = lax.axis_size("grp"), lax.axis_size("sub")
    rows = nx * ny
    perfs = locale.shape[0]
    wells, segments = place.shape[1], seg_press.shape[1]
    flat = lambda a: a.reshape(a.shape[:-3] + (rows, nz))
    line = lambda a: a.reshape(1, perfs)
    vm = pl.BlockSpec(memory_space=pltpu.VMEM)
    sm = pl.BlockSpec(memory_space=pltpu.SMEM)
    hbm = pl.BlockSpec(memory_space=pltpu.HBM)
    many_x = 1 if ng == 2 else 2

    amount, old = flat(amount), flat(old)
    press, heat, flag, perm, pore = (flat(a) for a in (press, heat, flag, perm, pore))
    locale, member, seg, strength = (line(a) for a in (locale, member, seg, strength))

    sources = (
        coupling, crit, attract, slope, covol, heat, press, locale, member, place,
        flag, visc, trans, inject, seg, strength, seg_press, perm, pore,
    )
    kept = [
        pltpu.SMEM(a.shape, a.dtype) if a.ndim == 1 else pltpu.VMEM(a.shape, a.dtype)
        for a in sources
    ]
    in_hbm = lambda a: pltpu.with_memory_space_constraint(a, pltpu.HBM)

    psi, terms, carried, mob, store, edge_x, edge_ya, edge_yb, part, pcell, consts, covols = pl.pallas_call(
        functools.partial(phase_kernel, nx, ny, axes),
        out_shape=(
            jax.ShapeDtypeStruct((nc, rows, nz), F32),
            jax.ShapeDtypeStruct((3, rows, nz), F32),
            jax.ShapeDtypeStruct((nc, rows + 2 * MARGIN, nz), F32),
            jax.ShapeDtypeStruct((rows, nz), F32),
            jax.ShapeDtypeStruct((rows, nz), F32),
            jax.ShapeDtypeStruct((many_x, nc + 2, ny, nz), F32),
            jax.ShapeDtypeStruct((nc + 2, nx, nz), F32),
            jax.ShapeDtypeStruct((nc + 2, nx, nz), F32),
            jax.ShapeDtypeStruct((wells, LANES), F32),
            jax.ShapeDtypeStruct((1, perfs), F32),
            jax.ShapeDtypeStruct((nc + 3, SUBLANES, LANES), F32),
            jax.ShapeDtypeStruct((nc, LANES), F32),
        ),
        in_specs=[hbm] * (1 + len(sources)),
        out_specs=(vm,) * 8 + (hbm,) + (vm,) * 3,
        scratch_shapes=[
            *kept,
            pltpu.VMEM((nc, rows, nz), F32),
            pltpu.VMEM((3 * nc * ny, nx * nz), BF16),
            pltpu.VMEM((4, rows, nz), F32),
            pltpu.VMEM((3, nc, SUBLANES, LANES), F32),
            pltpu.VMEM((wells, LANES), F32),
            pltpu.SemaphoreType.DMA((len(sources),)),
            pltpu.SemaphoreType.DMA((2,)),
            pltpu.SemaphoreType.DMA((1,)),
        ],
        compiler_params=pltpu.CompilerParams(vmem_limit_bytes=VMEM_LIMIT),
        name="phase",
    )(in_hbm(amount), *(in_hbm(a) for a in sources))

    got_ya = lax.ppermute(edge_ya, "sub", swaps_of(ns, False))
    got_x = [lax.ppermute(edge_x[k], "grp", swaps_of(ng, k == 1)) for k in range(many_x)]
    got_yb = lax.ppermute(edge_yb, axes, other_swaps_of(ng, ns))
    backward = [[member_at(row, ns) for row in range(ns)]]
    well_rows = lax.all_to_all(
        part, "sub", split_axis=0, concat_axis=0, axis_index_groups=backward, tiled=True
    )

    lnphi = pl.pallas_call(
        functools.partial(fugacity_kernel, ny),
        out_shape=jax.ShapeDtypeStruct((nc, rows, nz), BF16),
        in_specs=[vm] * 3,
        out_specs=hbm,
        scratch_shapes=[pltpu.VMEM((nc, rows, nz), BF16), pltpu.SemaphoreType.DMA((4,))],
        compiler_params=pltpu.CompilerParams(vmem_limit_bytes=VMEM_LIMIT),
        cost_estimate=pl.CostEstimate(
            flops=8 * nc * rows * nz, bytes_accessed=256 * nc * rows * nz, transcendentals=0
        ),
        name="fugacity",
    )(psi, terms, covols)

    resid, well = pl.pallas_call(
        functools.partial(flux_kernel, nx, ny, axes, many_x),
        out_shape=(
            jax.ShapeDtypeStruct((nc, rows, nz), F32),
            jax.ShapeDtypeStruct((1, segments), F32),
        ),
        in_specs=[vm] * 4 + [hbm] + [vm] * 13 + [sm] * 2 + [vm] * many_x,
        out_specs=(hbm, hbm),
        scratch_shapes=[
            pltpu.VMEM((nc, rows, nz), F32),
            pltpu.VMEM((2, nc + 2, nx, nz), F32),
            pltpu.VMEM((nc, rows, nz), F32),
            pltpu.VMEM((1, segments), F32),
            pltpu.SemaphoreType.DMA((nx,)),
            pltpu.SemaphoreType.DMA((nx + 1,)),
        ],
        compiler_params=pltpu.CompilerParams(vmem_limit_bytes=VMEM_LIMIT),
        name="flux",
    )(
        carried, press, perm, store, in_hbm(old), mob, got_ya, got_yb, well_rows,
        locale, member, seg, strength, place, pcell,
        consts, seg_press, order, exit_press, friction, *got_x,
    )
    block = (nc, nx, ny, nz)
    return resid.reshape(block), lnphi.reshape(block), well


def solution(mesh):
    cells, parts = P("grp", "sub", None), P(None, "grp", "sub", None)
    listed = P(("grp", "sub"))
    row = P(("grp", "sub"), None)
    in_specs = (
        (parts,) + (cells,) * 5 + (parts,) + (P(),) * 8
        + (listed, row, listed, listed, P("grp", None), row, row, listed, listed)
    )
    return jax.shard_map(
        per_device, mesh=mesh, in_specs=in_specs, out_specs=(parts, parts, row), check_vma=False
    )
```

```python
import functools
import math

import jax
import jax.numpy as jnp
from jax import lax
from jax.experimental import pallas as pl
from jax.experimental.pallas import tpu as pltpu
from jax.sharding import PartitionSpec as P

NEWT = 8
ROOT_TWO = math.sqrt(2.0)
LANES = 128
SUBLANES = 8
F32 = jnp.float32
BF16 = jnp.bfloat16
VMEM_LIMIT = 48 * 1024 * 1024
MARGIN = 8
WHOLE = (
    "coupling", "crit", "attract", "slope", "covol", "heat", "press", "loc", "member", "place",
    "flag", "visc", "trans", "inject", "seg", "strength", "own_press", "perm",
)


def iota(shape, dim):
    return lax.broadcasted_iota(jnp.int32, shape, dim)


def pieces_of(x, count):
    out = []
    for _ in range(count):
        piece = x.astype(BF16)
        out.append(piece)
        x = x - piece.astype(F32)
    return out


def mat(a, b):
    return lax.dot_general(a, b, (((1,), (0,)), ((), ())), preferred_element_type=F32)


def mat_nt(a, b):
    return lax.dot_general(a, b, (((1,), (1,)), ((), ())), preferred_element_type=F32)


def mat_hot(x, hot, count=3):
    return sum(mat(piece, hot) for piece in pieces_of(x, count))


def inverse(x):
    r = pl.reciprocal(x, approx=True)
    return r * (2.0 - x * r)


def hot(cond):
    return jnp.where(cond, 1.0, 0.0).astype(BF16)


def place_hots(loc, rows):
    n = loc.shape[1]
    row_hot = iota((rows, n), 0) == loc // LANES
    lane_hot = iota((LANES, n), 0) == loc % LANES
    return row_hot, lane_hot


def slot_hot_of(member, place):
    wells = place.shape[1]
    slot_of = hot(iota((wells, wells), 0) == wells - 1 - place)
    member_hot = hot(iota((wells, member.shape[1]), 0) == member)
    return mat(slot_of, member_hot)


def phase_kernel(
    nx,
    ny,
    axes,
    amount,
    *rest,
):
    sources, rest = rest[: len(WHOLE)], rest[len(WHOLE) :]
    (
        lnphi_out,
        carried_out,
        mob_out,
        edge_x_out,
        edge_ya_out,
        edge_yb_out,
        part_out,
        pcell_out,
        consts_out,
    ) = rest[:9]
    targets, rest = rest[9 : 9 + len(WHOLE)], rest[9 + len(WHOLE) :]
    amount_v, split_v, psi_v, lnphi_v, field_v, terms_v, table_v, part_v, small_sems, in_sems, out_sems = rest
    nc = amount.shape[0]
    per = 2
    chunks = nx // per
    half = chunks // 2
    rows = per * ny

    def go(source, target, sem):
        copy = pltpu.make_async_copy(source, target, sem)
        copy.start()
        return copy

    loads, copies = [], {}
    for k, name in enumerate(WHOLE):
        if name in ("press", "flag"):
            span = pl.ds(len(loads) * half * rows, half * rows)
            loads.append(go(amount.at[:, span], amount_v.at[:, span], in_sems.at[len(loads)]))
        copies[name] = go(sources[k], targets[k], small_sems.at[k])

    def arrived(*names):
        return [targets[WHOLE.index(name)] for name in names]

    for copy in [*copies.values(), *loads]:
        copy.wait()

    size = nc * ny
    spread = hot(iota((size, nc), 0) // ny == iota((size, nc), 1))
    same_row = iota((size, size), 0) % ny == iota((size, size), 1) % ny
    mixers = []
    (coupling,) = arrived("coupling")
    for piece in pieces_of(1.0 - coupling[...], 2):
        wide = mat(spread, piece).astype(BF16)
        mixers.append(jnp.where(same_row, mat_nt(wide, spread), 0.0).astype(BF16))
    mixer = jnp.concatenate([mixers[0], mixers[0], mixers[1]], axis=1)

    crit, attract, slope, covol = arrived("crit", "attract", "slope", "covol")
    for i in range(nc):
        root = jnp.sqrt(jnp.full((SUBLANES, LANES), attract[i], F32))
        kappa = jnp.full((SUBLANES, LANES), slope[i], F32)
        tc = jnp.full((SUBLANES, LANES), crit[i], F32)
        table_v[0, i] = root * (1.0 + kappa)
        table_v[1, i] = root * kappa / jnp.sqrt(tc)
        table_v[2, i] = jnp.full((SUBLANES, LANES), covol[i], F32)

    press, loc, member, place = arrived("press", "loc", "member", "place")
    row_hot, lane_hot = place_hots(loc[...], nx * ny)
    lane_hot = hot(lane_hot)

    def cells_of(field, count):
        found = mat_hot(field, lane_hot, count)
        return jnp.sum(jnp.where(row_hot, found, 0.0), axis=0, keepdims=True)

    p_cell = cells_of(press[...], 3)
    pcell_out[...] = p_cell
    slot_hot = slot_hot_of(member[...], place[...])
    (heat,) = arrived("heat")

    shape3 = (ny // SUBLANES, SUBLANES, LANES)
    root_t = [jnp.sqrt(heat[pl.ds(x * ny, ny)].reshape(shape3)) for x in range(nx)]
    for x in range(nx):
        span, lanes = pl.ds(x * ny, ny), pl.ds(x * LANES, LANES)
        total = jnp.zeros(shape3, F32)
        volume = jnp.zeros(shape3, F32)
        for i in range(nc):
            o = amount_v[i, span].reshape(shape3)
            v = jnp.abs(table_v[0, i] - table_v[1, i] * root_t[x]) * o
            total += o
            volume += table_v[2, i] * o
            high, low = pieces_of(v.reshape(ny, LANES), 2)
            split_v[pl.ds(i * ny, ny), lanes] = high
            split_v[pl.ds(size + i * ny, ny), lanes] = low
            split_v[pl.ds(2 * size + i * ny, ny), lanes] = high
        field_v[0, span] = total.reshape(ny, LANES)
        field_v[1, span] = volume.reshape(ny, LANES)
    for c in range(chunks):
        mixed = mat(mixer, split_v[:, pl.ds(c * per * LANES, per * LANES)])
        for k in range(per):
            x = c * per + k
            span = pl.ds(x * ny, ny)
            total = jnp.zeros(shape3, F32)
            for i in range(nc):
                m = mixed[i * ny : (i + 1) * ny, k * LANES : (k + 1) * LANES].reshape(shape3)
                psi = jnp.abs(table_v[0, i] - table_v[1, i] * root_t[x]) * m
                total += amount_v[i, span].reshape(shape3) * psi
                psi_v[i, span] = psi.reshape(ny, LANES)
            field_v[2, span] = total.reshape(ny, LANES)

    flag, visc, trans, inject = arrived("flag", "visc", "trans", "inject")
    states = []
    for h in range(2):
        span = pl.ds(h * half * rows, half * rows)
        p, t = press[span], heat[span]
        liquid = flag[span] == 1
        r = inverse(field_v[0, span])
        rt = inverse(t)
        ratio_pt = p * rt
        beta = field_v[1, span] * r
        gr = ratio_pt * rt * r
        big_a = gr * r * field_v[2, span]
        big_b = ratio_pt * beta
        z = jnp.where(liquid, big_b + 0.01, 1.0 + big_b)
        c1 = big_a - 3.0 * big_b * big_b - 2.0 * big_b
        c0 = big_b * big_b + big_b * big_b * big_b - big_a * big_b
        states.append([z, big_b, big_b + 0.01, big_b - 1.0, c1, c0])
        field_v[1, span] = inverse(beta)
        field_v[3, span] = r
        terms_v[0, span] = ratio_pt
        terms_v[1, span] = 0.5 * big_a
        terms_v[2, span] = gr
    for _ in range(NEWT):
        for state in states:
            z, _, floor, c2, c1, c0 = state
            near = z + c2
            value = (near * z + c1) * z + c0
            incline = (near + near + z) * z + c1
            state[0] = jnp.maximum(z - value * inverse(jnp.maximum(incline, 0.1)), floor)
    for h, (z, big_b, *_) in enumerate(states):
        span = pl.ds(h * half * rows, half * rows)
        ratio_pt, gr = terms_v[0, span], terms_v[2, span]
        log_ratio = jnp.log(
            (z + (1.0 + ROOT_TWO) * big_b) * inverse(z + (1.0 - ROOT_TWO) * big_b)
        )
        lb = log_ratio * inverse(ROOT_TWO * big_b)
        mob = ratio_pt * inverse(z * jnp.where(flag[span] == 1, visc[1], visc[0]))
        mob_out[span] = mob
        field_v[3, span] = mob * field_v[3, span]
        terms_v[0, span] = jnp.log(z - big_b)
        terms_v[1, span] = (z - 1.0 + terms_v[1, span] * lb) * field_v[1, span]
        terms_v[2, span] = gr * lb
    seg, strength, own_press, perm = arrived("seg", "strength", "own_press", "perm")
    weight = strength[...] * cells_of(mob_out[...], 2)
    segments = own_press.shape[1]
    lanes = iota((LANES, loc.shape[1]), 0)
    shift = hot(iota((segments, LANES), 0) + 2 * segments == iota((segments, LANES), 1))
    sums = mat_hot(own_press[...], shift)
    for k, value in enumerate((weight, weight * (p_cell - 1.0))):
        seg_hot = hot(lanes == seg[...] + k * segments)
        for piece in pieces_of(slot_hot * value, 2):
            sums += mat_nt(piece, seg_hot)
    part_v[...] = sums
    part_copy = go(part_v, part_out, out_sems.at[2])

    total = sum(inject[i] for i in range(nc))
    share = 1.0 / jnp.full((SUBLANES, LANES), total, F32)
    numbers = [trans[0], trans[1], trans[2], visc[0], visc[1]]
    for i in range(nc):
        consts_out[i] = inject[i] * share
    for i, number in enumerate(numbers):
        consts_out[nc + i] = jnp.full((SUBLANES, LANES), number, F32)

    stores = []
    for x in range(nx):
        span = pl.ds(x * ny, ny)
        e0, e1, e2 = (terms_v[k, span].reshape(shape3) for k in range(3))
        mr = field_v[3, span].reshape(shape3)
        for i in range(nc):
            value = table_v[2, i] * e1 - e0 - psi_v[i, span].reshape(shape3) * e2
            lnphi_v[i, span] = value.reshape(ny, LANES).astype(BF16)
            carried = (mr * amount_v[i, span].reshape(shape3)).reshape(ny, LANES)
            carried_out[i, pl.ds(MARGIN + x * ny, ny)] = carried
        if (x + 1) * 2 % nx == 0:
            span = pl.ds((x + 1 - nx // 2) * ny, nx // 2 * ny)
            stores.append(go(lnphi_v.at[:, span], lnphi_out.at[:, span], out_sems.at[len(stores)]))

    odd_g = lax.axis_index(axes[0]) % 2 == 1
    odd_s = lax.axis_index(axes[1]) % 2 == 1
    for k in range(edge_x_out.shape[0]):
        at_low = odd_g if k == 0 else jnp.logical_not(odd_g)
        start = pl.multiple_of(jnp.where(at_low, 0, (nx - 1) * ny), ny)
        for i in range(nc):
            edge_x_out[k, i] = carried_out[i, pl.ds(start + MARGIN, ny)]
        edge_x_out[k, nc] = press[pl.ds(start, ny)]
        edge_x_out[k, nc + 1] = perm[pl.ds(start, ny)]
    for i in range(nc + 2):
        source = carried_out.at[i] if i < nc else press if i == nc else perm
        skip = MARGIN if i < nc else 0
        low = source[pl.ds(skip, nx, stride=ny)]
        high = source[pl.ds(skip + ny - 1, nx, stride=ny)]
        edge_ya_out[i] = jnp.where(odd_s, low, high)
        edge_yb_out[i] = jnp.where(odd_s, high, low)
    for copy in [part_copy, *stores]:
        copy.wait()


def flux_kernel(
    nx,
    ny,
    axes,
    many_x,
    carried,
    press,
    perm,
    pore,
    flag,
    old,
    mob,
    edge_ya,
    edge_yb,
    well_rows,
    loc,
    member,
    seg,
    strength,
    place,
    pcell,
    consts,
    own_press,
    order,
    exit_press,
    friction,
    *rest,
):
    edge_x, rest = rest[:many_x], rest[many_x:]
    resid_out, well_out, y_v, res_v, well_v, out_sems = rest
    nc = carried.shape[0]
    g, s = lax.axis_index(axes[0]), lax.axis_index(axes[1])
    ng, ns = lax.axis_size(axes[0]), lax.axis_size(axes[1])
    odd_g, odd_s = g % 2 == 1, s % 2 == 1
    has_low_y, has_high_y = s > 0, s < ns - 1
    has_low_x, has_high_x = g > 0, g < ng - 1

    for i in range(nc + 2):
        a, b = edge_ya[i], edge_yb[i]
        low, high = jnp.where(odd_s, a, b), jnp.where(odd_s, b, a)
        if i == nc + 1:
            low, high = jnp.where(has_low_y, low, 0.0), jnp.where(has_high_y, high, 0.0)
        y_v[0, i] = low
        y_v[1, i] = high

    def side_x(i, high):
        if many_x == 1:
            return edge_x[0][i]
        return jnp.where(odd_g != high, edge_x[0][i], edge_x[1][i])

    row_hot, lane_hot = place_hots(loc[...], nx * ny)
    slot_hot = slot_hot_of(member[...], place[...])
    segments = own_press.shape[1]
    gathered = well_rows[...]
    seg_hot = hot(iota((LANES, loc.shape[1]), 0) == seg[...] + 2 * segments)
    p_seg = jnp.sum(mat_hot(gathered, seg_hot) * slot_hot, axis=0, keepdims=True)
    push = strength[...] * (pcell[...] - p_seg)
    flows = jnp.concatenate(
        [
            jnp.where(row_hot, jnp.maximum(push, 0.0), 0.0),
            jnp.where(row_hot, jnp.minimum(push, 0.0), 0.0),
        ],
        axis=0,
    )
    lane_hot = hot(lane_hot)
    spread = sum(mat_nt(piece, lane_hot) for piece in pieces_of(flows, 2))

    own = jnp.sum(gathered, axis=0, keepdims=True)
    well_p = own_press[...]
    rate = own[:, segments : 2 * segments] - (well_p - 1.0) * own[:, :segments]
    order_hot = hot(iota((segments, segments), 0) == order[...])
    both = mat_hot(jnp.concatenate([rate, well_p], axis=0), order_hot)
    upper = hot(iota((segments, segments), 0) <= iota((segments, segments), 1))
    running = mat_hot(both[0:1], upper)
    press_ord = both[1:2]
    after = hot(iota((segments, segments), 0) == iota((segments, segments), 1) + 1)
    last = iota((1, segments), 1) == segments - 1
    nexts = jnp.where(last, exit_press[0], mat_hot(press_ord, after))
    res_ord = press_ord - nexts - friction[0] * running * jnp.abs(running)
    well_v[...] = sum(mat_nt(piece, order_hot) for piece in pieces_of(res_ord, 3))
    stores = [pltpu.make_async_copy(well_v, well_out, out_sems.at[nx])]
    stores[0].start()

    lane = iota((ny, LANES), 1)
    row = iota((ny, LANES), 0)
    first, final = row == 0, row == ny - 1

    def const(k):
        return jnp.concatenate([consts[k]] * (ny // SUBLANES), axis=0)

    for x in range(nx):
        rows = pl.ds(x * ny, ny)
        p_a, k_a = press[rows], perm[rows]
        twice_k = 2.0 * k_a

        def face(p_b, k_b, axis):
            t = const(nc + axis) * (twice_k * k_b) * inverse(k_a + k_b)
            flow = t * (p_a - p_b)
            return jnp.maximum(flow, 0.0), jnp.minimum(flow, 0.0)

        def other_x(field, i, high):
            at = x + 1 if high else x - 1
            return field[pl.ds(at * ny, ny)] if 0 <= at < nx else side_x(i, high)

        def other_y(field, i, high):
            if high:
                return jnp.where(final, y_v[1, i, pl.ds(x, 1)], pltpu.roll(field, ny - 1, 0))
            return jnp.where(first, y_v[0, i, pl.ds(x, 1)], pltpu.roll(field, 1, 0))

        centre = pore[rows] * jnp.where(flag[rows] == 1, const(nc + 4), const(nc + 3))
        centre += spread[x * ny : (x + 1) * ny]
        ins = []
        for high in (True, False):
            p_b, k_b = other_x(press, nc, high), other_x(perm, nc + 1, high)
            if x == nx - 1 and high:
                k_b = jnp.where(has_high_x, k_b, 0.0)
            if x == 0 and not high:
                k_b = jnp.where(has_low_x, k_b, 0.0)
            ins.append(face(p_b, k_b, 0))
        for high in (True, False):
            ins.append(face(other_y(p_a, nc, high), other_y(k_a, nc + 1, high), 1))
        for shift, edge in ((LANES - 1, LANES - 1), (1, 0)):
            k_b = jnp.where(lane == edge, 0.0, pltpu.roll(k_a, shift, 1))
            ins.append(face(pltpu.roll(p_a, shift, 1), k_b, 2))
        for out, _ in ins:
            centre += out
        ins = [into for _, into in ins]
        pushed = mob[rows] * spread[(nx + x) * ny : (nx + x + 1) * ny]
        for i in range(nc):
            base = MARGIN + x * ny
            c = carried[i, pl.ds(base, ny)]
            value = centre * c - old[i, rows] + const(i) * pushed
            for k, high in ((0, True), (1, False)):
                at = x + 1 if high else x - 1
                inside = 0 <= at < nx
                c_b = carried[i, pl.ds(MARGIN + at * ny, ny)] if inside else side_x(i, high)
                value += ins[k] * c_b
            up, down = carried[i, pl.ds(base + 1, ny)], carried[i, pl.ds(base - 1, ny)]
            value += ins[2] * jnp.where(final, y_v[1, i, pl.ds(x, 1)], up)
            value += ins[3] * jnp.where(first, y_v[0, i, pl.ds(x, 1)], down)
            value += ins[4] * pltpu.roll(c, LANES - 1, 1)
            value += ins[5] * pltpu.roll(c, 1, 1)
            res_v[i, rows] = value
        copy = pltpu.make_async_copy(res_v.at[:, rows], resid_out.at[:, rows], out_sems.at[x])
        copy.start()
        stores.append(copy)
    for copy in stores:
        copy.wait()


def swaps_of(count, other):
    pairs = [(i, i + 1) for i in range(1 if other else 0, count - 1, 2)]
    return pairs + [(b, a) for a, b in pairs]


def other_swaps_of(groups, count):
    swaps = [(g * count + a, g * count + b) for g in range(groups) for a, b in swaps_of(count, True)]
    ends = [(g * count + e, (g ^ 1) * count + e) for g in range(groups) for e in (0, count - 1)]
    return sorted(swaps + ends)


def per_device(
    amount,
    press,
    heat,
    flag,
    perm,
    pore,
    old,
    trans,
    visc,
    crit,
    attract,
    covol,
    slope,
    coupling,
    inject,
    locale,
    member,
    seg,
    strength,
    place,
    order,
    seg_press,
    exit_press,
    friction,
):
    axes = ("grp", "sub")
    nc, nx, ny, nz = amount.shape
    ng, ns = lax.axis_size("grp"), lax.axis_size("sub")
    rows = nx * ny
    perfs = locale.shape[0]
    wells, segments = place.shape[1], seg_press.shape[1]
    flat = lambda a: a.reshape(a.shape[:-3] + (rows, nz))
    line = lambda a: a.reshape(1, perfs)
    vm = pl.BlockSpec(memory_space=pltpu.VMEM)
    sm = pl.BlockSpec(memory_space=pltpu.SMEM)
    hbm = pl.BlockSpec(memory_space=pltpu.HBM)
    many_x = 1 if ng == 2 else 2

    amount, old = flat(amount), flat(old)
    press, heat, flag, perm, pore = (flat(a) for a in (press, heat, flag, perm, pore))
    locale, member, seg, strength = (line(a) for a in (locale, member, seg, strength))

    sources = (
        coupling, crit, attract, slope, covol, heat, press, locale, member, place,
        flag, visc, trans, inject, seg, strength, seg_press, perm,
    )
    kept = [
        pltpu.SMEM(a.shape, a.dtype) if a.ndim == 1 else pltpu.VMEM(a.shape, a.dtype)
        for a in sources
    ]
    in_hbm = lambda a: pltpu.with_memory_space_constraint(a, pltpu.HBM)

    lnphi, carried, mob, edge_x, edge_ya, edge_yb, part, pcell, consts = pl.pallas_call(
        functools.partial(phase_kernel, nx, ny, axes),
        out_shape=(
            jax.ShapeDtypeStruct((nc, rows, nz), BF16),
            jax.ShapeDtypeStruct((nc, rows + 2 * MARGIN, nz), F32),
            jax.ShapeDtypeStruct((rows, nz), F32),
            jax.ShapeDtypeStruct((many_x, nc + 2, ny, nz), F32),
            jax.ShapeDtypeStruct((nc + 2, nx, nz), F32),
            jax.ShapeDtypeStruct((nc + 2, nx, nz), F32),
            jax.ShapeDtypeStruct((wells, LANES), F32),
            jax.ShapeDtypeStruct((1, perfs), F32),
            jax.ShapeDtypeStruct((nc + 8, SUBLANES, LANES), F32),
        ),
        in_specs=[hbm] * (1 + len(sources)),
        out_specs=(hbm,) + (vm,) * 5 + (hbm,) + (vm,) * 2,
        scratch_shapes=[
            *kept,
            pltpu.VMEM((nc, rows, nz), F32),
            pltpu.VMEM((3 * nc * ny, nx * nz), BF16),
            pltpu.VMEM((nc, rows, nz), F32),
            pltpu.VMEM((nc, rows, nz), BF16),
            pltpu.VMEM((4, rows, nz), F32),
            pltpu.VMEM((3, rows, nz), F32),
            pltpu.VMEM((3, nc, SUBLANES, LANES), F32),
            pltpu.VMEM((wells, LANES), F32),
            pltpu.SemaphoreType.DMA((len(sources),)),
            pltpu.SemaphoreType.DMA((2,)),
            pltpu.SemaphoreType.DMA((3,)),
        ],
        compiler_params=pltpu.CompilerParams(vmem_limit_bytes=VMEM_LIMIT),
        name="phase",
    )(in_hbm(amount), *(in_hbm(a) for a in sources))

    got_ya = lax.ppermute(edge_ya, "sub", swaps_of(ns, False))
    got_x = [lax.ppermute(edge_x[k], "grp", swaps_of(ng, k == 1)) for k in range(many_x)]
    got_yb = lax.ppermute(edge_yb, axes, other_swaps_of(ng, ns))
    backward = [list(range(ns))[::-1]]
    well_rows = lax.all_to_all(
        part, "sub", split_axis=0, concat_axis=0, axis_index_groups=backward, tiled=True
    )

    resid, well = pl.pallas_call(
        functools.partial(flux_kernel, nx, ny, axes, many_x),
        out_shape=(
            jax.ShapeDtypeStruct((nc, rows, nz), F32),
            jax.ShapeDtypeStruct((1, segments), F32),
        ),
        in_specs=[vm] * 19 + [sm] * 2 + [vm] * many_x,
        out_specs=(hbm, hbm),
        scratch_shapes=[
            pltpu.VMEM((2, nc + 2, nx, nz), F32),
            pltpu.VMEM((nc, rows, nz), F32),
            pltpu.VMEM((1, segments), F32),
            pltpu.SemaphoreType.DMA((nx + 1,)),
        ],
        compiler_params=pltpu.CompilerParams(vmem_limit_bytes=VMEM_LIMIT),
        name="flux",
    )(
        carried, press, perm, pore, flag, old, mob, got_ya, got_yb, well_rows,
        locale, member, seg, strength, place, pcell,
        consts, seg_press, order, exit_press, friction, *got_x,
    )
    block = (nc, nx, ny, nz)
    return resid.reshape(block), lnphi.reshape(block), well


def solution(mesh):
    cells, parts = P("grp", "sub", None), P(None, "grp", "sub", None)
    listed = P(("grp", "sub"))
    row = P(("grp", "sub"), None)
    in_specs = (
        (parts,) + (cells,) * 5 + (parts,) + (P(),) * 8
        + (listed, row, listed, listed, P("grp", None), row, row, listed, listed)
    )
    return jax.shard_map(
        per_device, mesh=mesh, in_specs=in_specs, out_specs=(parts, parts, row), check_vma=False
    )
```
